256 devices in a mesh: gx: 8 (over x, y_hi), gy: 8 (over z), gz: 4 (over y_lo, core).
Axes of the slice: x: 4, y: 4 (y_hi: 2, y_lo: 2; y = y_hi * 2 + y_lo), z: 8, core: 2. Of those that a mesh axis runs over, the one named last changes fastest.
Arguments:
- force: float32 [3, 64, 256, 512], P(None, 'gx', 'gy', 'gz'), may hold values from -6 to 6
- grain: int32 [64, 256, 512], P('gx', 'gy', 'gz'), may hold values from 0 to 15
- density: float32 [64, 256, 512], P('gx', 'gy', 'gz'), may hold values from 0.6 to 0.98
Outputs:
- velocity: float32 [3, 64, 256, 512], P(None, 'gx', 'gy', 'gz')
- new_density: float32 [64, 256, 512], P('gx', 'gy', 'gz')
The draws below stay inside these ranges and needn't reach their ends.
All inputs are finite; a program needn't handle non-finite values.
Results may differ from the reference program's by a relative error of at most 0.0001.
Values sent between devices are 32-bit elements; how exact they have to be, the bound alone decides.
No kernel may reach another device: no remote copies, remote signals or barrier semaphores. Data moves between devices by JAX's collectives and lax.ppermute only.
A program may use at most 128 MiB of HBM per device.

```python
import jax
import jax.numpy as jnp

LEVELS = 4
COARSE_SWEEPS = 4
NX = 64
NY = 256
NZ = 512


def spread_blocks(field, width):
    return jnp.repeat(jnp.repeat(jnp.repeat(field, width, axis=-3), width, axis=-2), width, axis=-1)


def draw_grain(key, part):
    key = jax.random.fold_in(key, 11)
    width = 2 ** (LEVELS - 1)
    coarse_ids = jax.random.randint(key, (NX // width, NY // width, NZ // width), 0, 16)
    return spread_blocks(coarse_ids, width).astype(jnp.int32)


def draw_force(key, part):
    key = jax.random.fold_in(key, 23)
    noise_key, block_key = jax.random.split(key)
    width = 2 ** (LEVELS - 1)
    blocks = jax.random.normal(block_key, (3, NX // width, NY // width, NZ // width), jnp.float32)
    noise = jax.random.normal(noise_key, (3, NX, NY, NZ), jnp.float32)
    total = noise + 0.8 * spread_blocks(blocks, width)
    return jnp.clip(total, -6.0, 6.0)


def level_of(stream_key, shape, shards, least, largest):
    loudness, own = 1.0, jax.random.fold_in(stream_key, 6)
    for axis_at, shards_of in shards:
        steps = jnp.exp(jax.random.uniform(jax.random.fold_in(own, axis_at), (shards_of,), jnp.float32, least / len(shards), largest / len(shards)))
        loudness = loudness * jnp.repeat(steps, shape[axis_at] // shards_of).reshape([-1 if axis == axis_at else 1 for axis in range(len(shape))])
    return loudness


def setup_inputs(seed: int = 0) -> dict:
    streams_of = jax.random.split(jax.random.key(seed), 4)
    force = draw_force(jax.random.fold_in(streams_of[3], 71), 0)
    grain = draw_grain(jax.random.fold_in(streams_of[3], 71), 0)
    density = jnp.clip(0.6 + 0.38 * jax.random.uniform(streams_of[2], (NX, NY, NZ), jnp.float32) ** level_of(streams_of[2], (NX, NY, NZ), ((0, 8), (1, 8), (2, 4)), -0.2, 0.2), 0.6, 0.98)
    return dict(force=force, grain=grain, density=density)


OMEGA = 0.8
STEP_TIME = 0.1
DIFFUSION = 0.05
grain_table = [0.5 * 8.0 ** (entry / 15.0) for entry in range(16)]


def beside(padded, axis_dim, offset):
    pieces = [slice(1, -1), slice(1, -1), slice(1, -1)]
    length = padded.shape[padded.ndim - 3 + axis_dim]
    pieces[axis_dim] = slice(1 + offset, length - 1 + offset)
    leading = tuple([slice(None)] * (padded.ndim - 3))
    return padded[leading + tuple(pieces)]


def centre(padded):
    return beside(padded, 0, 0)


def diagonal_of(coeffs, factor):
    viscous = coeffs[0]
    middle = centre(viscous)
    result = centre(coeffs[1])
    for axis_dim in range(3):
        for offset in (-1, 1):
            result = result + (0.5 * factor) * (middle + beside(viscous, axis_dim, offset))
    return result


def operate(field_pad, coeffs, factor):
    viscous = coeffs[0]
    middle = centre(viscous)
    inner = centre(field_pad)
    result = centre(coeffs[1]) * inner
    for axis_dim in range(3):
        for offset in (-1, 1):
            weight = (0.5 * factor) * (middle + beside(viscous, axis_dim, offset))
            result = result + weight * (inner - beside(field_pad, axis_dim, offset))
    return result


def coarsen(field):
    chans, sx, sy, sz = field.shape
    return field.reshape(chans, sx // 2, 2, sy // 2, 2, sz // 2, 2).mean(axis=(2, 4, 6))


def refine(field):
    return jnp.repeat(jnp.repeat(jnp.repeat(field, 2, axis=1), 2, axis=2), 2, axis=3)


def pad_cells(field):
    return jnp.pad(field, ((0, 0), (1, 1), (1, 1), (1, 1)))


def advect(padded):
    dens = padded[0]
    flow = padded[1:]
    middle = centre(dens)
    change = jnp.zeros_like(middle)
    for axis_dim in range(3):
        moving = flow[axis_dim]
        here = centre(moving)
        face_hi = 0.5 * (here + beside(moving, axis_dim, 1))
        face_lo = 0.5 * (beside(moving, axis_dim, -1) + here)
        flux_hi = jnp.maximum(face_hi, 0.0) * middle + jnp.minimum(face_hi, 0.0) * beside(dens, axis_dim, 1)
        flux_lo = jnp.maximum(face_lo, 0.0) * beside(dens, axis_dim, -1) + jnp.minimum(face_lo, 0.0) * middle
        change = change + (flux_hi - flux_lo)
    spread = -6.0 * middle
    for axis_dim in range(3):
        for offset in (-1, 1):
            spread = spread + beside(dens, axis_dim, offset)
    return middle - STEP_TIME * change + (STEP_TIME * DIFFUSION) * spread


def smooth(guess, source, coeffs, factor, weight_sum):
    return guess + OMEGA * (source - operate(pad_cells(guess), coeffs, factor)) / weight_sum


def cycle(source, coeff_list, depth):
    factor = 0.25 ** depth
    coeffs = pad_cells(coeff_list[depth])
    weight_sum = diagonal_of(coeffs, factor)
    guess = OMEGA * source / weight_sum
    if depth == LEVELS - 1:
        for counter in range(COARSE_SWEEPS - 1):
            guess = smooth(guess, source, coeffs, factor, weight_sum)
        return guess
    guess = smooth(guess, source, coeffs, factor, weight_sum)
    remainder = source - operate(pad_cells(guess), coeffs, factor)
    correction = cycle(coarsen(remainder), coeff_list, depth + 1)
    guess = guess + refine(correction)
    for counter in range(2):
        guess = smooth(guess, source, coeffs, factor, weight_sum)
    return guess


def reference(force, grain, density):
    looked = jnp.asarray(grain_table, dtype=jnp.float32)[grain]
    coeffs = jnp.stack([looked * density * density * density, 0.02 + 0.08 * density])
    coeff_list = [coeffs]
    for depth in range(1, LEVELS):
        coeff_list.append(coarsen(coeff_list[-1]))
    velocity = cycle(force, coeff_list, 0)
    packed = pad_cells(jnp.concatenate([density[None], velocity]))
    return velocity, advect(packed)
```

```python
import jax
import jax.numpy as jnp
from jax import lax
from jax.experimental import pallas as pl
from jax.experimental.pallas import tpu as pltpu
from jax.sharding import PartitionSpec as P

OMEGA = 0.8
STEP_TIME = 0.1
DIFFUSION = 0.05
grain_table = [0.5 * 8.0 ** (entry / 15.0) for entry in range(16)]
F32 = jnp.float32
MIB = 1024 * 1024

W0 = (4, 4, 4, 5, 4)
OFF0 = (0, 4, 8, 12, 17)
NX0, NY0, NZ0 = 18, 48, 256
W1 = (5, 5, 5, 6, 5)
OFF1 = (0, 5, 10, 15, 21)
NX1, NY1 = 16, 48
PIECE1 = (0, 14, 28, 42, 58)
PIECES1 = [(f, x) for f in range(5) for x in range(-W1[f], 4 + W1[f])]
NX2, NY2 = 17, 48
NX3, NY3 = 9, 24


def iota(shape, dim):
    return lax.broadcasted_iota(jnp.int32, shape, dim)


def back(value, axis):
    return pltpu.roll(value, value.shape[axis] - 1, axis)


def forth(value, axis):
    return pltpu.roll(value, 1, axis)


def turn(value, shift, axis):
    shift = shift % value.shape[axis]
    return value if shift == 0 else pltpu.roll(value, shift, axis)


def call(body, outs, scratch=(), limit=56):
    def run(flags, *operands):
        return pl.pallas_call(
            body,
            out_shape=[jax.ShapeDtypeStruct(s, F32) for s in outs],
            in_specs=[pl.BlockSpec(memory_space=pltpu.SMEM)]
            + [pl.BlockSpec(memory_space=pltpu.VMEM)] * len(operands),
            out_specs=[pl.BlockSpec(memory_space=pltpu.VMEM)] * len(outs),
            scratch_shapes=[pltpu.VMEM(s, F32) for s in scratch],
            compiler_params=pltpu.CompilerParams(vmem_limit_bytes=limit * MIB),
        )(flags, *operands)

    return run


def flag(flags, index):
    return flags[index].astype(F32)


def weighted(v, w, c, x, xp, xm):
    wx, wy, wz = w
    here = v[c, x]
    total = wx[x] * v[c, xp] + wx[xm] * v[c, xm]
    a = wy[x]
    total = total + a * back(here, 0) + forth(a * here, 0)
    a = wz[x]
    total = total + a * back(here, 1) + forth(a * here, 1)
    return here, total


def planes(lo, hi, n, body):
    def step(k, carry):
        x = lax.rem(k + (lo + n), n)
        body(x, lax.rem(x + 1, n), lax.rem(x + n - 1, n))
        return carry

    lax.fori_loop(0, hi - lo, step, 0)


def sweep(dst, src, b, w, dinv, lo, hi, n):
    def body(x, xp, xm):
        scale = dinv[x]
        for c in range(3):
            here, total = weighted(src, w, c, x, xp, xm)
            dst[c, x] = 0.2 * here + scale * (b[c, x] + total)

    planes(lo, hi, n, body)


def weights(eta, w, factor, lo, hi, n):
    wx, wy, wz = w
    half = 0.5 * factor

    def body(x, xp, xm):
        here = eta[x]
        wx[x] = half * (here + eta[xp])
        wy[x] = half * (here + back(here, 0))
        wz[x] = half * (here + back(here, 1))

    planes(lo, hi, n, body)


def diagonals(kap, w, dg, dinv, lo, hi, n):
    wx, wy, wz = w

    def body(x, xp, xm):
        k, a, g = kap[x], wy[x], wz[x]
        d = k + (wx[x] + wx[xm]) + (a + forth(a, 0)) + (g + forth(g, 1))
        inside = k > 0.0
        dg[x] = d
        dinv[x] = jnp.where(inside, OMEGA / jnp.where(inside, d, 1.0), 0.0)

    planes(lo, hi, n, body)


def first(v, b, dinv, lo, hi, n):
    def body(x, xp, xm):
        for c in range(3):
            v[c, x] = dinv[x] * b[c, x]

    planes(lo, hi, n, body)


def rest(v, b, w, dg, c, x, xp, xm):
    here, total = weighted(v, w, c, x, xp, xm)
    return b[c, x] - dg[x] * here + total


def mean_matrix(lanes):
    k, j = iota((128, 128), 0), iota((128, 128), 1)
    return jnp.where((k >> 1) == (j & (lanes - 1)), 0.125, 0.0).astype(F32)


def repeat_matrix(lanes, out):
    k, j = iota((128, out), 0), iota((128, out), 1)
    return jnp.where(k == ((j & (lanes - 1)) >> 1), 1.0, 0.0).astype(F32)


def dot(a, b):
    return jnp.dot(a, b, precision=lax.Precision.HIGHEST, preferred_element_type=F32)


def row_pairs(tmp, value):
    rows = value.shape[0]
    tmp[pl.ds(0, rows), :] = value
    return tmp[pl.ds(0, rows // 2, stride=2), :] + tmp[pl.ds(1, rows // 2, stride=2), :]


def prepare(flags, force, grain, dens, eta, up, down):
    for x in range(8):
        ids = grain[x]
        looked = jnp.full(ids.shape, grain_table[0], F32)
        for entry in range(1, 16):
            looked = jnp.where(ids == entry, grain_table[entry], looked)
        d = dens[x]
        eta[x] = looked * d * d * d
    for f in range(5):
        for k in range(W0[f]):
            for out, x in ((up, 8 - W0[f] + k), (down, k)):
                out[OFF0[f] + k] = force[f, x] if f < 3 else (eta if f == 3 else dens)[x]


def plane0(flags, own, f, x, rows):
    force, eta, dens, low, high = own
    if 0 <= x < 8:
        return force[f, x, rows] if f < 3 else (eta if f == 3 else dens)[x, rows]
    away = x - 8 if x >= 8 else -x - 1
    if away >= W0[f]:
        return jnp.zeros((rows.stop - rows.start, 128), F32)
    if x >= 8:
        return high[OFF0[f] + away, rows] * flag(flags, 1)
    return low[OFF0[f] + W0[f] - 1 - away, rows] * flag(flags, 0)


def rel0(x):
    return x if x < 13 else x - NX0


YF = (0, 1, 2, 4, 3)


def pack_y0(flags, force, eta, dens, low, high, up, down):
    own = (force, eta, dens, low, high)
    sub = iota((8, 128), 0)
    for i, f in enumerate(YF):
        for q in range(9):
            a, b = rel0(2 * q), rel0(2 * q + 1)
            top, bottom = slice(24, 32), slice(0, 8)
            up[9 * i + q] = jnp.where(
                sub < 4, turn(plane0(flags, own, f, a, top), 4, 0), plane0(flags, own, f, b, top)
            )
            down[9 * i + q] = jnp.where(
                sub < 4, plane0(flags, own, f, a, bottom), turn(plane0(flags, own, f, b, bottom), 4, 0)
            )
    for t in range(3):
        hi, lo = jnp.zeros((8, 128), F32), jnp.zeros((8, 128), F32)
        for s in range(8):
            if 8 * t + s < NX0:
                x = rel0(8 * t + s)
                hi = jnp.where(sub == s, turn(plane0(flags, own, 3, x, slice(24, 32)), s - 3, 0), hi)
                lo = jnp.where(sub == s, turn(plane0(flags, own, 3, x, slice(0, 8)), s - 4, 0), lo)
        up[45 + t], down[45 + t] = hi, lo


def rows0(flags, own, lowy, highy, f, x):
    sub = iota((8, 128), 0)
    i = YF.index(f)
    high, low = highy[9 * i + x // 2], lowy[9 * i + x // 2]
    if x % 2:
        high = turn(high, 4, 0)
    else:
        low = turn(low, 4, 0)
    if f == 3:
        high = jnp.where(sub == 4, turn(highy[45 + x // 8], 4 - x % 8, 0), high)
        low = jnp.where(sub == 3, turn(lowy[45 + x // 8], 3 - x % 8, 0), low)
    middle = plane0(flags, own, f, rel0(x), slice(0, 32))
    return jnp.concatenate([middle, high * flag(flags, 3), low * flag(flags, 2)], axis=0)


def pack_z0(flags, force, eta, dens, lowx, highx, lowy, highy, up, down):
    own = (force, eta, dens, lowx, highx)
    lane = iota((NY0, 128), 1)
    for g in range(3):
        hi, lo = jnp.zeros((NY0, 128), F32), jnp.zeros((NY0, 128), F32)
        for s in range(6):
            for f in range(5):
                at, w = 21 * s + OFF0[f], W0[f]
                value = rows0(flags, own, lowy, highy, f, 6 * g + s)
                there = (lane >= at) & (lane < at + w)
                hi = jnp.where(there, turn(value, at - (128 - w), 1), hi)
                lo = jnp.where(there, turn(value, at, 1), lo)
        up[g], down[g] = hi, lo


def fine(flags, force, eta, dens, lowx, highx, lowy, highy, lowz, highz,
         b, v, dinv, wx, wy, wz, den, own1, up, down,
         eta0, kap, dg, v0, pairs, tmp):
    own = (force, eta, dens, lowx, highx)
    lane = iota((NY0, 128), 1)
    for x in range(NX0):
        for f in range(5):
            at, w = 21 * (x % 6) + OFF0[f], W0[f]
            middle = rows0(flags, own, lowy, highy, f, x)
            high = turn(highz[x // 6], -at, 1) * flag(flags, 5)
            low = turn(lowz[x // 6], 128 - w - at, 1) * flag(flags, 4)
            beyond = jnp.where(lane < w, high, jnp.where(lane >= 128 - w, low, 0.0))
            if f < 3:
                b[f, x, :, 0:128] = middle
                b[f, x, :, 128:256] = beyond
            elif f == 3:
                eta0[x, :, 0:128] = middle
                eta0[x, :, 128:256] = beyond
            else:
                den[x, :, 0:128] = middle
                den[x, :, 128:256] = beyond
                for half, value in ((slice(0, 128), middle), (slice(128, 256), beyond)):
                    kap[x, :, half] = jnp.where(value > 0.0, 0.02 + 0.08 * value, 0.0)
    w = (wx, wy, wz)
    weights(eta0, w, 1.0, -5, 13, NX0)
    diagonals(kap, w, dg, dinv, -4, 12, NX0)
    first(v0, b, dinv, -4, 12, NX0)
    sweep(v, v0, b, w, dinv, -3, 11, NX0)

    def blocks(i, carry):
        x0 = lax.rem(2 * i + NX0 - 2, NX0)
        xm, xp, xq = lax.rem(x0 + NX0 - 1, NX0), lax.rem(x0 + 1, NX0), lax.rem(x0 + 2, NX0)
        for c in range(3):
            r = rest(v, b, w, dg, c, x0, xp, xm) + rest(v, b, w, dg, c, xp, xq, x0)
            at = pl.multiple_of((c * 6 + i) * 16, 16)
            pairs[pl.ds(at, 16), :] = row_pairs(tmp, r[0:32, 0:128])
        return carry

    lax.fori_loop(0, 6, blocks, 0)
    for i in range(-2, 6):
        x = (2 * i) % NX0
        r = eta0[x, 0:32, 0:128] + eta0[x + 1, 0:32, 0:128]
        pairs[pl.ds((18 + i + 2) * 16, 16), :] = row_pairs(tmp, r)
        if -1 <= i < 5:
            r = kap[x, 0:32, 0:128] + kap[x + 1, 0:32, 0:128]
            pairs[pl.ds((26 + i + 1) * 16, 16), :] = row_pairs(tmp, r)
    pairs[...] = dot(pairs[...], mean_matrix(64))

    def piece(f, i):
        at = f * 6 + i + 1 if f < 3 else (20 + i if f == 3 else 27 + i)
        return pairs[pl.ds(at * 16, 16), :]

    half = iota((16, 128), 1) < 64
    ups = [(f, i) for f in range(5) for i in range(4 - W1[f], 4)]
    downs = [(f, i) for f in range(5) for i in range(0, W1[f])]
    for k in range(13):
        up[k] = jnp.where(half, piece(*ups[2 * k]), piece(*ups[2 * k + 1]))
        down[k] = jnp.where(half, piece(*downs[2 * k]), piece(*downs[2 * k + 1]))
    for f in range(5):
        for i in range(4):
            own1[f, i] = piece(f, i)


def twice(value, half):
    left = iota(value.shape, 1) < 64
    other = pltpu.roll(value, 64, 1)
    return jnp.where(left, value, other) if half == 0 else jnp.where(left, other, value)


def plane1(flags, own1, lowx, highx, f, x, rows):
    if 0 <= x < 4:
        return own1[f, x, rows]
    away = x - 4 if x >= 4 else -x - 1
    if x >= 4:
        at = OFF1[f] + away
        return twice(highx[at // 2, rows], at % 2) * flag(flags, 1)
    at = OFF1[f] + W1[f] - 1 - away
    return twice(lowx[at // 2, rows], at % 2) * flag(flags, 0)


def pack_y1(flags, own1, lowx, highx, up, down):
    sub = iota((8, 128), 0)
    left = iota((16, 128), 1) < 64
    for u in range(0, 36, 2):
        two = []
        for k in range(2):
            a, b = PIECES1[2 * (u + k)], PIECES1[2 * (u + k) + 1]
            value = jnp.where(
                left,
                plane1(flags, own1, lowx, highx, *a, slice(0, 16)),
                plane1(flags, own1, lowx, highx, *b, slice(0, 16)),
            )
            two.append((value[0:8], value[8:16]))
            up[u + k], down[u + k] = value[8:16], value[0:8]
        (a0, a1), (b0, b1) = two
        up[36 + u // 2] = jnp.where(sub < 4, turn(a0, 4, 0), b0)
        down[36 + u // 2] = jnp.where(sub < 4, a1, turn(b1, 4, 0))


def rows1(flags, own1, lowx, highx, lowy, highy, f, x):
    p = PIECE1[f] + x + W1[f]
    u = p // 2
    high, low = highy[36 + u // 2], lowy[36 + u // 2]
    if u % 2:
        high = turn(high, 4, 0)
    else:
        low = turn(low, 4, 0)
    above = twice(jnp.concatenate([highy[u], high], axis=0), p % 2) * flag(flags, 3)
    below = twice(jnp.concatenate([low, lowy[u]], axis=0), p % 2) * flag(flags, 2)
    return jnp.concatenate([plane1(flags, own1, lowx, highx, f, x, slice(0, 16)), above, below], axis=0)


def pack_z1(flags, own1, lowx, highx, lowy, highy, up, down):
    sub = iota((8, 128), 0)
    slot = iota((40, 128), 1) >> 5
    for g in range(18):
        hi, lo = None, None
        for s in range(4):
            value = rows1(flags, own1, lowx, highx, lowy, highy, *PIECES1[4 * g + s])
            mix = jnp.where(sub < 4, value[24:32], value[32:40])
            value = jnp.concatenate([value[0:24], mix, value[40:48]], axis=0)
            moved = pltpu.roll(value, 32, 1)
            a, b = (value, moved) if s % 2 else (moved, value)
            hi = a if s == 0 else jnp.where(slot == s, a, hi)
            lo = b if s == 0 else jnp.where(slot == s, b, lo)
        up[g], down[g] = hi, lo


def coarse(flags, own1, lowx, highx, lowy, highy, lowz, highz,
           b, v, dinv, wx, wy, wz, own2, up, down,
           eta, kap, dg, v0, pairs, tmp):
    lane = iota((NY1, 128), 1)
    for x in range(NX1):
        kap[x] = jnp.zeros((NY1, 128), F32)
    for p, (f, x) in enumerate(PIECES1):
        g, s = p // 4, p % 4
        middle = rows1(flags, own1, lowx, highx, lowy, highy, f, x)
        high = turn(highz[g], 64 - 32 * s, 1) * flag(flags, 5)
        low = turn(lowz[g], 96 - 32 * s, 1) * flag(flags, 4)
        high = jnp.concatenate([high[0:32], high[24:40]], axis=0)
        low = jnp.concatenate([low[0:32], low[24:40]], axis=0)
        value = jnp.where(lane < 64, middle, jnp.where(lane < 96, high, low))
        if f < 3:
            b[f, x % NX1] = value
        else:
            (eta if f == 3 else kap)[x % NX1] = value
    w = (wx, wy, wz)
    weights(eta, w, 0.25, -6, 10, NX1)
    diagonals(kap, w, dg, dinv, -5, 9, NX1)
    first(v0, b, dinv, -5, 9, NX1)
    sweep(v, v0, b, w, dinv, -4, 8, NX1)

    def blocks(i, carry):
        x0 = 2 * i
        for c in range(3):
            r = rest(v, b, w, dg, c, x0, x0 + 1, lax.rem(x0 + NX1 - 1, NX1))
            r = r + rest(v, b, w, dg, c, x0 + 1, x0 + 2, x0)
            at = pl.multiple_of((c * 2 + i) * 24, 8)
            pairs[pl.ds(at, 24), :] = row_pairs(tmp, r)
        at = pl.multiple_of((6 + i) * 24, 8)
        pairs[pl.ds(at, 24), :] = row_pairs(tmp, eta[x0] + eta[x0 + 1])
        at = pl.multiple_of((8 + i) * 24, 8)
        pairs[pl.ds(at, 24), :] = row_pairs(tmp, kap[x0] + kap[x0 + 1])
        return carry

    lax.fori_loop(0, 2, blocks, 0)
    pairs[...] = dot(pairs[...], mean_matrix(64))
    left = iota((24, 128), 1) < 64
    for f in range(5):
        value = jnp.where(left, pairs[pl.ds(48 * f, 24), :], pairs[pl.ds(48 * f + 24, 24), :])
        own2[f] = value
        up[f, 0:8], up[f, 8:16] = value[16:24], value[0:8]
        down[f] = value[0:16]


def pack_x2(flags, own2, lowy, highy, out):
    sub = iota((8, 128), 0)
    for f in range(5):
        near, far = highy[f, 0:8] * flag(flags, 3), highy[f, 8:16] * flag(flags, 3)
        far_low, near_low = lowy[f, 0:8] * flag(flags, 2), lowy[f, 8:16] * flag(flags, 2)
        value = jnp.concatenate([own2[f, 0:8], near, jnp.where(sub < 4, far, far_low), near_low], axis=0)
        for d in range(8):
            out[d, 32 * f:32 * f + 32] = value
        if f == 3:
            for d in range(8):
                out[d, 160:168] = jnp.where(sub == 4, far, far_low)


def finish(flags, got, b1, v1, dinv1, wx1, wy1, wz1, b0, v0, dinv0, wx0, wy0, wz0, den,
           velocity, new_density,
           b2, eta2, kap2, dg2, dinv2, wx2, wy2, wz2, va2, vb2,
           b3, eta3, kap3, dg3, dinv3, wx3, wy3, wz3, va3, vb3,
           pairs, spread, tmp, e2, va1, vb1, va0, vb0, wide):
    sub = iota((8, 128), 0)
    none = jnp.zeros((NY2, 128), F32)
    for f in range(5):
        for d in range(8):
            own, near = got[d, 32 * f:32 * f + 8], got[d, 32 * f + 8:32 * f + 16]
            mix, low = got[d, 32 * f + 16:32 * f + 24], got[d, 32 * f + 24:32 * f + 32]
            far, far_low = mix, mix
            if f == 3:
                extra = got[d, 160:168]
                far, far_low = jnp.where(sub == 4, extra, mix), jnp.where(sub == 3, extra, mix)
            value = jnp.concatenate([own, near, far, mix, far_low, low], axis=0)
            for h in range(2):
                piece = twice(value, h)
                if f < 3:
                    b2[f, 2 * d + h] = piece
                else:
                    (eta2 if f == 3 else kap2)[2 * d + h] = piece
    eta2[16], kap2[16] = none, none
    for c in range(3):
        b2[c, 16], va2[c, 16], vb2[c, 16] = none, none, none
    w2 = (wx2, wy2, wz2)
    weights(eta2, w2, 0.0625, 0, 17, NX2)
    diagonals(kap2, w2, dg2, dinv2, 0, 17, NX2)
    first(va2, b2, dinv2, 0, 16, NX2)
    sweep(vb2, va2, b2, w2, dinv2, 0, 16, NX2)

    def blocks(i, carry):
        x0 = 2 * i
        xm, xp, xq = lax.rem(x0 + NX2 - 1, NX2), x0 + 1, x0 + 2
        for c in range(3):
            r = rest(vb2, b2, w2, dg2, c, x0, xp, xm) + rest(vb2, b2, w2, dg2, c, xp, xq, x0)
            pairs[pl.ds(pl.multiple_of((c * 8 + i) * 24, 8), 24), :] = row_pairs(tmp, r)
        pairs[pl.ds(pl.multiple_of((24 + i) * 24, 8), 24), :] = row_pairs(tmp, eta2[x0] + eta2[xp])
        pairs[pl.ds(pl.multiple_of((32 + i) * 24, 8), 24), :] = row_pairs(tmp, kap2[x0] + kap2[xp])
        return carry

    lax.fori_loop(0, 8, blocks, 0)
    pairs[...] = dot(pairs[...], mean_matrix(32))
    none = jnp.zeros((NY3, 128), F32)
    for i in range(8):
        for c in range(3):
            b3[c, i] = pairs[pl.ds((c * 8 + i) * 24, 24), :]
        eta3[i] = pairs[pl.ds((24 + i) * 24, 24), :]
        kap3[i] = pairs[pl.ds((32 + i) * 24, 24), :]
    eta3[8], kap3[8] = none, none
    for c in range(3):
        b3[c, 8], va3[c, 8], vb3[c, 8] = none, none, none
    w3 = (wx3, wy3, wz3)
    weights(eta3, w3, 0.015625, 0, 9, NX3)
    diagonals(kap3, w3, dg3, dinv3, 0, 9, NX3)
    first(va3, b3, dinv3, 0, 8, NX3)
    sweep(vb3, va3, b3, w3, dinv3, 0, 8, NX3)
    sweep(va3, vb3, b3, w3, dinv3, 0, 8, NX3)
    sweep(vb3, va3, b3, w3, dinv3, 0, 8, NX3)

    for c in range(3):
        for i in range(8):
            pairs[pl.ds((c * 8 + i) * 24, 24), :] = vb3[c, i]
    spread[pl.ds(0, 576), :] = dot(pairs[pl.ds(0, 576), :], repeat_matrix(64, 128))

    def rise2(i, carry):
        for c in range(3):
            e = spread[pl.ds(pl.multiple_of((c * 8 + i) * 24, 8), 24), :]
            tmp[pl.ds(0, 24, stride=2), :] = e
            tmp[pl.ds(1, 24, stride=2), :] = e
            e = tmp[...]
            vb2[c, 2 * i] = vb2[c, 2 * i] + e
            vb2[c, 2 * i + 1] = vb2[c, 2 * i + 1] + e
        return carry

    lax.fori_loop(0, 8, rise2, 0)
    sweep(va2, vb2, b2, w2, dinv2, 0, 16, NX2)
    sweep(vb2, va2, b2, w2, dinv2, 0, 16, NX2)

    none = jnp.zeros((24, 128), F32)
    for c in range(3):
        for x in (0, 1, 18, 19):
            e2[c, x] = none
        for x in range(16):
            e2[c, 2 + x, 0:16] = vb2[c, x, 0:16]
            e2[c, 2 + x, 16:24] = vb2[c, x, 40:48]
    start = 2 * flags[6]
    for c in range(3):
        for k in range(6):
            pairs[pl.ds((c * 6 + k) * 24, 24), :] = e2[c, start + k]
    spread[pl.ds(0, 432), :] = dot(pairs[pl.ds(0, 432), :], repeat_matrix(128, 128))

    def rise1(k, carry):
        x = lax.rem(2 * k - 4 + NX1, NX1)
        for c in range(3):
            e = spread[pl.ds(pl.multiple_of((c * 6 + k) * 24, 8), 24), :]
            tmp[pl.ds(0, 24, stride=2), :] = e
            tmp[pl.ds(1, 24, stride=2), :] = e
            e = tmp[...]
            va1[c, x] = v1[c, x] + e
            va1[c, x + 1] = v1[c, x + 1] + e
        return carry

    lax.fori_loop(0, 6, rise1, 0)
    w1 = (wx1, wy1, wz1)
    sweep(vb1, va1, b1, w1, dinv1, -3, 7, NX1)
    sweep(va1, vb1, b1, w1, dinv1, -2, 6, NX1)

    for c in range(3):
        for i in range(-2, 6):
            at = (c * 8 + i + 2) * 24
            x = i % NX1
            pairs[pl.ds(at, 16), :] = va1[c, x, 0:16]
            pairs[pl.ds(at + 16, 8), :] = jnp.where(sub < 4, va1[c, x, 16:24], va1[c, x, 40:48])
    wide[...] = dot(pairs[pl.ds(0, 576), :], repeat_matrix(256, 256))

    def rise0(i, carry):
        x = lax.rem(2 * i - 4 + NX0, NX0)
        for c in range(3):
            at = pl.multiple_of((c * 8 + i) * 24, 8)
            for half in range(2):
                lanes = slice(128 * half, 128 * half + 128)
                e = wide[pl.ds(at, 24), lanes]
                tmp[pl.ds(0, 24, stride=2), :] = e
                tmp[pl.ds(1, 24, stride=2), :] = e
                e = tmp[...]
                va0[c, x, :, lanes] = v0[c, x, :, lanes] + e
                va0[c, x + 1, :, lanes] = v0[c, x + 1, :, lanes] + e
        return carry

    lax.fori_loop(0, 8, rise0, 0)
    w0 = (wx0, wy0, wz0)
    sweep(vb0, va0, b0, w0, dinv0, -2, 10, NX0)
    sweep(va0, vb0, b0, w0, dinv0, -1, 9, NX0)

    def advect(x, carry):
        xm, xp = lax.rem(x + NX0 - 1, NX0), x + 1
        d = den[x]
        change = jnp.zeros_like(d)
        spreading = -6.0 * d
        for axis in range(3):
            u = va0[axis, x]
            if axis == 0:
                u_up, u_lo, d_up, d_lo = va0[0, xp], va0[0, xm], den[xp], den[xm]
            else:
                u_up, u_lo = back(u, axis - 1), forth(u, axis - 1)
                d_up, d_lo = back(d, axis - 1), forth(d, axis - 1)
            hi, lo = 0.5 * (u + u_up), 0.5 * (u_lo + u)
            change = change + (jnp.maximum(hi, 0.0) * d + jnp.minimum(hi, 0.0) * d_up)
            change = change - (jnp.maximum(lo, 0.0) * d_lo + jnp.minimum(lo, 0.0) * d)
            spreading = spreading + (d_up + d_lo)
            velocity[axis, x] = u[0:32, 0:128]
        out = d - STEP_TIME * change + STEP_TIME * DIFFUSION * spreading
        new_density[x] = out[0:32, 0:128]
        return carry

    lax.fori_loop(0, 8, advect, 0)


def exchange(up, down, axis):
    n = lax.axis_size(axis)
    low = lax.ppermute(up, axis, [(i, (i + 1) % n) for i in range(n)])
    high = lax.ppermute(down, axis, [(i, (i - 1) % n) for i in range(n)])
    return low, high


def per_device(force, grain, density):
    gx, gy, gz = (lax.axis_index(a) for a in ("gx", "gy", "gz"))
    last = [lax.axis_size(a) - 1 for a in ("gx", "gy", "gz")]
    flags = jnp.stack(
        [gx > 0, gx < last[0], gy > 0, gy < last[1], gz > 0, gz < last[2], gx, gx]
    ).astype(jnp.int32)

    eta, up, down = call(prepare, [(8, 32, 128), (21, 32, 128), (21, 32, 128)])(flags, force, grain, density)
    x0 = exchange(up, down, "gx")
    up, down = call(pack_y0, [(48, 8, 128)] * 2)(flags, force, eta, density, *x0)
    y0 = exchange(up, down, "gy")
    up, down = call(pack_z0, [(3, 48, 128)] * 2)(flags, force, eta, density, *x0, *y0)
    z0 = exchange(up, down, "gz")
    vec, one = (3, NX0, NY0, NZ0), (NX0, NY0, NZ0)
    b0, v0, dinv0, wx0, wy0, wz0, den, own1, up, down = call(
        fine,
        [vec, vec, one, one, one, one, one, (5, 4, 16, 128), (13, 16, 128), (13, 16, 128)],
        [one, one, one, vec, (512, 128), (48, 128)],
    )(flags, force, eta, density, *x0, *y0, *z0)
    x1 = exchange(up, down, "gx")
    up, down = call(pack_y1, [(54, 8, 128)] * 2)(flags, own1, *x1)
    y1 = exchange(up, down, "gy")
    up, down = call(pack_z1, [(18, 40, 128)] * 2)(flags, own1, *x1, *y1)
    z1 = exchange(up, down, "gz")
    vec1, one1 = (3, NX1, NY1, 128), (NX1, NY1, 128)
    b1, v1, dinv1, wx1, wy1, wz1, own2, up, down = call(
        coarse,
        [vec1, vec1, one1, one1, one1, one1, (5, 24, 128), (5, 16, 128), (5, 16, 128)],
        [one1, one1, one1, vec1, (240, 128), (48, 128)],
    )(flags, own1, *x1, *y1, *z1)
    y2 = exchange(up, down, "gy")
    (chunk,) = call(pack_x2, [(8, 168, 128)])(flags, own2, *y2)
    got = lax.all_to_all(chunk, "gx", 0, 0, tiled=True)
    vec2, one2 = (3, NX2, NY2, 128), (NX2, NY2, 128)
    vec3, one3 = (3, NX3, NY3, 128), (NX3, NY3, 128)
    velocity, new_density = call(
        finish,
        [(3, 8, 32, 128), (8, 32, 128)],
        [vec2, one2, one2, one2, one2, one2, one2, one2, vec2, vec2]
        + [vec3, one3, one3, one3, one3, one3, one3, one3, vec3, vec3]
        + [(960, 128), (576, 128), (48, 128), (3, 20, 24, 128), vec1, vec1, vec, vec, (576, 256)],
    )(flags, got, b1, v1, dinv1, wx1, wy1, wz1, b0, v0, dinv0, wx0, wy0, wz0, den)
    return velocity, new_density


def solution(mesh):
    return jax.shard_map(
        per_device,
        mesh=mesh,
        in_specs=(P(None, "gx", "gy", "gz"), P("gx", "gy", "gz"), P("gx", "gy", "gz")),
        out_specs=(P(None, "gx", "gy", "gz"), P("gx", "gy", "gz")),
        check_vma=False,
    )
```

```python
import jax
import jax.numpy as jnp
from jax import lax
from jax.experimental import pallas as pl
from jax.experimental.pallas import tpu as pltpu
from jax.sharding import PartitionSpec as P

OMEGA = 0.8
STEP_TIME = 0.1
DIFFUSION = 0.05
grain_table = [0.5 * 8.0 ** (entry / 15.0) for entry in range(16)]
F32 = jnp.float32
MIB = 1024 * 1024

W0 = (4, 4, 4, 5, 4)
OFF0 = (0, 4, 8, 12, 17)
NX0, NY0, NZ0 = 18, 48, 256
W1 = (5, 5, 5, 6, 5)
OFF1 = (0, 5, 10, 15, 21)
NX1, NY1 = 16, 48
PIECE1 = (0, 14, 28, 42, 58)
PIECES1 = [(f, x) for f in range(5) for x in range(-W1[f], 4 + W1[f])]
NX2, NY2 = 10, 48
NX3, NY3 = 6, 24


def iota(shape, dim):
    return lax.broadcasted_iota(jnp.int32, shape, dim)


def back(value, axis):
    return pltpu.roll(value, value.shape[axis] - 1, axis)


def forth(value, axis):
    return pltpu.roll(value, 1, axis)


def turn(value, shift, axis):
    shift = shift % value.shape[axis]
    return value if shift == 0 else pltpu.roll(value, shift, axis)


def call(body, outs, scratch=(), limit=12, start=False, final=False):
    def run(flags, *operands):
        if not final:
            shapes = [pltpu.VMEM(s, F32) for s in outs]
        else:
            shapes = [jax.ShapeDtypeStruct(s, F32) for s in outs]
        return pl.pallas_call(
            body,
            out_shape=shapes,
            in_specs=[pl.BlockSpec(memory_space=pltpu.SMEM)]
            + [pl.BlockSpec(memory_space=pltpu.VMEM)] * len(operands),
            out_specs=[pl.BlockSpec(memory_space=pltpu.VMEM)] * len(outs),
            scratch_shapes=[pltpu.VMEM(s, F32) for s in scratch],
            compiler_params=pltpu.CompilerParams(vmem_limit_bytes=limit * MIB),
        )(flags, *[pltpu.with_memory_space_constraint(o, pltpu.HBM if start else pltpu.VMEM) for o in operands])

    return run


def flag(flags, index):
    return flags[index].astype(F32)


def weighted(v, w, c, x, xp, xm):
    wx, wy, wz = w
    here = v[c, x]
    total = wx[x] * v[c, xp] + wx[xm] * v[c, xm]
    a = wy[x]
    total = total + a * back(here, 0) + forth(a * here, 0)
    a = wz[x]
    total = total + a * back(here, 1) + forth(a * here, 1)
    return here, total


def planes(lo, hi, n, body, unroll=2):
    assert (hi - lo) % unroll == 0

    def step(k, carry):
        for j in range(unroll):
            x = lax.rem(unroll * k + (lo + n + j), n)
            body(x, lax.rem(x + 1, n), lax.rem(x + n - 1, n))
        return carry

    lax.fori_loop(0, (hi - lo) // unroll, step, 0)


def sweep(dst, src, b, w, dinv, lo, hi, n, unroll=2):
    def body(x, xp, xm):
        scale = dinv[x]
        for c in range(3):
            here, total = weighted(src, w, c, x, xp, xm)
            dst[c, x] = 0.2 * here + scale * (b[c, x] + total)

    planes(lo, hi, n, body, unroll)


def weights(eta, w, factor, lo, hi, n, unroll=2):
    wx, wy, wz = w
    half = 0.5 * factor

    def body(x, xp, xm):
        here = eta[x]
        wx[x] = half * (here + eta[xp])
        wy[x] = half * (here + back(here, 0))
        wz[x] = half * (here + back(here, 1))

    planes(lo, hi, n, body, unroll)


def diagonals(kap, w, dg, dinv, lo, hi, n):
    wx, wy, wz = w

    def body(x, xp, xm):
        k, a, g = kap[x], wy[x], wz[x]
        d = k + (wx[x] + wx[xm]) + (a + forth(a, 0)) + (g + forth(g, 1))
        inside = k > 0.0
        dg[x] = d
        dinv[x] = jnp.where(inside, OMEGA / jnp.where(inside, d, 1.0), 0.0)

    planes(lo, hi, n, body)


def first(v, b, dinv, lo, hi, n):
    def body(x, xp, xm):
        for c in range(3):
            v[c, x] = dinv[x] * b[c, x]

    planes(lo, hi, n, body)


def rest(v, b, w, dg, c, x, xp, xm):
    here, total = weighted(v, w, c, x, xp, xm)
    return b[c, x] - dg[x] * here + total


def mean_matrix(source):
    k, j = iota((128, 128), 0), iota((128, 128), 1)
    return jnp.where((k >> 1) == source(j), 0.125, 0.0).astype(F32)


def repeat_matrix(source, out=128):
    k, j = iota((128, out), 0), iota((128, out), 1)
    return jnp.where(k == source(j), 1.0, 0.0).astype(F32)


def mean1(j):
    return j & 63


def mean2(j):
    return (j + 48) & 63


def mean3(j):
    return jnp.where((j & 63) < 32, ((j >> 6) << 5) + (j & 63), -1)


def repeat2(j):
    return (j & 64) + ((j & 63) >> 1)


def repeat1(j):
    return ((j >> 1) + 16) & 63


def repeat0(j):
    return j >> 1


def dot(a, b):
    return jnp.dot(a, b, precision=lax.Precision.HIGHEST, preferred_element_type=F32)


def row_pairs(tmp, value):
    rows = value.shape[0]
    tmp[pl.ds(0, rows), :] = value
    return tmp[pl.ds(0, rows // 2, stride=2), :] + tmp[pl.ds(1, rows // 2, stride=2), :]


def prepare(flags, force, grain, dens, eta, force_kept, dens_kept, up, down):
    for x in range(8):
        ids = grain[x]
        looked = jnp.full(ids.shape, grain_table[0], F32)
        for entry in range(1, 16):
            looked = jnp.where(ids == entry, grain_table[entry], looked)
        d = dens[x]
        eta[x] = looked * d * d * d
        dens_kept[x] = d
        for c in range(3):
            force_kept[c, x] = force[c, x]
    for f in range(5):
        for k in range(W0[f]):
            for out, x in ((up, 8 - W0[f] + k), (down, k)):
                out[OFF0[f] + k] = force[f, x] if f < 3 else (eta if f == 3 else dens)[x]


def plane0(flags, own, f, x, rows):
    force, eta, dens, low, high = own
    if 0 <= x < 8:
        return force[f, x, rows] if f < 3 else (eta if f == 3 else dens)[x, rows]
    away = x - 8 if x >= 8 else -x - 1
    if away >= W0[f]:
        return jnp.zeros((rows.stop - rows.start, 128), F32)
    if x >= 8:
        return high[OFF0[f] + away, rows] * flag(flags, 1)
    return low[OFF0[f] + W0[f] - 1 - away, rows] * flag(flags, 0)


def rel0(x):
    return x if x < 13 else x - NX0


YF = (0, 1, 2, 4, 3)


def pack_y0(flags, force, eta, dens, low, high, up, down):
    own = (force, eta, dens, low, high)
    sub = iota((8, 128), 0)
    for i, f in enumerate(YF):
        for q in range(9):
            a, b = rel0(2 * q), rel0(2 * q + 1)
            top, bottom = slice(24, 32), slice(0, 8)
            up[9 * i + q] = jnp.where(
                sub < 4, turn(plane0(flags, own, f, a, top), 4, 0), plane0(flags, own, f, b, top)
            )
            down[9 * i + q] = jnp.where(
                sub < 4, plane0(flags, own, f, a, bottom), turn(plane0(flags, own, f, b, bottom), 4, 0)
            )
    for t in range(3):
        hi, lo = jnp.zeros((8, 128), F32), jnp.zeros((8, 128), F32)
        for s in range(8):
            if 8 * t + s < NX0:
                x = rel0(8 * t + s)
                hi = jnp.where(sub == s, turn(plane0(flags, own, 3, x, slice(24, 32)), s - 3, 0), hi)
                lo = jnp.where(sub == s, turn(plane0(flags, own, 3, x, slice(0, 8)), s - 4, 0), lo)
        up[45 + t], down[45 + t] = hi, lo


def rows0(flags, own, lowy, highy, f, x):
    sub = iota((8, 128), 0)
    i = YF.index(f)
    high, low = highy[9 * i + x // 2], lowy[9 * i + x // 2]
    if x % 2:
        high = turn(high, 4, 0)
    else:
        low = turn(low, 4, 0)
    if f == 3:
        high = jnp.where(sub == 4, turn(highy[45 + x // 8], 4 - x % 8, 0), high)
        low = jnp.where(sub == 3, turn(lowy[45 + x // 8], 3 - x % 8, 0), low)
    middle = plane0(flags, own, f, rel0(x), slice(0, 32))
    return jnp.concatenate([middle, high * flag(flags, 3), low * flag(flags, 2)], axis=0)


def pack_z0(flags, force, eta, dens, lowx, highx, lowy, highy, rows, up, down):
    own = (force, eta, dens, lowx, highx)
    lane = iota((NY0, 128), 1)
    for g in range(3):
        hi, lo = jnp.zeros((NY0, 128), F32), jnp.zeros((NY0, 128), F32)
        for s in range(6):
            for f in range(5):
                at, w = 21 * s + OFF0[f], W0[f]
                value = rows0(flags, own, lowy, highy, f, 6 * g + s)
                rows[f, 6 * g + s] = value
                there = (lane >= at) & (lane < at + w)
                hi = jnp.where(there, turn(value, at - (128 - w), 1), hi)
                lo = jnp.where(there, turn(value, at, 1), lo)
        up[g], down[g] = hi, lo


def fine(flags, rows, lowz, highz,
         b, v, dinv, wx, wy, wz, den, own1, up, down,
         eta0, kap, dg, v0, pairs, tmp):
    lane = iota((NY0, 128), 1)
    for x in range(NX0):
        for f in range(5):
            at, w = 21 * (x % 6) + OFF0[f], W0[f]
            middle = rows[f, x]
            high = turn(highz[x // 6], -at, 1) * flag(flags, 5)
            low = turn(lowz[x // 6], 128 - w - at, 1) * flag(flags, 4)
            beyond = jnp.where(lane < w, high, jnp.where(lane >= 128 - w, low, 0.0))
            if f < 3:
                b[f, x, :, 0:128] = middle
                b[f, x, :, 128:256] = beyond
            elif f == 3:
                eta0[x, :, 0:128] = middle
                eta0[x, :, 128:256] = beyond
            else:
                den[x, :, 0:128] = middle
                den[x, :, 128:256] = beyond
                for half, value in ((slice(0, 128), middle), (slice(128, 256), beyond)):
                    kap[x, :, half] = jnp.where(value > 0.0, 0.02 + 0.08 * value, 0.0)
    w = (wx, wy, wz)
    weights(eta0, w, 1.0, -5, 13, NX0)
    diagonals(kap, w, dg, dinv, -4, 12, NX0)
    first(v0, b, dinv, -4, 12, NX0)
    sweep(v, v0, b, w, dinv, -3, 11, NX0)

    def blocks(i, carry):
        x0 = lax.rem(2 * i + NX0 - 2, NX0)
        xm, xp, xq = lax.rem(x0 + NX0 - 1, NX0), lax.rem(x0 + 1, NX0), lax.rem(x0 + 2, NX0)
        for c in range(3):
            r = rest(v, b, w, dg, c, x0, xp, xm) + rest(v, b, w, dg, c, xp, xq, x0)
            at = pl.multiple_of((c * 6 + i) * 16, 16)
            pairs[pl.ds(at, 16), :] = row_pairs(tmp, r[0:32, 0:128])
        return carry

    lax.fori_loop(0, 6, blocks, 0)
    for i in range(-2, 6):
        x = (2 * i) % NX0
        r = eta0[x, 0:32, 0:128] + eta0[x + 1, 0:32, 0:128]
        pairs[pl.ds((18 + i + 2) * 16, 16), :] = row_pairs(tmp, r)
        if -1 <= i < 5:
            r = kap[x, 0:32, 0:128] + kap[x + 1, 0:32, 0:128]
            pairs[pl.ds((26 + i + 1) * 16, 16), :] = row_pairs(tmp, r)
    pairs[...] = dot(pairs[...], mean_matrix(mean1))

    def piece(f, i):
        at = f * 6 + i + 1 if f < 3 else (20 + i if f == 3 else 27 + i)
        return pairs[pl.ds(at * 16, 16), :]

    half = iota((16, 128), 1) < 64
    ups = [(f, i) for f in range(5) for i in range(4 - W1[f], 4)]
    downs = [(f, i) for f in range(5) for i in range(0, W1[f])]
    for k in range(13):
        up[k] = jnp.where(half, piece(*ups[2 * k]), piece(*ups[2 * k + 1]))
        down[k] = jnp.where(half, piece(*downs[2 * k]), piece(*downs[2 * k + 1]))
    for f in range(5):
        for i in range(4):
            own1[f, i] = piece(f, i)


def twice(value, half):
    left = iota(value.shape, 1) < 64
    other = pltpu.roll(value, 64, 1)
    return jnp.where(left, value, other) if half == 0 else jnp.where(left, other, value)


def plane1(flags, own1, lowx, highx, f, x, rows):
    if 0 <= x < 4:
        return own1[f, x, rows]
    away = x - 4 if x >= 4 else -x - 1
    if x >= 4:
        at = OFF1[f] + away
        return twice(highx[at // 2, rows], at % 2) * flag(flags, 1)
    at = OFF1[f] + W1[f] - 1 - away
    return twice(lowx[at // 2, rows], at % 2) * flag(flags, 0)


def pack_y1(flags, own1, lowx, highx, up, down):
    sub = iota((8, 128), 0)
    left = iota((16, 128), 1) < 64
    for u in range(0, 36, 2):
        two = []
        for k in range(2):
            a, b = PIECES1[2 * (u + k)], PIECES1[2 * (u + k) + 1]
            value = jnp.where(
                left,
                plane1(flags, own1, lowx, highx, *a, slice(0, 16)),
                plane1(flags, own1, lowx, highx, *b, slice(0, 16)),
            )
            two.append((value[0:8], value[8:16]))
            up[u + k], down[u + k] = value[8:16], value[0:8]
        (a0, a1), (b0, b1) = two
        up[36 + u // 2] = jnp.where(sub < 4, turn(a0, 4, 0), b0)
        down[36 + u // 2] = jnp.where(sub < 4, a1, turn(b1, 4, 0))


def rows1(flags, own1, lowx, highx, lowy, highy, f, x):
    p = PIECE1[f] + x + W1[f]
    u = p // 2
    high, low = highy[36 + u // 2], lowy[36 + u // 2]
    if u % 2:
        high = turn(high, 4, 0)
    else:
        low = turn(low, 4, 0)
    above = twice(jnp.concatenate([highy[u], high], axis=0), p % 2) * flag(flags, 3)
    below = twice(jnp.concatenate([low, lowy[u]], axis=0), p % 2) * flag(flags, 2)
    return jnp.concatenate([plane1(flags, own1, lowx, highx, f, x, slice(0, 16)), above, below], axis=0)


def pack_z1(flags, own1, lowx, highx, lowy, highy, rows, up, down):
    sub = iota((8, 128), 0)
    slot = iota((40, 128), 1) >> 5
    for g in range(18):
        hi, lo = None, None
        for s in range(4):
            value = rows1(flags, own1, lowx, highx, lowy, highy, *PIECES1[4 * g + s])
            rows[4 * g + s] = value
            mix = jnp.where(sub < 4, value[24:32], value[32:40])
            value = jnp.concatenate([value[0:24], mix, value[40:48]], axis=0)
            moved = pltpu.roll(value, 32, 1)
            a, b = (value, moved) if s % 2 else (moved, value)
            hi = a if s == 0 else jnp.where(slot == s, a, hi)
            lo = b if s == 0 else jnp.where(slot == s, b, lo)
        up[g], down[g] = hi, lo


def coarse(flags, rows, lowz, highz,
           b, v, dinv, wx, wy, wz, own2, up, down,
           eta, kap, dg, v0, pairs, tmp):
    lane = iota((NY1, 128), 1)
    for x in range(NX1):
        kap[x] = jnp.zeros((NY1, 128), F32)
    for p, (f, x) in enumerate(PIECES1):
        g, s = p // 4, p % 4
        middle = rows[p]
        high = turn(highz[g], 64 - 32 * s, 1) * flag(flags, 5)
        low = turn(lowz[g], 96 - 32 * s, 1) * flag(flags, 4)
        high = jnp.concatenate([high[0:32], high[24:40]], axis=0)
        low = jnp.concatenate([low[0:32], low[24:40]], axis=0)
        value = jnp.where(lane < 64, middle, jnp.where(lane < 96, high, low))
        if f < 3:
            b[f, x % NX1] = value
        else:
            (eta if f == 3 else kap)[x % NX1] = value
    w = (wx, wy, wz)
    weights(eta, w, 0.25, -6, 10, NX1)
    diagonals(kap, w, dg, dinv, -5, 9, NX1)
    first(v0, b, dinv, -5, 9, NX1)
    sweep(v, v0, b, w, dinv, -4, 8, NX1)

    def blocks(i, carry):
        x0 = 2 * i
        for c in range(3):
            r = rest(v, b, w, dg, c, x0, x0 + 1, lax.rem(x0 + NX1 - 1, NX1))
            r = r + rest(v, b, w, dg, c, x0 + 1, x0 + 2, x0)
            at = pl.multiple_of((c * 2 + i) * 24, 8)
            pairs[pl.ds(at, 24), :] = row_pairs(tmp, r)
        at = pl.multiple_of((6 + i) * 24, 8)
        pairs[pl.ds(at, 24), :] = row_pairs(tmp, eta[x0] + eta[x0 + 1])
        at = pl.multiple_of((8 + i) * 24, 8)
        pairs[pl.ds(at, 24), :] = row_pairs(tmp, kap[x0] + kap[x0 + 1])
        return carry

    lax.fori_loop(0, 2, blocks, 0)
    pairs[...] = dot(pairs[...], mean_matrix(mean2))
    left = iota((24, 128), 1) < 64
    for f in range(5):
        value = jnp.where(left, pairs[pl.ds(48 * f, 24), :], pairs[pl.ds(48 * f + 24, 24), :])
        own2[f] = value
        up[f, 0:8], up[f, 8:16] = value[16:24], value[0:8]
        down[f] = value[0:16]


def pack_x2(flags, own2, lowy, highy, out):
    sub = iota((8, 128), 0)
    for f in range(5):
        near, far = highy[f, 0:8] * flag(flags, 3), highy[f, 8:16] * flag(flags, 3)
        far_low, near_low = lowy[f, 0:8] * flag(flags, 2), lowy[f, 8:16] * flag(flags, 2)
        value = jnp.concatenate([own2[f, 0:8], near, jnp.where(sub < 4, far, far_low), near_low], axis=0)
        for d in range(8):
            out[d, 32 * f:32 * f + 32] = value
        if f == 3:
            for d in range(8):
                out[d, 160:168] = jnp.where(sub == 4, far, far_low)


def finish(flags, got, b1, v1, dinv1, wx1, wy1, wz1, b0, v0, dinv0, wx0, wy0, wz0, den,
           velocity, new_density,
           b2, eta2, kap2, dg2, dinv2, wx2, wy2, wz2, va2, vb2,
           b3, eta3, kap3, dg3, dinv3, wx3, wy3, wz3, va3, vb3,
           pairs, spread, tmp, e2, va1, vb1, va0, vb0, wide):
    sub = iota((8, 128), 0)
    left2, left3 = iota((NY2, 128), 1) < 64, iota((NY3, 128), 1) < 64
    for f in range(5):
        two = []
        for d in range(8):
            own, near = got[d, 32 * f:32 * f + 8], got[d, 32 * f + 8:32 * f + 16]
            mix, low = got[d, 32 * f + 16:32 * f + 24], got[d, 32 * f + 24:32 * f + 32]
            far, far_low = mix, mix
            if f == 3:
                extra = got[d, 160:168]
                far, far_low = jnp.where(sub == 4, extra, mix), jnp.where(sub == 3, extra, mix)
            two.append(jnp.concatenate([own, near, far, mix, far_low, low], axis=0))
        for d in range(4):
            even = jnp.where(left2, two[d], pltpu.roll(two[d + 4], 64, 1))
            odd = jnp.where(left2, pltpu.roll(two[d], 64, 1), two[d + 4])
            if f < 3:
                b2[f, 2 * d], b2[f, 2 * d + 1] = even, odd
            else:
                out = eta2 if f == 3 else kap2
                out[2 * d], out[2 * d + 1] = even, odd

    def ends(ref, n, left, lead=()):
        first_plane, last_plane = ref[lead + (0,)], ref[lead + (n - 1,)]
        ref[lead + (n,)] = jnp.where(left, pltpu.roll(first_plane, 64, 1), 0.0)
        ref[lead + (n + 1,)] = jnp.where(left, 0.0, pltpu.roll(last_plane, 64, 1))

    def ends2(ref):
        for c in range(3):
            ends(ref, 8, left2, (c,))

    def ends3(ref):
        for c in range(3):
            ends(ref, 4, left3, (c,))

    w2 = (wx2, wy2, wz2)
    ends(eta2, 8, left2)
    weights(eta2, w2, 0.0625, -1, 8, NX2, 3)
    diagonals(kap2, w2, dg2, dinv2, 0, 8, NX2)
    first(va2, b2, dinv2, 0, 8, NX2)
    ends2(va2)
    sweep(vb2, va2, b2, w2, dinv2, 0, 8, NX2, 4)
    ends2(vb2)

    def blocks(i, carry):
        x0 = 2 * i
        xm, xp, xq = lax.rem(x0 + NX2 - 1, NX2), x0 + 1, x0 + 2
        for c in range(3):
            r = rest(vb2, b2, w2, dg2, c, x0, xp, xm) + rest(vb2, b2, w2, dg2, c, xp, xq, x0)
            pairs[pl.ds(pl.multiple_of((c * 4 + i) * 24, 8), 24), :] = row_pairs(tmp.at[c], r)
        pairs[pl.ds(pl.multiple_of((12 + i) * 24, 8), 24), :] = row_pairs(tmp.at[3], eta2[x0] + eta2[xp])
        pairs[pl.ds(pl.multiple_of((16 + i) * 24, 8), 24), :] = row_pairs(tmp.at[4], kap2[x0] + kap2[xp])
        return carry

    lax.fori_loop(0, 4, blocks, 0)
    pairs[pl.ds(0, 480), :] = dot(pairs[pl.ds(0, 480), :], mean_matrix(mean3))
    for i in range(4):
        for c in range(3):
            b3[c, i] = pairs[pl.ds((c * 4 + i) * 24, 24), :]
        eta3[i] = pairs[pl.ds((12 + i) * 24, 24), :]
        kap3[i] = pairs[pl.ds((16 + i) * 24, 24), :]
    w3 = (wx3, wy3, wz3)
    ends(eta3, 4, left3)
    weights(eta3, w3, 0.015625, -1, 4, NX3, 5)
    diagonals(kap3, w3, dg3, dinv3, 0, 4, NX3)
    first(va3, b3, dinv3, 0, 4, NX3)
    ends3(va3)
    sweep(vb3, va3, b3, w3, dinv3, 0, 4, NX3, 4)
    ends3(vb3)
    sweep(va3, vb3, b3, w3, dinv3, 0, 4, NX3, 4)
    ends3(va3)
    sweep(vb3, va3, b3, w3, dinv3, 0, 4, NX3, 4)

    for c in range(3):
        for i in range(4):
            pairs[pl.ds((c * 4 + i) * 24, 24), :] = vb3[c, i]
    spread[pl.ds(0, 288), :] = dot(pairs[pl.ds(0, 288), :], repeat_matrix(repeat2))

    def rise2(i, carry):
        for c in range(3):
            e = spread[pl.ds(pl.multiple_of((c * 4 + i) * 24, 8), 24), :]
            tmp[c, pl.ds(0, 24, stride=2), :] = e
            tmp[c, pl.ds(1, 24, stride=2), :] = e
            e = tmp[c]
            vb2[c, 2 * i] = vb2[c, 2 * i] + e
            vb2[c, 2 * i + 1] = vb2[c, 2 * i + 1] + e
        return carry

    lax.fori_loop(0, 4, rise2, 0)
    ends2(vb2)
    sweep(va2, vb2, b2, w2, dinv2, 0, 8, NX2, 4)
    ends2(va2)
    sweep(vb2, va2, b2, w2, dinv2, 0, 8, NX2, 4)

    none = jnp.zeros((24, 128), F32)
    for c in range(3):
        for x in (0, 1, 18, 19):
            e2[c, x] = none
        for x in range(8):
            value = jnp.concatenate([vb2[c, x, 0:16], vb2[c, x, 40:48]], axis=0)
            e2[c, 2 + x] = value
            e2[c, 10 + x] = pltpu.roll(value, 64, 1)
    start = 2 * flags[6]
    for c in range(3):
        for k in range(6):
            pairs[pl.ds((c * 6 + k) * 24, 24), :] = e2[c, start + k]
    spread[pl.ds(0, 432), :] = dot(pairs[pl.ds(0, 432), :], repeat_matrix(repeat1))

    def rise1(k, carry):
        x = lax.rem(2 * k - 4 + NX1, NX1)
        for c in range(3):
            e = spread[pl.ds(pl.multiple_of((c * 6 + k) * 24, 8), 24), :]
            tmp[c, pl.ds(0, 24, stride=2), :] = e
            tmp[c, pl.ds(1, 24, stride=2), :] = e
            e = tmp[c]
            va1[c, x] = v1[c, x] + e
            va1[c, x + 1] = v1[c, x + 1] + e
        return carry

    lax.fori_loop(0, 6, rise1, 0)
    w1 = (wx1, wy1, wz1)
    sweep(vb1, va1, b1, w1, dinv1, -3, 7, NX1)
    sweep(va1, vb1, b1, w1, dinv1, -2, 6, NX1)

    for c in range(3):
        for i in range(-2, 6):
            at = (c * 8 + i + 2) * 24
            x = i % NX1
            pairs[pl.ds(at, 16), :] = va1[c, x, 0:16]
            pairs[pl.ds(at + 16, 8), :] = jnp.where(sub < 4, va1[c, x, 16:24], va1[c, x, 40:48])
    wide[...] = dot(pairs[pl.ds(0, 576), :], repeat_matrix(repeat0, 256))

    def rise0(i, carry):
        x = lax.rem(2 * i - 4 + NX0, NX0)
        for c in range(3):
            at = pl.multiple_of((c * 8 + i) * 24, 8)
            for half in range(2):
                lanes = slice(128 * half, 128 * half + 128)
                e = wide[pl.ds(at, 24), lanes]
                here = tmp.at[2 * c + half]
                here[pl.ds(0, 24, stride=2), :] = e
                here[pl.ds(1, 24, stride=2), :] = e
                e = here[...]
                va0[c, x, :, lanes] = v0[c, x, :, lanes] + e
                va0[c, x + 1, :, lanes] = v0[c, x + 1, :, lanes] + e
        return carry

    lax.fori_loop(0, 8, rise0, 0)
    w0 = (wx0, wy0, wz0)
    sweep(vb0, va0, b0, w0, dinv0, -2, 10, NX0)
    sweep(va0, vb0, b0, w0, dinv0, -1, 9, NX0)

    def advect(x, carry):
        xm, xp = lax.rem(x + NX0 - 1, NX0), x + 1
        d = den[x]
        change = jnp.zeros_like(d)
        spreading = -6.0 * d
        for axis in range(3):
            u = va0[axis, x]
            if axis == 0:
                u_up, u_lo, d_up, d_lo = va0[0, xp], va0[0, xm], den[xp], den[xm]
            else:
                u_up, u_lo = back(u, axis - 1), forth(u, axis - 1)
                d_up, d_lo = back(d, axis - 1), forth(d, axis - 1)
            hi, lo = 0.5 * (u + u_up), 0.5 * (u_lo + u)
            change = change + (jnp.maximum(hi, 0.0) * d + jnp.minimum(hi, 0.0) * d_up)
            change = change - (jnp.maximum(lo, 0.0) * d_lo + jnp.minimum(lo, 0.0) * d)
            spreading = spreading + (d_up + d_lo)
            velocity[axis, x] = u[0:32, 0:128]
        out = d - STEP_TIME * change + STEP_TIME * DIFFUSION * spreading
        new_density[x] = out[0:32, 0:128]
        return carry

    lax.fori_loop(0, 8, advect, 0)


def exchange(up, down, axis):
    n = lax.axis_size(axis)
    low = lax.ppermute(up, axis, [(i, (i + 1) % n) for i in range(n)])
    high = lax.ppermute(down, axis, [(i, (i - 1) % n) for i in range(n)])
    return low, high


def per_device(force, grain, density):
    gx, gy, gz = (lax.axis_index(a) for a in ("gx", "gy", "gz"))
    last = [lax.axis_size(a) - 1 for a in ("gx", "gy", "gz")]
    flags = jnp.stack(
        [gx > 0, gx < last[0], gy > 0, gy < last[1], gz > 0, gz < last[2], gx, gx]
    ).astype(jnp.int32)

    eta, force, density, up, down = call(
        prepare, [(8, 32, 128), (3, 8, 32, 128), (8, 32, 128), (21, 32, 128), (21, 32, 128)], start=True
    )(flags, force, grain, density)
    x0 = exchange(up, down, "gx")
    up, down = call(pack_y0, [(48, 8, 128)] * 2)(flags, force, eta, density, *x0)
    y0 = exchange(up, down, "gy")
    rows, up, down = call(pack_z0, [(5, 18, 48, 128)] + [(3, 48, 128)] * 2)(flags, force, eta, density, *x0, *y0)
    z0 = exchange(up, down, "gz")
    vec, one = (3, NX0, NY0, NZ0), (NX0, NY0, NZ0)
    b0, v0, dinv0, wx0, wy0, wz0, den, own1, up, down = call(
        fine,
        [vec, vec, one, one, one, one, one, (5, 4, 16, 128), (13, 16, 128), (13, 16, 128)],
        [one, one, one, vec, (512, 128), (48, 128)],
    )(flags, rows, *z0)
    x1 = exchange(up, down, "gx")
    up, down = call(pack_y1, [(54, 8, 128)] * 2)(flags, own1, *x1)
    y1 = exchange(up, down, "gy")
    rows, up, down = call(pack_z1, [(72, 48, 128)] + [(18, 40, 128)] * 2)(flags, own1, *x1, *y1)
    z1 = exchange(up, down, "gz")
    vec1, one1 = (3, NX1, NY1, 128), (NX1, NY1, 128)
    b1, v1, dinv1, wx1, wy1, wz1, own2, up, down = call(
        coarse,
        [vec1, vec1, one1, one1, one1, one1, (5, 24, 128), (5, 16, 128), (5, 16, 128)],
        [one1, one1, one1, vec1, (240, 128), (48, 128)],
    )(flags, rows, *z1)
    y2 = exchange(up, down, "gy")
    (chunk,) = call(pack_x2, [(8, 168, 128)])(flags, own2, *y2)
    got = lax.all_to_all(chunk, "gx", 0, 0, tiled=True)
    vec2, one2 = (3, NX2, NY2, 128), (NX2, NY2, 128)
    vec3, one3 = (3, NX3, NY3, 128), (NX3, NY3, 128)
    velocity, new_density = call(
        finish,
        [(3, 8, 32, 128), (8, 32, 128)],
        [vec2, one2, one2, one2, one2, one2, one2, one2, vec2, vec2]
        + [vec3, one3, one3, one3, one3, one3, one3, one3, vec3, vec3]
        + [(576, 128), (576, 128), (6, 48, 128), (3, 20, 24, 128), vec1, vec1, vec, vec, (576, 256)],
        limit=32,
        final=True,
    )(flags, got, b1, v1, dinv1, wx1, wy1, wz1, b0, v0, dinv0, wx0, wy0, wz0, den)
    return velocity, new_density


def solution(mesh):
    return jax.shard_map(
        per_device,
        mesh=mesh,
        in_specs=(P(None, "gx", "gy", "gz"), P("gx", "gy", "gz"), P("gx", "gy", "gz")),
        out_specs=(P(None, "gx", "gy", "gz"), P("gx", "gy", "gz")),
        check_vma=False,
    )
```

```python
import jax
import jax.numpy as jnp
from jax import lax
from jax.experimental import pallas as pl
from jax.experimental.pallas import tpu as pltpu
from jax.sharding import PartitionSpec as P

OMEGA = 0.8
STEP_TIME = 0.1
DIFFUSION = 0.05
grain_table = [0.5 * 8.0 ** (entry / 15.0) for entry in range(16)]
F32 = jnp.float32
MIB = 1024 * 1024

W0 = (2, 2, 2, 3, 2)
OFF0 = (0, 2, 4, 6, 9)
Z0 = (4, 4, 4, 5, 4)
ZOFF0 = (0, 4, 8, 12, 17)
NX0, NY0, NZ0 = 14, 48, 256
LATE = ((0, 3), (0, 2), (0, 1), (1, 2), (1, 1), (2, 2), (2, 1))
W1 = (4, 4, 4, 5, 5)
OFF1 = (0, 4, 8, 12, 17)
H1 = (5, 4, 4, 6, 5)
NX1, NY1 = 16, 48
PIECE1 = (0, 14, 26, 38, 54)
PIECES1 = [(f, x) for f in range(5) for x in range(-H1[f], 4 + H1[f])]
NX2, NY2 = 10, 48
NX3, NY3 = 6, 24


def iota(shape, dim):
    return lax.broadcasted_iota(jnp.int32, shape, dim)


def back(value, axis):
    return pltpu.roll(value, value.shape[axis] - 1, axis)


def forth(value, axis):
    return pltpu.roll(value, 1, axis)


def turn(value, shift, axis):
    shift = shift % value.shape[axis]
    return value if shift == 0 else pltpu.roll(value, shift, axis)


def call(body, outs, scratch=(), limit=12, start=False, final=False):
    def run(flags, *operands):
        if not final:
            shapes = [pltpu.VMEM(s, F32) for s in outs]
        else:
            shapes = [jax.ShapeDtypeStruct(s, F32) for s in outs]
        return pl.pallas_call(
            body,
            out_shape=shapes,
            in_specs=[pl.BlockSpec(memory_space=pltpu.SMEM)]
            + [pl.BlockSpec(memory_space=pltpu.VMEM)] * len(operands),
            out_specs=[pl.BlockSpec(memory_space=pltpu.VMEM)] * len(outs),
            scratch_shapes=[pltpu.VMEM(s, F32) for s in scratch],
            compiler_params=pltpu.CompilerParams(vmem_limit_bytes=limit * MIB),
        )(flags, *[pltpu.with_memory_space_constraint(o, pltpu.HBM if start else pltpu.VMEM) for o in operands])

    return run


def flag(flags, index):
    return flags[index].astype(F32)


def weighted(v, w, c, x, xp, xm):
    wx, wy, wz = w
    here = v[c, x]
    total = wx[x] * v[c, xp] + wx[xm] * v[c, xm]
    a = wy[x]
    total = total + a * back(here, 0) + forth(a * here, 0)
    a = wz[x]
    total = total + a * back(here, 1) + forth(a * here, 1)
    return here, total


def planes(lo, hi, n, body, unroll=2):
    assert (hi - lo) % unroll == 0

    def step(k, carry):
        for j in range(unroll):
            x = lax.rem(unroll * k + (lo + n + j), n)
            body(x, lax.rem(x + 1, n), lax.rem(x + n - 1, n))
        return carry

    lax.fori_loop(0, (hi - lo) // unroll, step, 0)


def sweep(dst, src, b, w, dinv, lo, hi, n, unroll=2):
    def body(x, xp, xm):
        scale = dinv[x]
        for c in range(3):
            here, total = weighted(src, w, c, x, xp, xm)
            dst[c, x] = 0.2 * here + scale * (b[c, x] + total)

    planes(lo, hi, n, body, unroll)


def weights(eta, w, factor, lo, hi, n, unroll=2):
    wx, wy, wz = w
    half = 0.5 * factor

    def body(x, xp, xm):
        here = eta[x]
        wx[x] = half * (here + eta[xp])
        wy[x] = half * (here + back(here, 0))
        wz[x] = half * (here + back(here, 1))

    planes(lo, hi, n, body, unroll)


def diagonals(kap, w, dg, dinv, lo, hi, n):
    wx, wy, wz = w

    def body(x, xp, xm):
        k, a, g = kap[x], wy[x], wz[x]
        d = k + (wx[x] + wx[xm]) + (a + forth(a, 0)) + (g + forth(g, 1))
        inside = k > 0.0
        dg[x] = d
        dinv[x] = jnp.where(inside, OMEGA / jnp.where(inside, d, 1.0), 0.0)

    planes(lo, hi, n, body)


def first(v, b, dinv, lo, hi, n):
    def body(x, xp, xm):
        for c in range(3):
            v[c, x] = dinv[x] * b[c, x]

    planes(lo, hi, n, body)


def rest(v, b, w, dg, c, x, xp, xm):
    here, total = weighted(v, w, c, x, xp, xm)
    return b[c, x] - dg[x] * here + total


def mean_matrix(source):
    k, j = iota((128, 128), 0), iota((128, 128), 1)
    return jnp.where((k >> 1) == source(j), 0.125, 0.0).astype(F32)


def repeat_matrix(source, out=128):
    k, j = iota((128, out), 0), iota((128, out), 1)
    return jnp.where(k == source(j), 1.0, 0.0).astype(F32)


def mean1(j):
    return j & 63


def mean2(j):
    return (j + 48) & 63


def mean3(j):
    return jnp.where((j & 63) < 32, ((j >> 6) << 5) + (j & 63), -1)


def repeat2(j):
    return (j & 64) + ((j & 63) >> 1)


def repeat1(j):
    return ((j >> 1) + 16) & 63


def repeat0(j):
    return j >> 1


def dot(a, b):
    return jnp.dot(a, b, precision=lax.Precision.HIGHEST, preferred_element_type=F32)


def row_pairs(tmp, value):
    rows = value.shape[0]
    tmp[pl.ds(0, rows), :] = value
    return tmp[pl.ds(0, rows // 2, stride=2), :] + tmp[pl.ds(1, rows // 2, stride=2), :]


def prepare(flags, force, grain, dens, eta, force_kept, dens_kept, up, down):
    for x in range(8):
        ids = grain[x]
        looked = jnp.full(ids.shape, grain_table[0], F32)
        for entry in range(1, 16):
            looked = jnp.where(ids == entry, grain_table[entry], looked)
        d = dens[x]
        eta[x] = looked * d * d * d
        dens_kept[x] = d
        for c in range(3):
            force_kept[c, x] = force[c, x]
    for f in range(5):
        for k in range(W0[f]):
            for out, x in ((up, 8 - W0[f] + k), (down, k)):
                out[OFF0[f] + k] = force[f, x] if f < 3 else (eta if f == 3 else dens)[x]


def plane0(flags, own, f, x, rows):
    force, eta, dens, low, high = own
    if 0 <= x < 8:
        return force[f, x, rows] if f < 3 else (eta if f == 3 else dens)[x, rows]
    away = x - 8 if x >= 8 else -x - 1
    if away >= W0[f]:
        return jnp.zeros((rows.stop - rows.start, 128), F32)
    if x >= 8:
        return high[OFF0[f] + away, rows] * flag(flags, 1)
    return low[OFF0[f] + W0[f] - 1 - away, rows] * flag(flags, 0)


def rel0(x):
    return x if x < 11 else x - NX0


YF = (0, 1, 2, 4, 3)


def pack_y0(flags, force, eta, dens, low, high, up, down):
    own = (force, eta, dens, low, high)
    sub = iota((8, 128), 0)
    for i, f in enumerate(YF):
        for q in range(7):
            a, b = rel0(2 * q), rel0(2 * q + 1)
            top, bottom = slice(24, 32), slice(0, 8)
            up[7 * i + q] = jnp.where(
                sub < 4, turn(plane0(flags, own, f, a, top), 4, 0), plane0(flags, own, f, b, top)
            )
            down[7 * i + q] = jnp.where(
                sub < 4, plane0(flags, own, f, a, bottom), turn(plane0(flags, own, f, b, bottom), 4, 0)
            )
    for t in range(2):
        hi, lo = jnp.zeros((8, 128), F32), jnp.zeros((8, 128), F32)
        for s in range(8):
            if 8 * t + s < NX0:
                x = rel0(8 * t + s)
                hi = jnp.where(sub == s, turn(plane0(flags, own, 3, x, slice(24, 32)), s - 3, 0), hi)
                lo = jnp.where(sub == s, turn(plane0(flags, own, 3, x, slice(0, 8)), s - 4, 0), lo)
        up[35 + t], down[35 + t] = hi, lo


def rows0(flags, own, lowy, highy, f, x):
    sub = iota((8, 128), 0)
    i = YF.index(f)
    high, low = highy[7 * i + x // 2], lowy[7 * i + x // 2]
    if x % 2:
        high = turn(high, 4, 0)
    else:
        low = turn(low, 4, 0)
    if f == 3:
        high = jnp.where(sub == 4, turn(highy[35 + x // 8], 4 - x % 8, 0), high)
        low = jnp.where(sub == 3, turn(lowy[35 + x // 8], 3 - x % 8, 0), low)
    middle = plane0(flags, own, f, rel0(x), slice(0, 32))
    return jnp.concatenate([middle, high * flag(flags, 3), low * flag(flags, 2)], axis=0)


def pack_z0(flags, force, eta, dens, lowx, highx, lowy, highy, rows, up, down):
    own = (force, eta, dens, lowx, highx)
    lane = iota((NY0, 128), 1)
    for g in range(3):
        hi, lo = jnp.zeros((NY0, 128), F32), jnp.zeros((NY0, 128), F32)
        for s in range(min(6, NX0 - 6 * g)):
            for f in range(5):
                at, w = 21 * s + ZOFF0[f], Z0[f]
                value = rows0(flags, own, lowy, highy, f, 6 * g + s)
                rows[f, 6 * g + s] = value
                there = (lane >= at) & (lane < at + w)
                hi = jnp.where(there, turn(value, at - (128 - w), 1), hi)
                lo = jnp.where(there, turn(value, at, 1), lo)
        up[g], down[g] = hi, lo


def fine(flags, rows, lowz, highz,
         b, v, dinv, wx, wy, wz, den, own1, up, down, far_up, far_down, late_up, late_down,
         eta0, kap, dg, v0, pairs, tmp):
    lane = iota((NY0, 128), 1)
    for x in range(NX0):
        for f in range(5):
            at, w = 21 * (x % 6) + ZOFF0[f], Z0[f]
            middle = rows[f, x]
            high = turn(highz[x // 6], -at, 1) * flag(flags, 5)
            low = turn(lowz[x // 6], 128 - w - at, 1) * flag(flags, 4)
            beyond = jnp.where(lane < w, high, jnp.where(lane >= 128 - w, low, 0.0))
            if f < 3:
                b[f, x, :, 0:128] = middle
                b[f, x, :, 128:256] = beyond
            elif f == 3:
                eta0[x, :, 0:128] = middle
                eta0[x, :, 128:256] = beyond
            else:
                den[x, :, 0:128] = middle
                den[x, :, 128:256] = beyond
                for half, value in ((slice(0, 128), middle), (slice(128, 256), beyond)):
                    kap[x, :, half] = jnp.where(value > 0.0, 0.02 + 0.08 * value, 0.0)
    w = (wx, wy, wz)
    weights(eta0, w, 1.0, -3, 11, NX0)
    diagonals(kap, w, dg, dinv, -2, 10, NX0)
    first(v0, b, dinv, -2, 10, NX0)
    sweep(v, v0, b, w, dinv, -1, 9, NX0)

    def blocks(i, carry):
        x0 = 2 * i
        xm, xp, xq = lax.rem(x0 + NX0 - 1, NX0), x0 + 1, x0 + 2
        for c in range(3):
            r = rest(v, b, w, dg, c, x0, xp, xm) + rest(v, b, w, dg, c, xp, xq, x0)
            at = pl.multiple_of((c * 4 + i) * 16, 16)
            pairs[pl.ds(at, 16), :] = row_pairs(tmp.at[c], r[0:32, 0:128])
        return carry

    lax.fori_loop(0, 4, blocks, 0)
    for i in range(-1, 5):
        x = (2 * i) % NX0
        r = eta0[x, 0:32, 0:128] + eta0[x + 1, 0:32, 0:128]
        pairs[pl.ds((12 + i + 1) * 16, 16), :] = row_pairs(tmp.at[3], r)
        r = kap[x, 0:32, 0:128] + kap[x + 1, 0:32, 0:128]
        pairs[pl.ds((18 + i + 1) * 16, 16), :] = row_pairs(tmp.at[4], r)
    pairs[...] = dot(pairs[...], mean_matrix(mean1))

    def piece(f, i):
        at = f * 4 + i if f < 3 else (13 + i if f == 3 else 19 + i)
        return pairs[pl.ds(at * 16, 16), :]

    half = iota((16, 128), 1) < 64
    ups = [(f, i) for f in range(5) for i in range(4 - W1[f], 4)]
    downs = [(f, i) for f in range(5) for i in range(0, W1[f])]
    for k in range(11):
        up[k] = jnp.where(half, piece(*ups[2 * k]), piece(*ups[2 * k + 1]))
        down[k] = jnp.where(half, piece(*downs[2 * k]), piece(*downs[2 * k + 1]))
    far_up[...] = jnp.where(half, piece(0, 3), piece(3, 2))
    far_down[...] = jnp.where(half, piece(0, 0), piece(3, 1))
    for f in range(5):
        for i in range(4):
            own1[f, i] = piece(f, i)

    sub, slot = iota((8, 128), 0), iota((40, 128), 1) >> 3
    for out, top in ((late_up, True), (late_down, False)):
        edge = jnp.zeros((40, 128), F32)
        for p, (c, away) in enumerate(LATE):
            x = 8 - away if top else away - 1
            for half in range(2):
                value = v[c, x, :, 128 * half:128 * half + 128]
                mix = jnp.where(sub < 4, value[32:40], value[40:48])
                value = jnp.concatenate([value[0:32], mix], axis=0)
                if half == 0:
                    out[p] = value
                else:
                    edge = jnp.where(slot == p, turn(value, 8 * p + 4, 1), edge)
        out[7] = edge


def twice(value, half):
    left = iota(value.shape, 1) < 64
    other = pltpu.roll(value, 64, 1)
    return jnp.where(left, value, other) if half == 0 else jnp.where(left, other, value)


def plane1(flags, own1, lowx, highx, far_low, far_high, f, x, rows):
    if 0 <= x < 4:
        return own1[f, x, rows]
    away = x - 4 if x >= 4 else -x - 1
    if away >= W1[f]:
        if x >= 4:
            return twice(far_high[rows], int(f == 3)) * flag(flags, 8)
        return twice(far_low[rows], int(f == 3)) * flag(flags, 7)
    if x >= 4:
        at = OFF1[f] + away
        return twice(highx[at // 2, rows], at % 2) * flag(flags, 1)
    at = OFF1[f] + W1[f] - 1 - away
    return twice(lowx[at // 2, rows], at % 2) * flag(flags, 0)


def pack_y1(flags, own1, lowx, highx, far_low, far_high, up, down):
    sub = iota((8, 128), 0)
    left = iota((16, 128), 1) < 64
    for u in range(0, 34, 2):
        two = []
        for k in range(2):
            a, b = PIECES1[2 * (u + k)], PIECES1[2 * (u + k) + 1]
            value = jnp.where(
                left,
                plane1(flags, own1, lowx, highx, far_low, far_high, *a, slice(0, 16)),
                plane1(flags, own1, lowx, highx, far_low, far_high, *b, slice(0, 16)),
            )
            two.append((value[0:8], value[8:16]))
            up[u + k], down[u + k] = value[8:16], value[0:8]
        (a0, a1), (b0, b1) = two
        up[34 + u // 2] = jnp.where(sub < 4, turn(a0, 4, 0), b0)
        down[34 + u // 2] = jnp.where(sub < 4, a1, turn(b1, 4, 0))


def rows1(flags, own1, lowx, highx, far_low, far_high, lowy, highy, f, x):
    p = PIECE1[f] + x + H1[f]
    u = p // 2
    high, low = highy[34 + u // 2], lowy[34 + u // 2]
    if u % 2:
        high = turn(high, 4, 0)
    else:
        low = turn(low, 4, 0)
    above = twice(jnp.concatenate([highy[u], high], axis=0), p % 2) * flag(flags, 3)
    below = twice(jnp.concatenate([low, lowy[u]], axis=0), p % 2) * flag(flags, 2)
    return jnp.concatenate([plane1(flags, own1, lowx, highx, far_low, far_high, f, x, slice(0, 16)), above, below], axis=0)


def pack_z1(flags, own1, lowx, highx, far_low, far_high, lowy, highy, rows, up, down):
    sub = iota((8, 128), 0)
    slot = iota((40, 128), 1) >> 5
    for g in range(17):
        hi, lo = None, None
        for s in range(4):
            value = rows1(flags, own1, lowx, highx, far_low, far_high, lowy, highy, *PIECES1[4 * g + s])
            rows[4 * g + s] = value
            mix = jnp.where(sub < 4, value[24:32], value[32:40])
            value = jnp.concatenate([value[0:24], mix, value[40:48]], axis=0)
            moved = pltpu.roll(value, 32, 1)
            a, b = (value, moved) if s % 2 else (moved, value)
            hi = a if s == 0 else jnp.where(slot == s, a, hi)
            lo = b if s == 0 else jnp.where(slot == s, b, lo)
        up[g], down[g] = hi, lo


def coarse(flags, rows, lowz, highz,
           b, v, dinv, wx, wy, wz, own2, up, down,
           eta, kap, dg, v0, pairs, tmp):
    lane = iota((NY1, 128), 1)
    none = jnp.zeros((NY1, 128), F32)
    for x in (-6, 9):
        kap[x % NX1] = none
    for x in (-5, 8):
        for c in (1, 2):
            b[c, x % NX1] = none
    for p, (f, x) in enumerate(PIECES1):
        g, s = p // 4, p % 4
        middle = rows[p]
        high = turn(highz[g], 64 - 32 * s, 1) * flag(flags, 5)
        low = turn(lowz[g], 96 - 32 * s, 1) * flag(flags, 4)
        high = jnp.concatenate([high[0:32], high[24:40]], axis=0)
        low = jnp.concatenate([low[0:32], low[24:40]], axis=0)
        value = jnp.where(lane < 64, middle, jnp.where(lane < 96, high, low))
        if f < 3:
            b[f, x % NX1] = value
        else:
            (eta if f == 3 else kap)[x % NX1] = value
    w = (wx, wy, wz)
    weights(eta, w, 0.25, -6, 10, NX1)
    diagonals(kap, w, dg, dinv, -5, 9, NX1)
    first(v0, b, dinv, -5, 9, NX1)
    sweep(v, v0, b, w, dinv, -4, 8, NX1)

    def blocks(i, carry):
        x0 = 2 * i
        for c in range(3):
            r = rest(v, b, w, dg, c, x0, x0 + 1, lax.rem(x0 + NX1 - 1, NX1))
            r = r + rest(v, b, w, dg, c, x0 + 1, x0 + 2, x0)
            at = pl.multiple_of((c * 2 + i) * 24, 8)
            pairs[pl.ds(at, 24), :] = row_pairs(tmp.at[c], r)
        at = pl.multiple_of((6 + i) * 24, 8)
        pairs[pl.ds(at, 24), :] = row_pairs(tmp.at[3], eta[x0] + eta[x0 + 1])
        at = pl.multiple_of((8 + i) * 24, 8)
        pairs[pl.ds(at, 24), :] = row_pairs(tmp.at[4], kap[x0] + kap[x0 + 1])
        return carry

    lax.fori_loop(0, 2, blocks, 0)
    pairs[...] = dot(pairs[...], mean_matrix(mean2))
    left = iota((24, 128), 1) < 64
    for f in range(5):
        value = jnp.where(left, pairs[pl.ds(48 * f, 24), :], pairs[pl.ds(48 * f + 24, 24), :])
        own2[f] = value
        up[f, 0:8], up[f, 8:16] = value[16:24], value[0:8]
        down[f] = value[0:16]


def pack_x2(flags, own2, lowy, highy, out):
    sub = iota((8, 128), 0)
    for f in range(5):
        near, far = highy[f, 0:8] * flag(flags, 3), highy[f, 8:16] * flag(flags, 3)
        far_low, near_low = lowy[f, 0:8] * flag(flags, 2), lowy[f, 8:16] * flag(flags, 2)
        value = jnp.concatenate([own2[f, 0:8], near, jnp.where(sub < 4, far, far_low), near_low], axis=0)
        for d in range(8):
            out[d, 32 * f:32 * f + 32] = value
        if f == 3:
            for d in range(8):
                out[d, 160:168] = jnp.where(sub == 4, far, far_low)


def finish(flags, got, late_low, late_high, b1, v1, dinv1, wx1, wy1, wz1, b0, v0, dinv0, wx0, wy0, wz0, den,
           velocity, new_density,
           b2, eta2, kap2, dg2, dinv2, wx2, wy2, wz2, va2, vb2,
           b3, eta3, kap3, dg3, dinv3, wx3, wy3, wz3, va3, vb3,
           pairs, spread, tmp, e2, va1, vb1, va0, vb0, wide):
    sub = iota((8, 128), 0)
    left2, left3 = iota((NY2, 128), 1) < 64, iota((NY3, 128), 1) < 64
    for f in range(5):
        two = []
        for d in range(8):
            own, near = got[d, 32 * f:32 * f + 8], got[d, 32 * f + 8:32 * f + 16]
            mix, low = got[d, 32 * f + 16:32 * f + 24], got[d, 32 * f + 24:32 * f + 32]
            far, far_low = mix, mix
            if f == 3:
                extra = got[d, 160:168]
                far, far_low = jnp.where(sub == 4, extra, mix), jnp.where(sub == 3, extra, mix)
            two.append(jnp.concatenate([own, near, far, mix, far_low, low], axis=0))
        for d in range(4):
            even = jnp.where(left2, two[d], pltpu.roll(two[d + 4], 64, 1))
            odd = jnp.where(left2, pltpu.roll(two[d], 64, 1), two[d + 4])
            if f < 3:
                b2[f, 2 * d], b2[f, 2 * d + 1] = even, odd
            else:
                out = eta2 if f == 3 else kap2
                out[2 * d], out[2 * d + 1] = even, odd

    def ends(ref, n, left, lead=()):
        first_plane, last_plane = ref[lead + (0,)], ref[lead + (n - 1,)]
        ref[lead + (n,)] = jnp.where(left, pltpu.roll(first_plane, 64, 1), 0.0)
        ref[lead + (n + 1,)] = jnp.where(left, 0.0, pltpu.roll(last_plane, 64, 1))

    def ends2(ref):
        for c in range(3):
            ends(ref, 8, left2, (c,))

    def ends3(ref):
        for c in range(3):
            ends(ref, 4, left3, (c,))

    w2 = (wx2, wy2, wz2)
    ends(eta2, 8, left2)
    weights(eta2, w2, 0.0625, -1, 8, NX2, 3)
    diagonals(kap2, w2, dg2, dinv2, 0, 8, NX2)
    first(va2, b2, dinv2, 0, 8, NX2)
    ends2(va2)
    sweep(vb2, va2, b2, w2, dinv2, 0, 8, NX2, 4)
    ends2(vb2)

    def blocks(i, carry):
        x0 = 2 * i
        xm, xp, xq = lax.rem(x0 + NX2 - 1, NX2), x0 + 1, x0 + 2
        for c in range(3):
            r = rest(vb2, b2, w2, dg2, c, x0, xp, xm) + rest(vb2, b2, w2, dg2, c, xp, xq, x0)
            pairs[pl.ds(pl.multiple_of((c * 4 + i) * 24, 8), 24), :] = row_pairs(tmp.at[c], r)
        pairs[pl.ds(pl.multiple_of((12 + i) * 24, 8), 24), :] = row_pairs(tmp.at[3], eta2[x0] + eta2[xp])
        pairs[pl.ds(pl.multiple_of((16 + i) * 24, 8), 24), :] = row_pairs(tmp.at[4], kap2[x0] + kap2[xp])
        return carry

    lax.fori_loop(0, 4, blocks, 0)
    pairs[pl.ds(0, 480), :] = dot(pairs[pl.ds(0, 480), :], mean_matrix(mean3))
    for i in range(4):
        for c in range(3):
            b3[c, i] = pairs[pl.ds((c * 4 + i) * 24, 24), :]
        eta3[i] = pairs[pl.ds((12 + i) * 24, 24), :]
        kap3[i] = pairs[pl.ds((16 + i) * 24, 24), :]
    w3 = (wx3, wy3, wz3)
    ends(eta3, 4, left3)
    weights(eta3, w3, 0.015625, -1, 4, NX3, 5)
    diagonals(kap3, w3, dg3, dinv3, 0, 4, NX3)
    first(va3, b3, dinv3, 0, 4, NX3)
    ends3(va3)
    sweep(vb3, va3, b3, w3, dinv3, 0, 4, NX3, 4)
    ends3(vb3)
    sweep(va3, vb3, b3, w3, dinv3, 0, 4, NX3, 4)
    ends3(va3)
    sweep(vb3, va3, b3, w3, dinv3, 0, 4, NX3, 4)

    for c in range(3):
        for i in range(4):
            pairs[pl.ds((c * 4 + i) * 24, 24), :] = vb3[c, i]
    spread[pl.ds(0, 288), :] = dot(pairs[pl.ds(0, 288), :], repeat_matrix(repeat2))

    def rise2(i, carry):
        for c in range(3):
            e = spread[pl.ds(pl.multiple_of((c * 4 + i) * 24, 8), 24), :]
            tmp[c, pl.ds(0, 24, stride=2), :] = e
            tmp[c, pl.ds(1, 24, stride=2), :] = e
            e = tmp[c]
            vb2[c, 2 * i] = vb2[c, 2 * i] + e
            vb2[c, 2 * i + 1] = vb2[c, 2 * i + 1] + e
        return carry

    lax.fori_loop(0, 4, rise2, 0)
    ends2(vb2)
    sweep(va2, vb2, b2, w2, dinv2, 0, 8, NX2, 4)
    ends2(va2)
    sweep(vb2, va2, b2, w2, dinv2, 0, 8, NX2, 4)

    none = jnp.zeros((24, 128), F32)
    for c in range(3):
        for x in (0, 1, 18, 19):
            e2[c, x] = none
        for x in range(8):
            value = jnp.concatenate([vb2[c, x, 0:16], vb2[c, x, 40:48]], axis=0)
            e2[c, 2 + x] = value
            e2[c, 10 + x] = pltpu.roll(value, 64, 1)
    start = 2 * flags[6]
    for c in range(3):
        for k in range(6):
            pairs[pl.ds((c * 6 + k) * 24, 24), :] = e2[c, start + k]
    spread[pl.ds(0, 432), :] = dot(pairs[pl.ds(0, 432), :], repeat_matrix(repeat1))

    def rise1(k, carry):
        x = lax.rem(2 * k - 4 + NX1, NX1)
        for c in range(3):
            e = spread[pl.ds(pl.multiple_of((c * 6 + k) * 24, 8), 24), :]
            tmp[c, pl.ds(0, 24, stride=2), :] = e
            tmp[c, pl.ds(1, 24, stride=2), :] = e
            e = tmp[c]
            va1[c, x] = v1[c, x] + e
            va1[c, x + 1] = v1[c, x + 1] + e
        return carry

    lax.fori_loop(0, 6, rise1, 0)
    w1 = (wx1, wy1, wz1)
    sweep(vb1, va1, b1, w1, dinv1, -3, 7, NX1)
    sweep(va1, vb1, b1, w1, dinv1, -2, 6, NX1)

    for c in range(3):
        for i in range(-2, 6):
            at = (c * 8 + i + 2) * 24
            x = i % NX1
            pairs[pl.ds(at, 16), :] = va1[c, x, 0:16]
            pairs[pl.ds(at + 16, 8), :] = jnp.where(sub < 4, va1[c, x, 16:24], va1[c, x, 40:48])
    wide[...] = dot(pairs[pl.ds(0, 576), :], repeat_matrix(repeat0, 256))

    def risen(c, i, half):
        here = tmp.at[2 * c + half]
        e = wide[pl.ds(pl.multiple_of((c * 8 + i) * 24, 8), 24), 128 * half:128 * half + 128]
        here[pl.ds(0, 24, stride=2), :] = e
        here[pl.ds(1, 24, stride=2), :] = e
        return here[...]

    def rise0(i, carry):
        for c in range(3):
            for half in range(2):
                e = risen(c, i + 2, half)
                lanes = slice(128 * half, 128 * half + 128)
                va0[c, 2 * i, :, lanes] = v0[c, 2 * i, :, lanes] + e
                va0[c, 2 * i + 1, :, lanes] = v0[c, 2 * i + 1, :, lanes] + e
        return carry

    lax.fori_loop(0, 4, rise0, 0)
    lane = iota((40, 128), 1)
    for high, late in ((True, late_high), (False, late_low)):
        there = flag(flags, 1 if high else 0)
        for p, (c, away) in enumerate(LATE):
            x = 7 + away if high else NX0 - away
            for half in range(2):
                if half == 0:
                    value = late[p]
                else:
                    value = turn(late[7], -8 * p - 4, 1)
                    value = jnp.where((lane < 4) | (lane >= 124), value, 0.0)
                value = jnp.concatenate([value, value[32:40]], axis=0) * there
                e = risen(c, (5 + (away + 1) // 2) if high else 2 - (away + 1) // 2, half)
                va0[c, x, :, 128 * half:128 * half + 128] = value + e
    w0 = (wx0, wy0, wz0)
    sweep(vb0, va0, b0, w0, dinv0, -2, 10, NX0)
    sweep(va0, vb0, b0, w0, dinv0, -1, 9, NX0)

    def advect(x, carry):
        xm, xp = lax.rem(x + NX0 - 1, NX0), x + 1
        d = den[x]
        change = jnp.zeros_like(d)
        spreading = -6.0 * d
        for axis in range(3):
            u = va0[axis, x]
            if axis == 0:
                u_up, u_lo, d_up, d_lo = va0[0, xp], va0[0, xm], den[xp], den[xm]
            else:
                u_up, u_lo = back(u, axis - 1), forth(u, axis - 1)
                d_up, d_lo = back(d, axis - 1), forth(d, axis - 1)
            hi, lo = 0.5 * (u + u_up), 0.5 * (u_lo + u)
            change = change + (jnp.maximum(hi, 0.0) * d + jnp.minimum(hi, 0.0) * d_up)
            change = change - (jnp.maximum(lo, 0.0) * d_lo + jnp.minimum(lo, 0.0) * d)
            spreading = spreading + (d_up + d_lo)
            velocity[axis, x] = u[0:32, 0:128]
        out = d - STEP_TIME * change + STEP_TIME * DIFFUSION * spreading
        new_density[x] = out[0:32, 0:128]
        return carry

    lax.fori_loop(0, 8, advect, 0)


def exchange(up, down, axis, away=1):
    n = lax.axis_size(axis)
    low = lax.ppermute(up, axis, [(i, (i + away) % n) for i in range(n)])
    high = lax.ppermute(down, axis, [(i, (i - away) % n) for i in range(n)])
    return low, high


def per_device(force, grain, density):
    gx, gy, gz = (lax.axis_index(a) for a in ("gx", "gy", "gz"))
    last = [lax.axis_size(a) - 1 for a in ("gx", "gy", "gz")]
    flags = jnp.stack(
        [gx > 0, gx < last[0], gy > 0, gy < last[1], gz > 0, gz < last[2], gx, gx > 1, gx < last[0] - 1]
    ).astype(jnp.int32)

    eta, force, density, up, down = call(
        prepare, [(8, 32, 128), (3, 8, 32, 128), (8, 32, 128), (11, 32, 128), (11, 32, 128)], start=True
    )(flags, force, grain, density)
    x0 = exchange(up, down, "gx")
    up, down = call(pack_y0, [(37, 8, 128)] * 2)(flags, force, eta, density, *x0)
    y0 = exchange(up, down, "gy")
    rows, up, down = call(pack_z0, [(5, NX0, 48, 128)] + [(3, 48, 128)] * 2)(flags, force, eta, density, *x0, *y0)
    z0 = exchange(up, down, "gz")
    vec, one = (3, NX0, NY0, NZ0), (NX0, NY0, NZ0)
    b0, v0, dinv0, wx0, wy0, wz0, den, own1, up, down, far_up, far_down, late_up, late_down = call(
        fine,
        [vec, vec, one, one, one, one, one, (5, 4, 16, 128)]
        + [(11, 16, 128)] * 2 + [(16, 128)] * 2 + [(8, 40, 128)] * 2,
        [one, one, one, vec, (384, 128), (5, 48, 128)],
    )(flags, rows, *z0)
    x1 = exchange(up, down, "gx") + exchange(far_up, far_down, "gx", 2)
    late = exchange(late_up, late_down, "gx")
    up, down = call(pack_y1, [(51, 8, 128)] * 2)(flags, own1, *x1)
    y1 = exchange(up, down, "gy")
    y1, late = lax.optimization_barrier((y1, late))
    rows, up, down = call(pack_z1, [(68, 48, 128)] + [(17, 40, 128)] * 2)(flags, own1, *x1, *y1)
    z1 = exchange(up, down, "gz")
    vec1, one1 = (3, NX1, NY1, 128), (NX1, NY1, 128)
    b1, v1, dinv1, wx1, wy1, wz1, own2, up, down = call(
        coarse,
        [vec1, vec1, one1, one1, one1, one1, (5, 24, 128), (5, 16, 128), (5, 16, 128)],
        [one1, one1, one1, vec1, (240, 128), (5, 48, 128)],
    )(flags, rows, *z1)
    y2 = exchange(up, down, "gy")
    (chunk,) = call(pack_x2, [(8, 168, 128)])(flags, own2, *y2)
    got = lax.all_to_all(chunk, "gx", 0, 0, tiled=True)
    vec2, one2 = (3, NX2, NY2, 128), (NX2, NY2, 128)
    vec3, one3 = (3, NX3, NY3, 128), (NX3, NY3, 128)
    velocity, new_density = call(
        finish,
        [(3, 8, 32, 128), (8, 32, 128)],
        [vec2, one2, one2, one2, one2, one2, one2, one2, vec2, vec2]
        + [vec3, one3, one3, one3, one3, one3, one3, one3, vec3, vec3]
        + [(576, 128), (576, 128), (6, 48, 128), (3, 20, 24, 128), vec1, vec1, vec, vec, (576, 256)],
        limit=32,
        final=True,
    )(flags, got, *late, b1, v1, dinv1, wx1, wy1, wz1, b0, v0, dinv0, wx0, wy0, wz0, den)
    return velocity, new_density


def solution(mesh):
    return jax.shard_map(
        per_device,
        mesh=mesh,
        in_specs=(P(None, "gx", "gy", "gz"), P("gx", "gy", "gz"), P("gx", "gy", "gz")),
        out_specs=(P(None, "gx", "gy", "gz"), P("gx", "gy", "gz")),
        check_vma=False,
    )
```

```python
import jax
import jax.numpy as jnp
from jax import lax
from jax.experimental import pallas as pl
from jax.experimental.pallas import tpu as pltpu
from jax.sharding import PartitionSpec as P

OMEGA = 0.8
STEP_TIME = 0.1
DIFFUSION = 0.05
grain_table = [0.5 * 8.0 ** (entry / 15.0) for entry in range(16)]
F32 = jnp.float32
MIB = 1024 * 1024

W0 = (2, 2, 2, 3, 2)
OFF0 = (0, 2, 4, 6, 9)
Z0 = (4, 4, 4, 5, 4)
ZOFF0 = (0, 4, 8, 12, 17)
NX0, NY0, NZ0 = 14, 48, 256
LATE = ((0, 3), (0, 2), (0, 1), (1, 2), (1, 1), (2, 2), (2, 1))
W1 = (4, 4, 4, 5, 5)
OFF1 = (0, 4, 8, 12, 17)
H1 = (5, 4, 4, 6, 5)
NX1, NY1 = 16, 48
NEAR1 = (2, 2, 2, 3, 2)
PIECES1 = [(f, x) for f in range(5) for x in range(-NEAR1[f], 4 + NEAR1[f])]
WIDE1 = len(PIECES1) // 2
PIECES1 += [(f, x) for f in range(5) for x in range(-H1[f], 4 + H1[f]) if (f, x) not in PIECES1]
UNITS1 = len(PIECES1) // 2
QUADS1 = (WIDE1 + 1) // 2
OCTS1 = (UNITS1 - WIDE1 + 7) // 8
NX2, NY2 = 10, 48
NX3, NY3 = 6, 24


def iota(shape, dim):
    return lax.broadcasted_iota(jnp.int32, shape, dim)


def back(value, axis):
    return pltpu.roll(value, value.shape[axis] - 1, axis)


def forth(value, axis):
    return pltpu.roll(value, 1, axis)


def turn(value, shift, axis):
    shift = shift % value.shape[axis]
    return value if shift == 0 else pltpu.roll(value, shift, axis)


def call(body, outs, scratch=(), limit=12, start=False, final=False):
    def run(flags, *operands):
        if not final:
            shapes = [pltpu.VMEM(s, F32) for s in outs]
        else:
            shapes = [jax.ShapeDtypeStruct(s, F32) for s in outs]
        return pl.pallas_call(
            body,
            out_shape=shapes,
            in_specs=[pl.BlockSpec(memory_space=pltpu.SMEM)]
            + [pl.BlockSpec(memory_space=pltpu.VMEM)] * len(operands),
            out_specs=[pl.BlockSpec(memory_space=pltpu.VMEM)] * len(outs),
            scratch_shapes=[pltpu.VMEM(s, F32) for s in scratch],
            compiler_params=pltpu.CompilerParams(vmem_limit_bytes=limit * MIB),
        )(flags, *[pltpu.with_memory_space_constraint(o, pltpu.HBM if start else pltpu.VMEM) for o in operands])

    return run


def flag(flags, index):
    return flags[index].astype(F32)


def weighted(v, w, c, x, xp, xm):
    wx, wy, wz = w
    here = v[c, x]
    total = wx[x] * v[c, xp] + wx[xm] * v[c, xm]
    a = wy[x]
    total = total + a * back(here, 0) + forth(a * here, 0)
    a = wz[x]
    total = total + a * back(here, 1) + forth(a * here, 1)
    return here, total


def planes(lo, hi, n, body, unroll=2):
    assert (hi - lo) % unroll == 0

    def step(k, carry):
        for j in range(unroll):
            x = lax.rem(unroll * k + (lo + n + j), n)
            body(x, lax.rem(x + 1, n), lax.rem(x + n - 1, n))
        return carry

    lax.fori_loop(0, (hi - lo) // unroll, step, 0)


def sweep(dst, src, b, w, dinv, lo, hi, n, unroll=2):
    def body(x, xp, xm):
        scale = dinv[x]
        for c in range(3):
            here, total = weighted(src, w, c, x, xp, xm)
            dst[c, x] = 0.2 * here + scale * (b[c, x] + total)

    planes(lo, hi, n, body, unroll)


def weights(eta, w, factor, lo, hi, n, unroll=2):
    wx, wy, wz = w
    half = 0.5 * factor

    def body(x, xp, xm):
        here = eta[x]
        wx[x] = half * (here + eta[xp])
        wy[x] = half * (here + back(here, 0))
        wz[x] = half * (here + back(here, 1))

    planes(lo, hi, n, body, unroll)


def diagonals(kap, w, dg, dinv, lo, hi, n):
    wx, wy, wz = w

    def body(x, xp, xm):
        k, a, g = kap[x], wy[x], wz[x]
        d = k + (wx[x] + wx[xm]) + (a + forth(a, 0)) + (g + forth(g, 1))
        inside = k > 0.0
        dg[x] = d
        dinv[x] = jnp.where(inside, OMEGA / jnp.where(inside, d, 1.0), 0.0)

    planes(lo, hi, n, body)


def first(v, b, dinv, lo, hi, n):
    def body(x, xp, xm):
        for c in range(3):
            v[c, x] = dinv[x] * b[c, x]

    planes(lo, hi, n, body)


def rest(v, b, w, dg, c, x, xp, xm):
    here, total = weighted(v, w, c, x, xp, xm)
    return b[c, x] - dg[x] * here + total


def mean_matrix(source):
    k, j = iota((128, 128), 0), iota((128, 128), 1)
    return jnp.where((k >> 1) == source(j), 0.125, 0.0).astype(F32)


def repeat_matrix(source, out=128):
    k, j = iota((128, out), 0), iota((128, out), 1)
    return jnp.where(k == source(j), 1.0, 0.0).astype(F32)


def mean1(j):
    return j & 63


def mean2(j):
    return (j + 48) & 63


def mean3(j):
    return jnp.where((j & 63) < 32, ((j >> 6) << 5) + (j & 63), -1)


def repeat2(j):
    return (j & 64) + ((j & 63) >> 1)


def repeat1(j):
    return ((j >> 1) + 16) & 63


def repeat0(j):
    return j >> 1


def dot(a, b):
    b = b.astype(jnp.bfloat16)
    high = a.astype(jnp.bfloat16)
    rest_of = a - high.astype(F32)
    middle = rest_of.astype(jnp.bfloat16)
    low = (rest_of - middle.astype(F32)).astype(jnp.bfloat16)
    product = lambda piece: jnp.dot(piece, b, preferred_element_type=F32)
    return product(high) + (product(middle) + product(low))


class Joined:
    def __init__(self, left, right):
        self.parts = (left, right)

    def __getitem__(self, index):
        return jnp.concatenate([part[index] for part in self.parts], axis=1)


def row_pairs(tmp, value):
    rows = value.shape[0]
    tmp[pl.ds(0, rows), :] = value
    return tmp[pl.ds(0, rows // 2, stride=2), :] + tmp[pl.ds(1, rows // 2, stride=2), :]


def prepare(flags, force, grain, dens, eta, force_kept, dens_kept, up, down):
    for x in range(8):
        ids = grain[x]
        looked = jnp.full(ids.shape, grain_table[0], F32)
        for entry in range(1, 16):
            looked = jnp.where(ids == entry, grain_table[entry], looked)
        d = dens[x]
        eta[x] = looked * d * d * d
        dens_kept[x] = d
        for c in range(3):
            force_kept[c, x] = force[c, x]
    for f in range(5):
        for k in range(W0[f]):
            for out, x in ((up, 8 - W0[f] + k), (down, k)):
                out[OFF0[f] + k] = force[f, x] if f < 3 else (eta if f == 3 else dens)[x]


def plane0(flags, own, f, x, rows):
    force, eta, dens, low, high = own
    if 0 <= x < 8:
        return force[f, x, rows] if f < 3 else (eta if f == 3 else dens)[x, rows]
    away = x - 8 if x >= 8 else -x - 1
    if away >= W0[f]:
        return jnp.zeros((rows.stop - rows.start, 128), F32)
    if x >= 8:
        return high[OFF0[f] + away, rows] * flag(flags, 1)
    return low[OFF0[f] + W0[f] - 1 - away, rows] * flag(flags, 0)


def rel0(x):
    return x if x < 11 else x - NX0


YF = (0, 1, 2, 4, 3)


def pack_y0(flags, force, eta, dens, low, high, up, down):
    own = (force, eta, dens, low, high)
    sub = iota((8, 128), 0)
    for i, f in enumerate(YF):
        for q in range(7):
            a, b = rel0(2 * q), rel0(2 * q + 1)
            top, bottom = slice(24, 32), slice(0, 8)
            up[7 * i + q] = jnp.where(
                sub < 4, turn(plane0(flags, own, f, a, top), 4, 0), plane0(flags, own, f, b, top)
            )
            down[7 * i + q] = jnp.where(
                sub < 4, plane0(flags, own, f, a, bottom), turn(plane0(flags, own, f, b, bottom), 4, 0)
            )
    for t in range(2):
        hi, lo = jnp.zeros((8, 128), F32), jnp.zeros((8, 128), F32)
        for s in range(8):
            if 8 * t + s < NX0:
                x = rel0(8 * t + s)
                hi = jnp.where(sub == s, turn(plane0(flags, own, 3, x, slice(24, 32)), s - 3, 0), hi)
                lo = jnp.where(sub == s, turn(plane0(flags, own, 3, x, slice(0, 8)), s - 4, 0), lo)
        up[35 + t], down[35 + t] = hi, lo


def rows0(flags, own, lowy, highy, f, x):
    sub = iota((8, 128), 0)
    i = YF.index(f)
    high, low = highy[7 * i + x // 2], lowy[7 * i + x // 2]
    if x % 2:
        high = turn(high, 4, 0)
    else:
        low = turn(low, 4, 0)
    if f == 3:
        high = jnp.where(sub == 4, turn(highy[35 + x // 8], 4 - x % 8, 0), high)
        low = jnp.where(sub == 3, turn(lowy[35 + x // 8], 3 - x % 8, 0), low)
    middle = plane0(flags, own, f, rel0(x), slice(0, 32))
    return jnp.concatenate([middle, high * flag(flags, 3), low * flag(flags, 2)], axis=0)


def pack_z0(flags, force, eta, dens, lowx, highx, lowy, highy, up, down):
    own = (force, eta, dens, lowx, highx)
    lane = iota((NY0, 128), 1)
    for g in range(3):
        hi, lo = jnp.zeros((NY0, 128), F32), jnp.zeros((NY0, 128), F32)
        for s in range(min(6, NX0 - 6 * g)):
            for f in range(5):
                at, w = 21 * s + ZOFF0[f], Z0[f]
                value = rows0(flags, own, lowy, highy, f, 6 * g + s)
                there = (lane >= at) & (lane < at + w)
                hi = jnp.where(there, turn(value, at - (128 - w), 1), hi)
                lo = jnp.where(there, turn(value, at, 1), lo)
        up[g], down[g] = hi, lo


def assemble0(flags, force, eta, dens, lowx, highx, lowy, highy, b, eta0, den):
    own = (force, eta, dens, lowx, highx)
    for x in range(NX0):
        for f in range(5):
            value = rows0(flags, own, lowy, highy, f, x)
            if f < 3:
                b[f, x] = value
            else:
                (eta0 if f == 3 else den)[x] = value


def fine(flags, b_own, eta_own, den_own, lowz, highz,
         b_far, den_far, v, dinv, wx, wy, wz, own1, up, down, far_up, far_down, late_up, late_down,
         eta_far, kap, dg, v0, pairs, tmp):
    lane = iota((NY0, 128), 1)
    fhi, flo = flag(flags, 5), flag(flags, 4)
    for x in range(NX0):
        for f in range(5):
            at, w = 21 * (x % 6) + ZOFF0[f], Z0[f]
            high = turn(highz[x // 6], -at, 1) * fhi
            low = turn(lowz[x // 6], 128 - w - at, 1) * flo
            beyond = jnp.where(lane < w, high, jnp.where(lane >= 128 - w, low, 0.0))
            if f < 3:
                b_far[f, x] = beyond
            elif f == 3:
                eta_far[x] = beyond
            else:
                den_far[x] = beyond
                for half, value in ((slice(0, 128), den_own[x]), (slice(128, 256), beyond)):
                    kap[x, :, half] = jnp.where(value > 0.0, 0.02 + 0.08 * value, 0.0)
    b, eta0 = Joined(b_own, b_far), Joined(eta_own, eta_far)
    w = (wx, wy, wz)
    weights(eta0, w, 1.0, -3, 11, NX0)
    diagonals(kap, w, dg, dinv, -2, 10, NX0)
    first(v0, b, dinv, -2, 10, NX0)
    sweep(v, v0, b, w, dinv, -1, 9, NX0)

    def blocks(i, carry):
        x0 = 2 * i
        xm, xp, xq = lax.rem(x0 + NX0 - 1, NX0), x0 + 1, x0 + 2
        for c in range(3):
            r = rest(v, b, w, dg, c, x0, xp, xm) + rest(v, b, w, dg, c, xp, xq, x0)
            at = pl.multiple_of((c * 4 + i) * 16, 16)
            pairs[pl.ds(at, 16), :] = row_pairs(tmp.at[c], r[0:32, 0:128])
        return carry

    lax.fori_loop(0, 4, blocks, 0)
    for i in range(-1, 5):
        x = (2 * i) % NX0
        r = eta_own[x, 0:32] + eta_own[x + 1, 0:32]
        pairs[pl.ds((12 + i + 1) * 16, 16), :] = row_pairs(tmp.at[3], r)
        r = kap[x, 0:32, 0:128] + kap[x + 1, 0:32, 0:128]
        pairs[pl.ds((18 + i + 1) * 16, 16), :] = row_pairs(tmp.at[4], r)
    pairs[...] = dot(pairs[...], mean_matrix(mean1))

    def piece(f, i):
        at = f * 4 + i if f < 3 else (13 + i if f == 3 else 19 + i)
        return pairs[pl.ds(at * 16, 16), :]

    half = iota((16, 128), 1) < 64
    ups = [(f, i) for f in range(5) for i in range(4 - W1[f], 4)]
    downs = [(f, i) for f in range(5) for i in range(0, W1[f])]
    for k in range(11):
        up[k] = jnp.where(half, piece(*ups[2 * k]), piece(*ups[2 * k + 1]))
        down[k] = jnp.where(half, piece(*downs[2 * k]), piece(*downs[2 * k + 1]))
    far_up[...] = jnp.where(half, piece(0, 3), piece(3, 2))
    far_down[...] = jnp.where(half, piece(0, 0), piece(3, 1))
    for f in range(5):
        for i in range(4):
            own1[f, i] = piece(f, i)

    sub, slot = iota((8, 128), 0), iota((40, 128), 1) >> 3
    for out, top in ((late_up, True), (late_down, False)):
        edge = jnp.zeros((40, 128), F32)
        for p, (c, away) in enumerate(LATE):
            x = 8 - away if top else away - 1
            for half in range(2):
                value = v[c, x, :, 128 * half:128 * half + 128]
                mix = jnp.where(sub < 4, value[32:40], value[40:48])
                value = jnp.concatenate([value[0:32], mix], axis=0)
                if half == 0:
                    out[p] = value
                else:
                    edge = jnp.where(slot == p, turn(value, 8 * p + 4, 1), edge)
        out[7] = edge


def plane1(flags, own1, lowx, highx, far_low, far_high, f, x, half):
    if 0 <= x < 4:
        return own1[f, x]
    away = x - 4 if x >= 4 else -x - 1
    if away >= W1[f]:
        at, source = int(f == 3), (far_high if x >= 4 else far_low)[...]
        there = flag(flags, 8 if x >= 4 else 7)
    elif x >= 4:
        at = OFF1[f] + away
        source, there = highx[at // 2], flag(flags, 1)
    else:
        at = OFF1[f] + W1[f] - 1 - away
        source, there = lowx[at // 2], flag(flags, 0)
    return turn(source, 64 * ((at + half) % 2), 1) * there


def pack_y1(flags, own1, lowx, highx, far_low, far_high, middle, up, down):
    sub = iota((8, 128), 0)
    left = iota((16, 128), 1) < 64
    sent = (flags, own1, lowx, highx, far_low, far_high)
    hi = lo = None
    for u in range(UNITS1):
        value = jnp.where(left, plane1(*sent, *PIECES1[2 * u], 0), plane1(*sent, *PIECES1[2 * u + 1], 1))
        middle[u] = value
        up[u], down[u] = value[8:16], value[0:8]
        if u < WIDE1:
            if u % 2 == 0:
                hi, lo = turn(value[0:8], 4, 0), value[8:16]
            else:
                hi, lo = jnp.where(sub < 4, hi, value[0:8]), jnp.where(sub < 4, lo, turn(value[8:16], 4, 0))
            up[UNITS1 + u // 2], down[UNITS1 + u // 2] = hi, lo


def unit1(flags, middle, lowy, highy, u):
    sub = iota((8, 128), 0)
    fhi, flo = flag(flags, 3), flag(flags, 2)
    if u < WIDE1:
        high, low = highy[UNITS1 + u // 2], lowy[UNITS1 + u // 2]
        high, low = (turn(high, 4, 0), low) if u % 2 else (high, turn(low, 4, 0))
        mix = jnp.where(sub < 4, high * fhi, low * flo)
    else:
        mix = jnp.zeros((8, 128), F32)
    value = jnp.concatenate([middle[u], highy[u] * fhi, mix, lowy[u] * flo], axis=0)
    return value


def assemble1(flags, middle, lowy, highy, rows):
    for u in range(UNITS1):
        value = all_rows1(unit1(flags, middle, lowy, highy, u))
        for h in range(2):
            f, x = PIECES1[2 * u + h]
            rows[f, x % NX1] = turn(value, 64 * h, 1)


def pack_z1(flags, middle, lowy, highy, up, down):
    lane = iota((40, 128), 1)

    def unit(u):
        return unit1(flags, middle, lowy, highy, u)

    odd = ((lane >> 5) & 1) == 1
    for g in range(QUADS1):
        a = unit(2 * g)
        b = unit(2 * g + 1) if 2 * g + 1 < WIDE1 else a
        up[pl.ds(40 * g, 40), :] = jnp.where(odd, a, turn(b, 96, 1))
        down[pl.ds(40 * g, 40), :] = jnp.where(odd, turn(b, 32, 1), a)
    slot = (iota((32, 128), 1) >> 3) & 7
    for q in range(OCTS1):
        hi = lo = jnp.zeros((32, 128), F32)
        for j in range(8):
            u = WIDE1 + 8 * q + j
            if u < UNITS1:
                value = unit(u)
                value = jnp.concatenate([value[0:24], value[32:40]], axis=0)
                hi = jnp.where(slot == j, turn(value, 8 * j - 56, 1), hi)
                lo = jnp.where(slot == j, turn(value, 8 * j, 1), lo)
        at = 40 * QUADS1 + 32 * q
        up[pl.ds(at, 32), :], down[pl.ds(at, 32), :] = hi, lo


def all_rows1(value):
    if value.shape[0] == 40:
        return jnp.concatenate([value[0:32], value[24:40]], axis=0)
    return jnp.concatenate([value[0:24], value[16:32], value[24:32]], axis=0)


def coarse(flags, rows, lowz, highz,
           b, v, dinv, wx, wy, wz, own2, up, down,
           eta, kap, dg, v0, pairs, tmp):
    lane = iota((NY1, 128), 1)
    none = jnp.zeros((NY1, 128), F32)
    for x in (-6, 9):
        kap[x % NX1] = none
    for x in (-5, 8):
        for c in (1, 2):
            b[c, x % NX1] = none
    fhi, flo = flag(flags, 5), flag(flags, 4)
    for p, (f, x) in enumerate(PIECES1):
        u, h = p // 2, 64 * (p % 2)
        middle = rows[f, x % NX1]
        if u < WIDE1:
            place = pl.ds(40 * (u // 2), 40)
            to_high, to_low = (32 - h, 96 - h) if u % 2 else (64 - h, 64 - h)
        else:
            q, j = (u - WIDE1) // 8, (u - WIDE1) % 8
            place = pl.ds(40 * QUADS1 + 32 * q, 32)
            to_high, to_low = 64 - 8 * j - h, 120 - 8 * j - h
        high = all_rows1(turn(highz[place, :], to_high, 1) * fhi)
        low = all_rows1(turn(lowz[place, :], to_low, 1) * flo)
        value = jnp.where(lane < 64, middle, jnp.where(lane < 96, high, low))
        if f < 3:
            b[f, x % NX1] = value
        else:
            (eta if f == 3 else kap)[x % NX1] = value
    w = (wx, wy, wz)
    weights(eta, w, 0.25, -6, 10, NX1)
    diagonals(kap, w, dg, dinv, -5, 9, NX1)
    first(v0, b, dinv, -5, 9, NX1)
    sweep(v, v0, b, w, dinv, -4, 8, NX1)

    def blocks(i, carry):
        x0 = 2 * i
        for c in range(3):
            r = rest(v, b, w, dg, c, x0, x0 + 1, lax.rem(x0 + NX1 - 1, NX1))
            r = r + rest(v, b, w, dg, c, x0 + 1, x0 + 2, x0)
            at = pl.multiple_of((c * 2 + i) * 24, 8)
            pairs[pl.ds(at, 24), :] = row_pairs(tmp.at[c], r)
        at = pl.multiple_of((6 + i) * 24, 8)
        pairs[pl.ds(at, 24), :] = row_pairs(tmp.at[3], eta[x0] + eta[x0 + 1])
        at = pl.multiple_of((8 + i) * 24, 8)
        pairs[pl.ds(at, 24), :] = row_pairs(tmp.at[4], kap[x0] + kap[x0 + 1])
        return carry

    lax.fori_loop(0, 2, blocks, 0)
    pairs[...] = dot(pairs[...], mean_matrix(mean2))
    left = iota((24, 128), 1) < 64
    for f in range(5):
        value = jnp.where(left, pairs[pl.ds(48 * f, 24), :], pairs[pl.ds(48 * f + 24, 24), :])
        own2[f] = value
        up[f, 0:8], up[f, 8:16] = value[16:24], value[0:8]
        down[f] = value[0:16]


def pack_x2(flags, own2, lowy, highy, out):
    sub = iota((8, 128), 0)
    for f in range(5):
        near, far = highy[f, 0:8] * flag(flags, 3), highy[f, 8:16] * flag(flags, 3)
        far_low, near_low = lowy[f, 0:8] * flag(flags, 2), lowy[f, 8:16] * flag(flags, 2)
        value = jnp.concatenate([own2[f, 0:8], near, jnp.where(sub < 4, far, far_low), near_low], axis=0)
        for d in range(8):
            out[d, 32 * f:32 * f + 32] = value
        if f == 3:
            for d in range(8):
                out[d, 160:168] = jnp.where(sub == 4, far, far_low)


def finish(flags, got, late_low, late_high, b1, v1, dinv1, wx1, wy1, wz1, b_own, b_far, den_own, den_far, v0, dinv0, wx0, wy0, wz0,
           velocity, new_density,
           b2, eta2, kap2, dg2, dinv2, wx2, wy2, wz2, va2, vb2,
           b3, eta3, kap3, dg3, dinv3, wx3, wy3, wz3, va3, vb3,
           pairs, spread, tmp, e2, va1, vb1, va0, vb0, wide):
    sub = iota((8, 128), 0)
    left2, left3 = iota((NY2, 128), 1) < 64, iota((NY3, 128), 1) < 64
    for f in range(5):
        two = []
        for d in range(8):
            own, near = got[d, 32 * f:32 * f + 8], got[d, 32 * f + 8:32 * f + 16]
            mix, low = got[d, 32 * f + 16:32 * f + 24], got[d, 32 * f + 24:32 * f + 32]
            far, far_low = mix, mix
            if f == 3:
                extra = got[d, 160:168]
                far, far_low = jnp.where(sub == 4, extra, mix), jnp.where(sub == 3, extra, mix)
            two.append(jnp.concatenate([own, near, far, mix, far_low, low], axis=0))
        for d in range(4):
            even = jnp.where(left2, two[d], pltpu.roll(two[d + 4], 64, 1))
            odd = jnp.where(left2, pltpu.roll(two[d], 64, 1), two[d + 4])
            if f < 3:
                b2[f, 2 * d], b2[f, 2 * d + 1] = even, odd
            else:
                out = eta2 if f == 3 else kap2
                out[2 * d], out[2 * d + 1] = even, odd

    def ends(ref, n, left, lead=()):
        first_plane, last_plane = ref[lead + (0,)], ref[lead + (n - 1,)]
        ref[lead + (n,)] = jnp.where(left, pltpu.roll(first_plane, 64, 1), 0.0)
        ref[lead + (n + 1,)] = jnp.where(left, 0.0, pltpu.roll(last_plane, 64, 1))

    def ends2(ref):
        for c in range(3):
            ends(ref, 8, left2, (c,))

    def ends3(ref):
        for c in range(3):
            ends(ref, 4, left3, (c,))

    w2 = (wx2, wy2, wz2)
    ends(eta2, 8, left2)
    weights(eta2, w2, 0.0625, -1, 8, NX2, 3)
    diagonals(kap2, w2, dg2, dinv2, 0, 8, NX2)
    first(va2, b2, dinv2, 0, 8, NX2)
    ends2(va2)
    sweep(vb2, va2, b2, w2, dinv2, 0, 8, NX2, 4)
    ends2(vb2)

    def blocks(i, carry):
        x0 = 2 * i
        xm, xp, xq = lax.rem(x0 + NX2 - 1, NX2), x0 + 1, x0 + 2
        for c in range(3):
            r = rest(vb2, b2, w2, dg2, c, x0, xp, xm) + rest(vb2, b2, w2, dg2, c, xp, xq, x0)
            pairs[pl.ds(pl.multiple_of((c * 4 + i) * 24, 8), 24), :] = row_pairs(tmp.at[c], r)
        pairs[pl.ds(pl.multiple_of((12 + i) * 24, 8), 24), :] = row_pairs(tmp.at[3], eta2[x0] + eta2[xp])
        pairs[pl.ds(pl.multiple_of((16 + i) * 24, 8), 24), :] = row_pairs(tmp.at[4], kap2[x0] + kap2[xp])
        return carry

    lax.fori_loop(0, 4, blocks, 0)
    pairs[pl.ds(0, 480), :] = dot(pairs[pl.ds(0, 480), :], mean_matrix(mean3))
    for i in range(4):
        for c in range(3):
            b3[c, i] = pairs[pl.ds((c * 4 + i) * 24, 24), :]
        eta3[i] = pairs[pl.ds((12 + i) * 24, 24), :]
        kap3[i] = pairs[pl.ds((16 + i) * 24, 24), :]
    w3 = (wx3, wy3, wz3)
    ends(eta3, 4, left3)
    weights(eta3, w3, 0.015625, -1, 4, NX3, 5)
    diagonals(kap3, w3, dg3, dinv3, 0, 4, NX3)
    first(va3, b3, dinv3, 0, 4, NX3)
    ends3(va3)
    sweep(vb3, va3, b3, w3, dinv3, 0, 4, NX3, 4)
    ends3(vb3)
    sweep(va3, vb3, b3, w3, dinv3, 0, 4, NX3, 4)
    ends3(va3)
    sweep(vb3, va3, b3, w3, dinv3, 0, 4, NX3, 4)

    for c in range(3):
        for i in range(4):
            pairs[pl.ds((c * 4 + i) * 24, 24), :] = vb3[c, i]
    spread[pl.ds(0, 288), :] = dot(pairs[pl.ds(0, 288), :], repeat_matrix(repeat2))

    def rise2(i, carry):
        for c in range(3):
            e = spread[pl.ds(pl.multiple_of((c * 4 + i) * 24, 8), 24), :]
            tmp[c, pl.ds(0, 24, stride=2), :] = e
            tmp[c, pl.ds(1, 24, stride=2), :] = e
            e = tmp[c]
            vb2[c, 2 * i] = vb2[c, 2 * i] + e
            vb2[c, 2 * i + 1] = vb2[c, 2 * i + 1] + e
        return carry

    lax.fori_loop(0, 4, rise2, 0)
    ends2(vb2)
    sweep(va2, vb2, b2, w2, dinv2, 0, 8, NX2, 4)
    ends2(va2)
    sweep(vb2, va2, b2, w2, dinv2, 0, 8, NX2, 4)

    none = jnp.zeros((24, 128), F32)
    for c in range(3):
        for x in (0, 1, 18, 19):
            e2[c, x] = none
        for x in range(8):
            value = jnp.concatenate([vb2[c, x, 0:16], vb2[c, x, 40:48]], axis=0)
            e2[c, 2 + x] = value
            e2[c, 10 + x] = pltpu.roll(value, 64, 1)
    start = 2 * flags[6]
    for c in range(3):
        for k in range(6):
            pairs[pl.ds((c * 6 + k) * 24, 24), :] = e2[c, start + k]
    spread[pl.ds(0, 432), :] = dot(pairs[pl.ds(0, 432), :], repeat_matrix(repeat1))

    def rise1(k, carry):
        x = lax.rem(2 * k - 4 + NX1, NX1)
        for c in range(3):
            e = spread[pl.ds(pl.multiple_of((c * 6 + k) * 24, 8), 24), :]
            tmp[c, pl.ds(0, 24, stride=2), :] = e
            tmp[c, pl.ds(1, 24, stride=2), :] = e
            e = tmp[c]
            va1[c, x] = v1[c, x] + e
            va1[c, x + 1] = v1[c, x + 1] + e
        return carry

    lax.fori_loop(0, 6, rise1, 0)
    w1 = (wx1, wy1, wz1)
    sweep(vb1, va1, b1, w1, dinv1, -3, 7, NX1)
    sweep(va1, vb1, b1, w1, dinv1, -2, 6, NX1)

    for c in range(3):
        for i in range(-2, 6):
            at = (c * 8 + i + 2) * 24
            x = i % NX1
            pairs[pl.ds(at, 16), :] = va1[c, x, 0:16]
            pairs[pl.ds(at + 16, 8), :] = jnp.where(sub < 4, va1[c, x, 16:24], va1[c, x, 40:48])
    wide[...] = dot(pairs[pl.ds(0, 576), :], repeat_matrix(repeat0, 256))

    def risen(c, i, half):
        here = tmp.at[2 * c + half]
        e = wide[pl.ds(pl.multiple_of((c * 8 + i) * 24, 8), 24), 128 * half:128 * half + 128]
        here[pl.ds(0, 24, stride=2), :] = e
        here[pl.ds(1, 24, stride=2), :] = e
        return here[...]

    def rise0(i, carry):
        for c in range(3):
            for half in range(2):
                e = risen(c, i + 2, half)
                lanes = slice(128 * half, 128 * half + 128)
                va0[c, 2 * i, :, lanes] = v0[c, 2 * i, :, lanes] + e
                va0[c, 2 * i + 1, :, lanes] = v0[c, 2 * i + 1, :, lanes] + e
        return carry

    lax.fori_loop(0, 4, rise0, 0)
    lane = iota((40, 128), 1)
    for high, late in ((True, late_high), (False, late_low)):
        there = flag(flags, 1 if high else 0)
        for p, (c, away) in enumerate(LATE):
            x = 7 + away if high else NX0 - away
            for half in range(2):
                if half == 0:
                    value = late[p]
                else:
                    value = turn(late[7], -8 * p - 4, 1)
                    value = jnp.where((lane < 4) | (lane >= 124), value, 0.0)
                value = jnp.concatenate([value, value[32:40]], axis=0) * there
                e = risen(c, (5 + (away + 1) // 2) if high else 2 - (away + 1) // 2, half)
                va0[c, x, :, 128 * half:128 * half + 128] = value + e
    w0 = (wx0, wy0, wz0)
    b0, den = Joined(b_own, b_far), Joined(den_own, den_far)
    sweep(vb0, va0, b0, w0, dinv0, -2, 10, NX0)
    sweep(va0, vb0, b0, w0, dinv0, -1, 9, NX0)

    def advect(x, carry):
        xm, xp = lax.rem(x + NX0 - 1, NX0), x + 1
        d = den[x]
        change = jnp.zeros_like(d)
        spreading = -6.0 * d
        for axis in range(3):
            u = va0[axis, x]
            if axis == 0:
                u_up, u_lo, d_up, d_lo = va0[0, xp], va0[0, xm], den[xp], den[xm]
            else:
                u_up, u_lo = back(u, axis - 1), forth(u, axis - 1)
                d_up, d_lo = back(d, axis - 1), forth(d, axis - 1)
            hi, lo = 0.5 * (u + u_up), 0.5 * (u_lo + u)
            change = change + (jnp.maximum(hi, 0.0) * d + jnp.minimum(hi, 0.0) * d_up)
            change = change - (jnp.maximum(lo, 0.0) * d_lo + jnp.minimum(lo, 0.0) * d)
            spreading = spreading + (d_up + d_lo)
            velocity[axis, x] = u[0:32, 0:128]
        out = d - STEP_TIME * change + STEP_TIME * DIFFUSION * spreading
        new_density[x] = out[0:32, 0:128]
        return carry

    lax.fori_loop(0, 8, advect, 0)


def exchange(up, down, axis, away=1):
    n = lax.axis_size(axis)
    low = lax.ppermute(up, axis, [(i, (i + away) % n) for i in range(n)])
    high = lax.ppermute(down, axis, [(i, (i - away) % n) for i in range(n)])
    return low, high


def per_device(force, grain, density):
    gx, gy, gz = (lax.axis_index(a) for a in ("gx", "gy", "gz"))
    last = [lax.axis_size(a) - 1 for a in ("gx", "gy", "gz")]
    flags = jnp.stack(
        [gx > 0, gx < last[0], gy > 0, gy < last[1], gz > 0, gz < last[2], gx, gx > 1, gx < last[0] - 1]
    ).astype(jnp.int32)

    eta, force, density, up, down = call(
        prepare, [(8, 32, 128), (3, 8, 32, 128), (8, 32, 128), (11, 32, 128), (11, 32, 128)], start=True
    )(flags, force, grain, density)
    x0 = exchange(up, down, "gx")
    up, down = call(pack_y0, [(37, 8, 128)] * 2)(flags, force, eta, density, *x0)
    y0 = exchange(up, down, "gy")
    up, down = call(pack_z0, [(3, 48, 128)] * 2)(flags, force, eta, density, *x0, *y0)
    z0 = exchange(up, down, "gz")
    vec, one = (3, NX0, NY0, NZ0), (NX0, NY0, NZ0)
    vech, oneh = (3, NX0, NY0, 128), (NX0, NY0, 128)
    b_own, eta_own, den_own = call(assemble0, [vech, oneh, oneh])(flags, force, eta, density, *x0, *y0)
    b_far, den_far, v0, dinv0, wx0, wy0, wz0, own1, up, down, far_up, far_down, late_up, late_down = call(
        fine,
        [vech, oneh, vec, one, one, one, one, (5, 4, 16, 128)]
        + [(11, 16, 128)] * 2 + [(16, 128)] * 2 + [(8, 40, 128)] * 2,
        [oneh, one, one, vec, (384, 128), (5, 48, 128)],
    )(flags, b_own, eta_own, den_own, *z0)
    x1 = exchange(up, down, "gx") + exchange(far_up, far_down, "gx", 2)
    late = exchange(late_up, late_down, "gx")
    middle, up, down = call(
        pack_y1, [(UNITS1, 16, 128)] + [(UNITS1 + QUADS1, 8, 128)] * 2
    )(flags, own1, *x1)
    y1 = exchange(up, down, "gy")
    y1, late = lax.optimization_barrier((y1, late))
    up, down = call(pack_z1, [(40 * QUADS1 + 32 * OCTS1, 128)] * 2)(flags, middle, *y1)
    z1 = exchange(up, down, "gz")
    (rows,) = call(assemble1, [(5, NX1, NY1, 128)])(flags, middle, *y1)
    vec1, one1 = (3, NX1, NY1, 128), (NX1, NY1, 128)
    b1, v1, dinv1, wx1, wy1, wz1, own2, up, down = call(
        coarse,
        [vec1, vec1, one1, one1, one1, one1, (5, 24, 128), (5, 16, 128), (5, 16, 128)],
        [one1, one1, one1, vec1, (240, 128), (5, 48, 128)],
    )(flags, rows, *z1)
    y2 = exchange(up, down, "gy")
    (chunk,) = call(pack_x2, [(8, 168, 128)])(flags, own2, *y2)
    got = lax.all_to_all(chunk, "gx", 0, 0, tiled=True)
    vec2, one2 = (3, NX2, NY2, 128), (NX2, NY2, 128)
    vec3, one3 = (3, NX3, NY3, 128), (NX3, NY3, 128)
    velocity, new_density = call(
        finish,
        [(3, 8, 32, 128), (8, 32, 128)],
        [vec2, one2, one2, one2, one2, one2, one2, one2, vec2, vec2]
        + [vec3, one3, one3, one3, one3, one3, one3, one3, vec3, vec3]
        + [(576, 128), (576, 128), (6, 48, 128), (3, 20, 24, 128), vec1, vec1, vec, vec, (576, 256)],
        limit=32,
        final=True,
    )(flags, got, *late, b1, v1, dinv1, wx1, wy1, wz1, b_own, b_far, den_own, den_far, v0, dinv0, wx0, wy0, wz0)
    return velocity, new_density


def solution(mesh):
    return jax.shard_map(
        per_device,
        mesh=mesh,
        in_specs=(P(None, "gx", "gy", "gz"), P("gx", "gy", "gz"), P("gx", "gy", "gz")),
        out_specs=(P(None, "gx", "gy", "gz"), P("gx", "gy", "gz")),
        check_vma=False,
    )
```

```python
import jax
import jax.numpy as jnp
from jax import lax
from jax.experimental import pallas as pl
from jax.experimental.pallas import tpu as pltpu
from jax.sharding import PartitionSpec as P

OMEGA = 0.8
STEP_TIME = 0.1
DIFFUSION = 0.05
grain_table = [0.5 * 8.0 ** (entry / 15.0) for entry in range(16)]
F32 = jnp.float32
MIB = 1024 * 1024

W0 = (2, 2, 2, 3, 2)
OFF0 = (0, 2, 4, 6, 9)
Z0 = (4, 4, 4, 5, 4)
ZOFF0 = (5, 9, 13, 0, 17)
ZSLOT0 = 22
NX0, NY0, NZ0 = 14, 48, 256
LATE = ((0, 3), (0, 2), (0, 1), (1, 2), (1, 1), (2, 2), (2, 1))
W1 = (4, 4, 4, 5, 5)
OFF1 = (0, 4, 8, 12, 17)
H1 = (5, 4, 4, 6, 5)
NX1, NY1 = 16, 48
NEAR1 = (2, 2, 2, 3, 2)
PIECES1 = [(f, x) for f in range(5) for x in range(-NEAR1[f], 4 + NEAR1[f])]
WIDE1 = len(PIECES1) // 2
PIECES1 += [(f, x) for f in range(5) for x in range(-H1[f], 4 + H1[f]) if (f, x) not in PIECES1]
UNITS1 = len(PIECES1) // 2
QUADS1 = (WIDE1 + 1) // 2
OCTS1 = (UNITS1 - WIDE1 + 7) // 8
NX2, NY2 = 10, 48
NX3, NY3 = 6, 24


def iota(shape, dim):
    return lax.broadcasted_iota(jnp.int32, shape, dim)


def back(value, axis):
    return pltpu.roll(value, value.shape[axis] - 1, axis)


def forth(value, axis):
    return pltpu.roll(value, 1, axis)


def turn(value, shift, axis):
    shift = shift % value.shape[axis]
    return value if shift == 0 else pltpu.roll(value, shift, axis)


def call(body, outs, scratch=(), limit=12, start=False, final=False):
    def run(flags, *operands):
        if not final:
            shapes = [pltpu.VMEM(s, F32) for s in outs]
        else:
            shapes = [jax.ShapeDtypeStruct(s, F32) for s in outs]
        return pl.pallas_call(
            body,
            out_shape=shapes,
            in_specs=[pl.BlockSpec(memory_space=pltpu.SMEM)]
            + [pl.BlockSpec(memory_space=pltpu.VMEM)] * len(operands),
            out_specs=[pl.BlockSpec(memory_space=pltpu.VMEM)] * len(outs),
            scratch_shapes=[pltpu.VMEM(s, F32) for s in scratch],
            compiler_params=pltpu.CompilerParams(vmem_limit_bytes=limit * MIB),
        )(flags, *[pltpu.with_memory_space_constraint(o, pltpu.HBM if start else pltpu.VMEM) for o in operands])

    return run


def flag(flags, index):
    return flags[index].astype(F32)


def weighted(v, w, c, x, xp, xm):
    wx, wy, wz = w
    here = v[c, x]
    total = wx[x] * v[c, xp] + wx[xm] * v[c, xm]
    a = wy[x]
    total = total + a * back(here, 0) + forth(a * here, 0)
    a = wz[x]
    total = total + a * back(here, 1) + forth(a * here, 1)
    return here, total


def planes(lo, hi, n, body, unroll=2):
    assert (hi - lo) % unroll == 0

    def step(k, carry):
        for j in range(unroll):
            x = lax.rem(unroll * k + (lo + n + j), n)
            body(x, lax.rem(x + 1, n), lax.rem(x + n - 1, n))
        return carry

    lax.fori_loop(0, (hi - lo) // unroll, step, 0)


def sweep(dst, src, b, w, dinv, lo, hi, n, unroll=2):
    def body(x, xp, xm):
        scale = dinv[x]
        for c in range(3):
            here, total = weighted(src, w, c, x, xp, xm)
            dst[c, x] = 0.2 * here + scale * (b[c, x] + total)

    planes(lo, hi, n, body, unroll)


def sweep_wider(dst, src, b, w, dinv, lo, hi, n):
    sweep(dst, src, b, w, dinv, lo + 1, hi - 1, n)
    for x in (lo % n, (hi - 1) % n):
        here, total = weighted(src, w, 0, x, (x + 1) % n, (x - 1) % n)
        dst[0, x] = 0.2 * here + dinv[x] * (b[0, x] + total)


def weights(eta, w, factor, lo, hi, n, unroll=2):
    wx, wy, wz = w
    half = 0.5 * factor

    def body(x, xp, xm):
        here = eta[x]
        wx[x] = half * (here + eta[xp])
        wy[x] = half * (here + back(here, 0))
        wz[x] = half * (here + back(here, 1))

    planes(lo, hi, n, body, unroll)


def diagonals(kap, w, dg, dinv, v, b, lo, hi, n):
    wx, wy, wz = w

    def body(x, xp, xm):
        k, a, g = kap[x], wy[x], wz[x]
        d = k + (wx[x] + wx[xm]) + (a + forth(a, 0)) + (g + forth(g, 1))
        inside = k > 0.0
        scale = jnp.where(inside, OMEGA / jnp.where(inside, d, 1.0), 0.0)
        dg[x] = d
        dinv[x] = scale
        for c in range(3):
            v[c, x] = scale * b[c, x]

    planes(lo, hi, n, body)


def rest(v, b, w, dg, c, x, xp, xm):
    here, total = weighted(v, w, c, x, xp, xm)
    return b[c, x] - dg[x] * here + total


def mean_matrix(source):
    k, j = iota((128, 128), 0), iota((128, 128), 1)
    return jnp.where((k >> 1) == source(j), 0.125, 0.0).astype(F32)


def repeat_matrix(source, out=128):
    k, j = iota((128, out), 0), iota((128, out), 1)
    return jnp.where(k == source(j), 1.0, 0.0).astype(F32)


def mean1(j):
    return j & 63


def mean2(j):
    return (j + 48) & 63


def mean3(j):
    return jnp.where((j & 63) < 32, ((j >> 6) << 5) + (j & 63), -1)


def repeat2(j):
    return (j & 64) + ((j & 63) >> 1)


def repeat1(j):
    return ((j >> 1) + 16) & 63


def repeat0(j):
    return j >> 1


def dot(a, b):
    b = b.astype(jnp.bfloat16)
    high = a.astype(jnp.bfloat16)
    rest_of = a - high.astype(F32)
    middle = rest_of.astype(jnp.bfloat16)
    low = (rest_of - middle.astype(F32)).astype(jnp.bfloat16)
    product = lambda piece: jnp.dot(piece, b, preferred_element_type=F32)
    return product(high) + (product(middle) + product(low))


class Joined:
    def __init__(self, left, right):
        self.parts = (left, right)

    def __getitem__(self, index):
        return jnp.concatenate([part[index] for part in self.parts], axis=1)


def row_pairs(tmp, value):
    rows = value.shape[0]
    tmp[pl.ds(0, rows), :] = value
    return tmp[pl.ds(0, rows // 2, stride=2), :] + tmp[pl.ds(1, rows // 2, stride=2), :]


def prepare(flags, force, grain, dens, eta, force_kept, dens_kept, up, down):
    for x in range(8):
        ids = grain[x]
        looked = jnp.full(ids.shape, grain_table[0], F32)
        for entry in range(1, 16):
            looked = jnp.where(ids == entry, grain_table[entry], looked)
        d = dens[x]
        eta[x] = looked * d * d * d
        dens_kept[x] = d
        for c in range(3):
            force_kept[c, x] = force[c, x]
    for f in range(5):
        for k in range(W0[f]):
            for out, x in ((up, 8 - W0[f] + k), (down, k)):
                out[OFF0[f] + k] = force[f, x] if f < 3 else (eta if f == 3 else dens)[x]


def plane0(flags, own, f, x, rows):
    force, eta, dens, low, high = own
    if 0 <= x < 8:
        return force[f, x, rows] if f < 3 else (eta if f == 3 else dens)[x, rows]
    away = x - 8 if x >= 8 else -x - 1
    if away >= W0[f]:
        return jnp.zeros((rows.stop - rows.start, 128), F32)
    if x >= 8:
        return high[OFF0[f] + away, rows] * flag(flags, 1)
    return low[OFF0[f] + W0[f] - 1 - away, rows] * flag(flags, 0)


def rel0(x):
    return x if x < 11 else x - NX0


YF = (0, 1, 2, 4, 3)


def pack_y0(flags, force, eta, dens, low, high, up, down):
    own = (force, eta, dens, low, high)
    sub = iota((8, 128), 0)
    for i, f in enumerate(YF):
        for q in range(7):
            a, b = rel0(2 * q), rel0(2 * q + 1)
            top, bottom = slice(24, 32), slice(0, 8)
            up[7 * i + q] = jnp.where(
                sub < 4, turn(plane0(flags, own, f, a, top), 4, 0), plane0(flags, own, f, b, top)
            )
            down[7 * i + q] = jnp.where(
                sub < 4, plane0(flags, own, f, a, bottom), turn(plane0(flags, own, f, b, bottom), 4, 0)
            )
    for t in range(2):
        hi, lo = jnp.zeros((8, 128), F32), jnp.zeros((8, 128), F32)
        for s in range(8):
            if 8 * t + s < NX0:
                x = rel0(8 * t + s)
                hi = jnp.where(sub == s, turn(plane0(flags, own, 3, x, slice(24, 32)), s - 3, 0), hi)
                lo = jnp.where(sub == s, turn(plane0(flags, own, 3, x, slice(0, 8)), s - 4, 0), lo)
        up[35 + t], down[35 + t] = hi, lo


def rows0(flags, own, lowy, highy, f, x):
    sub = iota((8, 128), 0)
    i = YF.index(f)
    high, low = highy[7 * i + x // 2], lowy[7 * i + x // 2]
    if x % 2:
        high = turn(high, 4, 0)
    else:
        low = turn(low, 4, 0)
    if f == 3:
        high = jnp.where(sub == 4, turn(highy[35 + x // 8], 4 - x % 8, 0), high)
        low = jnp.where(sub == 3, turn(lowy[35 + x // 8], 3 - x % 8, 0), low)
    middle = plane0(flags, own, f, rel0(x), slice(0, 32))
    return jnp.concatenate([middle, high * flag(flags, 3), low * flag(flags, 2)], axis=0)


def slot0(f, x):
    return x // 5, ZSLOT0 * (x % 5) + 5 + ZOFF0[f]


def sent0(f, x):
    x = rel0(x)
    return max(x - 8, -x - 1) < W0[f]


def pack_z0(flags, force, eta, dens, lowx, highx, lowy, highy, up, down):
    own = (force, eta, dens, lowx, highx)
    lane, sub = iota((40, 128), 1), iota((8, 128), 0)
    for g in range(3):
        hi = lo = jnp.zeros((40, 128), F32)
        for x in range(5 * g, min(5 * g + 5, NX0)):
            for f in range(5):
                if not sent0(f, x):
                    continue
                at, w = slot0(f, x)[1], Z0[f]
                value = rows0(flags, own, lowy, highy, f, x)
                mix = jnp.where(sub < 4, value[32:40], value[40:48])
                value = turn(jnp.concatenate([value[0:32], mix], axis=0), at, 1)
                hi = jnp.where((lane >= at - w) & (lane < at), value, hi)
                lo = jnp.where((lane >= at) & (lane < at + w), value, lo)
        up[g], down[g] = hi, lo


def assemble0(flags, force, eta, dens, lowx, highx, lowy, highy, b, eta0, den, kap, coeffs, pairs, tmp):
    own = (force, eta, dens, lowx, highx)
    for x in range(NX0):
        for f in range(5):
            value = rows0(flags, own, lowy, highy, f, x)
            if f < 3:
                b[f, x] = value
            else:
                (eta0 if f == 3 else den)[x] = value
                if f == 4:
                    kap[x] = jnp.where(value > 0.0, 0.02 + 0.08 * value, 0.0)
    for i in range(-1, 5):
        x = (2 * i) % NX0
        for k, field in enumerate((eta0, kap)):
            r = field[x, 0:32] + field[x + 1, 0:32]
            pairs[pl.ds((6 * k + i + 1) * 16, 16), :] = row_pairs(tmp.at[k], r)
    coeffs[...] = dot(pairs[...], mean_matrix(mean1))


def fine(flags, b_own, eta_own, kap_own, coeffs, lowz, highz,
         b_far, den_far, v, dinv, wx, wy, wz, own1, up, down, far_up, far_down,
         eta_far, kap_far, dg, v0, pairs, tmp):
    lane = iota((40, 128), 1)
    fhi, flo = flag(flags, 5), flag(flags, 4)
    packets = [(highz[g] * fhi, lowz[g] * flo) for g in range(3)]
    for x in range(NX0):
        for f in range(5):
            if not sent0(f, x):
                continue
            (g, at), w = slot0(f, x), Z0[f]
            both = turn(jnp.where(lane >= at, *packets[g]), -at, 1)
            beyond = jnp.where((lane < w) | (lane >= 128 - w), both, 0.0)
            beyond = jnp.concatenate([beyond, beyond[32:40]], axis=0)
            if f < 3:
                b_far[f, x] = beyond
            elif f == 3:
                eta_far[x] = beyond
            else:
                den_far[x] = beyond
                kap_far[x] = jnp.where(beyond > 0.0, 0.02 + 0.08 * beyond, 0.0)
    b, eta0, kap = Joined(b_own, b_far), Joined(eta_own, eta_far), Joined(kap_own, kap_far)
    w = (wx, wy, wz)
    weights(eta0, w, 1.0, -3, 11, NX0)
    diagonals(kap, w, dg, dinv, v0, b, -2, 10, NX0)
    sweep(v, v0, b, w, dinv, -1, 9, NX0)

    def blocks(i, carry):
        x0 = 2 * i
        xm, xp, xq = lax.rem(x0 + NX0 - 1, NX0), x0 + 1, x0 + 2
        for c in range(3):
            r = rest(v, b, w, dg, c, x0, xp, xm) + rest(v, b, w, dg, c, xp, xq, x0)
            at = pl.multiple_of((c * 4 + i) * 16, 16)
            pairs[pl.ds(at, 16), :] = row_pairs(tmp.at[c], r[0:32, 0:128])
        return carry

    lax.fori_loop(0, 4, blocks, 0)
    pairs[...] = dot(pairs[...], mean_matrix(mean1))

    def piece(f, i):
        if f < 3:
            return pairs[pl.ds((f * 4 + i) * 16, 16), :]
        return coeffs[pl.ds((6 * (f - 3) + i + 1) * 16, 16), :]

    half = iota((16, 128), 1) < 64
    ups = [(f, i) for f in range(5) for i in range(4 - W1[f], 4)]
    downs = [(f, i) for f in range(5) for i in range(0, W1[f])]
    for k in range(11):
        up[k] = jnp.where(half, piece(*ups[2 * k]), piece(*ups[2 * k + 1]))
        down[k] = jnp.where(half, piece(*downs[2 * k]), piece(*downs[2 * k + 1]))
    far_up[...] = jnp.where(half, piece(0, 3), piece(3, 2))
    far_down[...] = jnp.where(half, piece(0, 0), piece(3, 1))
    for f in range(5):
        for i in range(4):
            own1[f, i] = piece(f, i)


def pack_late(flags, v, late_up, late_down):
    sub, slot = iota((8, 128), 0), iota((40, 128), 1) >> 3
    for out, top in ((late_up, True), (late_down, False)):
        edge = jnp.zeros((40, 128), F32)
        for p, (c, away) in enumerate(LATE):
            x = 8 - away if top else away - 1
            for half in range(2):
                value = v[c, x, :, 128 * half:128 * half + 128]
                mix = jnp.where(sub < 4, value[32:40], value[40:48])
                value = jnp.concatenate([value[0:32], mix], axis=0)
                if half == 0:
                    out[p] = value
                else:
                    edge = jnp.where(slot == p, turn(value, 8 * p + 4, 1), edge)
        out[7] = edge


def plane1(flags, own1, lowx, highx, far_low, far_high, f, x, half):
    if 0 <= x < 4:
        return own1[f, x]
    away = x - 4 if x >= 4 else -x - 1
    if away >= W1[f]:
        at, source = int(f == 3), (far_high if x >= 4 else far_low)[...]
        there = flag(flags, 8 if x >= 4 else 7)
    elif x >= 4:
        at = OFF1[f] + away
        source, there = highx[at // 2], flag(flags, 1)
    else:
        at = OFF1[f] + W1[f] - 1 - away
        source, there = lowx[at // 2], flag(flags, 0)
    return turn(source, 64 * ((at + half) % 2), 1) * there


def pack_y1(flags, own1, lowx, highx, far_low, far_high, middle, up, down):
    sub = iota((8, 128), 0)
    left = iota((16, 128), 1) < 64
    sent = (flags, own1, lowx, highx, far_low, far_high)
    hi = lo = None
    for u in range(UNITS1):
        value = jnp.where(left, plane1(*sent, *PIECES1[2 * u], 0), plane1(*sent, *PIECES1[2 * u + 1], 1))
        middle[u] = value
        up[u], down[u] = value[8:16], value[0:8]
        if u < WIDE1:
            if u % 2 == 0:
                hi, lo = turn(value[0:8], 4, 0), value[8:16]
            else:
                hi, lo = jnp.where(sub < 4, hi, value[0:8]), jnp.where(sub < 4, lo, turn(value[8:16], 4, 0))
            up[UNITS1 + u // 2], down[UNITS1 + u // 2] = hi, lo


def unit1(flags, middle, lowy, highy, u):
    sub = iota((8, 128), 0)
    fhi, flo = flag(flags, 3), flag(flags, 2)
    if u < WIDE1:
        high, low = highy[UNITS1 + u // 2], lowy[UNITS1 + u // 2]
        high, low = (turn(high, 4, 0), low) if u % 2 else (high, turn(low, 4, 0))
        mix = jnp.where(sub < 4, high * fhi, low * flo)
    else:
        mix = jnp.zeros((8, 128), F32)
    value = jnp.concatenate([middle[u], highy[u] * fhi, mix, lowy[u] * flo], axis=0)
    return value


def assemble1(flags, middle, lowy, highy, rows):
    for u in range(UNITS1):
        value = all_rows1(unit1(flags, middle, lowy, highy, u))
        for h in range(2):
            f, x = PIECES1[2 * u + h]
            rows[f, x % NX1] = turn(value, 64 * h, 1)


def pack_z1(flags, middle, lowy, highy, up, down):
    lane = iota((40, 128), 1)

    def unit(u):
        return unit1(flags, middle, lowy, highy, u)

    odd = ((lane >> 5) & 1) == 1
    for g in range(QUADS1):
        a = unit(2 * g)
        b = unit(2 * g + 1) if 2 * g + 1 < WIDE1 else a
        b = turn(b, 32, 1)
        up[pl.ds(40 * g, 40), :] = jnp.where(odd, a, b)
        down[pl.ds(40 * g, 40), :] = jnp.where(odd, b, a)
    slot = (iota((32, 128), 1) >> 3) & 7
    for q in range(OCTS1):
        hi = lo = jnp.zeros((32, 128), F32)
        for j in range(8):
            u = WIDE1 + 8 * q + j
            if u < UNITS1:
                value = unit(u)
                value = jnp.concatenate([value[0:24], value[32:40]], axis=0)
                hi = jnp.where(slot == j, turn(value, 8 * j - 56, 1), hi)
                lo = jnp.where(slot == j, turn(value, 8 * j, 1), lo)
        at = 40 * QUADS1 + 32 * q
        up[pl.ds(at, 32), :], down[pl.ds(at, 32), :] = hi, lo


def all_rows1(value):
    if value.shape[0] == 40:
        return jnp.concatenate([value[0:32], value[24:40]], axis=0)
    return jnp.concatenate([value[0:24], value[16:32], value[24:32]], axis=0)


def load1(flags, rows, lowz, highz, b, eta, kap, count):
    lane = iota((NY1, 128), 1)
    slot = iota((40, 128), 1) >> 5
    fhi, flo = flag(flags, 5), flag(flags, 4)
    for p, (f, x) in enumerate(PIECES1[:count]):
        u, h = p // 2, p % 2
        if u < WIDE1:
            place = pl.ds(40 * (u // 2), 40)
            part = 2 * h + u % 2
            both = jnp.where(slot == part, highz[place, :] * fhi, lowz[place, :] * flo)
            beyond = all_rows1(turn(both, 64 - 32 * part, 1))
        else:
            q, j = (u - WIDE1) // 8, (u - WIDE1) % 8
            place = pl.ds(40 * QUADS1 + 32 * q, 32)
            high = all_rows1(turn(highz[place, :] * fhi, 64 - 8 * j - 64 * h, 1))
            low = all_rows1(turn(lowz[place, :] * flo, 120 - 8 * j - 64 * h, 1))
            beyond = jnp.where(lane < 96, high, low)
        value = jnp.where(lane < 64, rows[f, x % NX1], beyond)
        if f < 3:
            b[f, x % NX1] = value
        else:
            (eta if f == 3 else kap)[x % NX1] = value

def coarse(flags, rows, lowz, highz, own2, up, down, b, eta, kap, wx, wy, wz, dg, dinv, v0, v, pairs, tmp):
    load1(flags, rows, lowz, highz, b, eta, kap, 2 * WIDE1)
    w = (wx, wy, wz)
    weights(eta, w, 0.25, -3, 7, NX1)
    diagonals(kap, w, dg, dinv, v0, b, -2, 6, NX1)
    sweep(v, v0, b, w, dinv, -1, 5, NX1)

    def blocks(i, carry):
        x0 = 2 * i
        for c in range(3):
            r = rest(v, b, w, dg, c, x0, x0 + 1, lax.rem(x0 + NX1 - 1, NX1))
            r = r + rest(v, b, w, dg, c, x0 + 1, x0 + 2, x0)
            at = pl.multiple_of((c * 2 + i) * 24, 8)
            pairs[pl.ds(at, 24), :] = row_pairs(tmp.at[c], r)
        at = pl.multiple_of((6 + i) * 24, 8)
        pairs[pl.ds(at, 24), :] = row_pairs(tmp.at[3], eta[x0] + eta[x0 + 1])
        at = pl.multiple_of((8 + i) * 24, 8)
        pairs[pl.ds(at, 24), :] = row_pairs(tmp.at[4], kap[x0] + kap[x0 + 1])
        return carry

    lax.fori_loop(0, 2, blocks, 0)
    pairs[...] = dot(pairs[...], mean_matrix(mean2))
    left = iota((24, 128), 1) < 64
    for f in range(5):
        value = jnp.where(left, pairs[pl.ds(48 * f, 24), :], pairs[pl.ds(48 * f + 24, 24), :])
        own2[f] = value
        up[f, 0:8], up[f, 8:16] = value[16:24], value[0:8]
        down[f] = value[0:16]


def smooth1(flags, rows, lowz, highz, b, v, dinv, wx, wy, wz, eta, kap, dg, v0):
    none = jnp.zeros((NY1, 128), F32)
    for x in (-6, 9):
        kap[x % NX1] = none
    for x in (-5, 8):
        for c in (1, 2):
            b[c, x % NX1] = none
    load1(flags, rows, lowz, highz, b, eta, kap, len(PIECES1))
    w = (wx, wy, wz)
    weights(eta, w, 0.25, -6, 10, NX1)
    diagonals(kap, w, dg, dinv, v0, b, -5, 9, NX1)
    sweep(v, v0, b, w, dinv, -4, 8, NX1)


def pack_x2(flags, own2, lowy, highy, out):
    sub = iota((8, 128), 0)
    for f in range(5):
        near, far = highy[f, 0:8] * flag(flags, 3), highy[f, 8:16] * flag(flags, 3)
        far_low, near_low = lowy[f, 0:8] * flag(flags, 2), lowy[f, 8:16] * flag(flags, 2)
        value = jnp.concatenate([own2[f, 0:8], near, jnp.where(sub < 4, far, far_low), near_low], axis=0)
        for d in range(8):
            out[d, 32 * f:32 * f + 32] = value
        if f == 3:
            for d in range(8):
                out[d, 160:168] = jnp.where(sub == 4, far, far_low)


def finish(flags, got, late_low, late_high, b1, v1, dinv1, wx1, wy1, wz1, b_own, b_far, den_own, den_far, v0, dinv0, wx0, wy0, wz0,
           velocity, new_density,
           b2, eta2, kap2, dg2, dinv2, wx2, wy2, wz2, va2, vb2,
           b3, eta3, kap3, dg3, dinv3, wx3, wy3, wz3, va3, vb3,
           pairs, spread, tmp, e2, va1, vb1, va0, vb0, wide):
    sub = iota((8, 128), 0)
    left2, left3 = iota((NY2, 128), 1) < 64, iota((NY3, 128), 1) < 64
    for f in range(5):
        two = []
        for d in range(8):
            own, near = got[d, 32 * f:32 * f + 8], got[d, 32 * f + 8:32 * f + 16]
            mix, low = got[d, 32 * f + 16:32 * f + 24], got[d, 32 * f + 24:32 * f + 32]
            far, far_low = mix, mix
            if f == 3:
                extra = got[d, 160:168]
                far, far_low = jnp.where(sub == 4, extra, mix), jnp.where(sub == 3, extra, mix)
            two.append(jnp.concatenate([own, near, far, mix, far_low, low], axis=0))
        for d in range(4):
            even = jnp.where(left2, two[d], pltpu.roll(two[d + 4], 64, 1))
            odd = jnp.where(left2, pltpu.roll(two[d], 64, 1), two[d + 4])
            if f < 3:
                b2[f, 2 * d], b2[f, 2 * d + 1] = even, odd
            else:
                out = eta2 if f == 3 else kap2
                out[2 * d], out[2 * d + 1] = even, odd

    def ends(ref, n, left, lead=()):
        first_plane, last_plane = ref[lead + (0,)], ref[lead + (n - 1,)]
        ref[lead + (n,)] = jnp.where(left, pltpu.roll(first_plane, 64, 1), 0.0)
        ref[lead + (n + 1,)] = jnp.where(left, 0.0, pltpu.roll(last_plane, 64, 1))

    def ends2(ref):
        for c in range(3):
            ends(ref, 8, left2, (c,))

    def ends3(ref):
        for c in range(3):
            ends(ref, 4, left3, (c,))

    w2 = (wx2, wy2, wz2)
    ends(eta2, 8, left2)
    weights(eta2, w2, 0.0625, -1, 8, NX2, 3)
    diagonals(kap2, w2, dg2, dinv2, va2, b2, 0, 8, NX2)
    ends2(va2)
    sweep(vb2, va2, b2, w2, dinv2, 0, 8, NX2, 4)
    ends2(vb2)

    def blocks(i, carry):
        x0 = 2 * i
        xm, xp, xq = lax.rem(x0 + NX2 - 1, NX2), x0 + 1, x0 + 2
        for c in range(3):
            r = rest(vb2, b2, w2, dg2, c, x0, xp, xm) + rest(vb2, b2, w2, dg2, c, xp, xq, x0)
            pairs[pl.ds(pl.multiple_of((c * 4 + i) * 24, 8), 24), :] = row_pairs(tmp.at[c], r)
        pairs[pl.ds(pl.multiple_of((12 + i) * 24, 8), 24), :] = row_pairs(tmp.at[3], eta2[x0] + eta2[xp])
        pairs[pl.ds(pl.multiple_of((16 + i) * 24, 8), 24), :] = row_pairs(tmp.at[4], kap2[x0] + kap2[xp])
        return carry

    lax.fori_loop(0, 4, blocks, 0)
    pairs[pl.ds(0, 480), :] = dot(pairs[pl.ds(0, 480), :], mean_matrix(mean3))
    for i in range(4):
        for c in range(3):
            b3[c, i] = pairs[pl.ds((c * 4 + i) * 24, 24), :]
        eta3[i] = pairs[pl.ds((12 + i) * 24, 24), :]
        kap3[i] = pairs[pl.ds((16 + i) * 24, 24), :]
    w3 = (wx3, wy3, wz3)
    ends(eta3, 4, left3)
    weights(eta3, w3, 0.015625, -1, 4, NX3, 5)
    diagonals(kap3, w3, dg3, dinv3, va3, b3, 0, 4, NX3)
    ends3(va3)
    sweep(vb3, va3, b3, w3, dinv3, 0, 4, NX3, 4)
    ends3(vb3)
    sweep(va3, vb3, b3, w3, dinv3, 0, 4, NX3, 4)
    ends3(va3)
    sweep(vb3, va3, b3, w3, dinv3, 0, 4, NX3, 4)

    for c in range(3):
        for i in range(4):
            pairs[pl.ds((c * 4 + i) * 24, 24), :] = vb3[c, i]
    spread[pl.ds(0, 288), :] = dot(pairs[pl.ds(0, 288), :], repeat_matrix(repeat2))

    def rise2(i, carry):
        for c in range(3):
            e = spread[pl.ds(pl.multiple_of((c * 4 + i) * 24, 8), 24), :]
            tmp[c, pl.ds(0, 24, stride=2), :] = e
            tmp[c, pl.ds(1, 24, stride=2), :] = e
            e = tmp[c]
            vb2[c, 2 * i] = vb2[c, 2 * i] + e
            vb2[c, 2 * i + 1] = vb2[c, 2 * i + 1] + e
        return carry

    lax.fori_loop(0, 4, rise2, 0)
    ends2(vb2)
    sweep(va2, vb2, b2, w2, dinv2, 0, 8, NX2, 4)
    ends2(va2)
    sweep(vb2, va2, b2, w2, dinv2, 0, 8, NX2, 4)

    none = jnp.zeros((24, 128), F32)
    for c in range(3):
        for x in (0, 1, 18, 19):
            e2[c, x] = none
        for x in range(8):
            value = jnp.concatenate([vb2[c, x, 0:16], vb2[c, x, 40:48]], axis=0)
            e2[c, 2 + x] = value
            e2[c, 10 + x] = pltpu.roll(value, 64, 1)
    start = 2 * flags[6]
    for c in range(3):
        for k in range(6):
            pairs[pl.ds((c * 6 + k) * 24, 24), :] = e2[c, start + k]
    spread[pl.ds(0, 432), :] = dot(pairs[pl.ds(0, 432), :], repeat_matrix(repeat1))

    def rise1(k, carry):
        x = lax.rem(2 * k - 4 + NX1, NX1)
        for c in range(3):
            e = spread[pl.ds(pl.multiple_of((c * 6 + k) * 24, 8), 24), :]
            tmp[c, pl.ds(0, 24, stride=2), :] = e
            tmp[c, pl.ds(1, 24, stride=2), :] = e
            e = tmp[c]
            va1[c, x] = v1[c, x] + e
            va1[c, x + 1] = v1[c, x + 1] + e
        return carry

    lax.fori_loop(0, 6, rise1, 0)
    w1 = (wx1, wy1, wz1)
    sweep_wider(vb1, va1, b1, w1, dinv1, -3, 7, NX1)
    sweep_wider(va1, vb1, b1, w1, dinv1, -2, 6, NX1)

    for c in range(3):
        for i in range(-2, 6):
            at = (c * 8 + i + 2) * 24
            x = i % NX1
            pairs[pl.ds(at, 16), :] = va1[c, x, 0:16]
            pairs[pl.ds(at + 16, 8), :] = jnp.where(sub < 4, va1[c, x, 16:24], va1[c, x, 40:48])
    wide[...] = dot(pairs[pl.ds(0, 576), :], repeat_matrix(repeat0, 256))

    def risen(c, i, half):
        here = tmp.at[2 * c + half]
        e = wide[pl.ds(pl.multiple_of((c * 8 + i) * 24, 8), 24), 128 * half:128 * half + 128]
        here[pl.ds(0, 24, stride=2), :] = e
        here[pl.ds(1, 24, stride=2), :] = e
        return here[...]

    def rise0(i, carry):
        for c in range(3):
            for half in range(2):
                e = risen(c, i + 2, half)
                lanes = slice(128 * half, 128 * half + 128)
                va0[c, 2 * i, :, lanes] = v0[c, 2 * i, :, lanes] + e
                va0[c, 2 * i + 1, :, lanes] = v0[c, 2 * i + 1, :, lanes] + e
        return carry

    lax.fori_loop(0, 4, rise0, 0)
    lane = iota((40, 128), 1)
    for high, late in ((True, late_high), (False, late_low)):
        there = flag(flags, 1 if high else 0)
        for p, (c, away) in enumerate(LATE):
            x = 7 + away if high else NX0 - away
            for half in range(2):
                if half == 0:
                    value = late[p]
                else:
                    value = turn(late[7], -8 * p - 4, 1)
                    value = jnp.where((lane < 4) | (lane >= 124), value, 0.0)
                value = jnp.concatenate([value, value[32:40]], axis=0) * there
                e = risen(c, (5 + (away + 1) // 2) if high else 2 - (away + 1) // 2, half)
                va0[c, x, :, 128 * half:128 * half + 128] = value + e
    w0 = (wx0, wy0, wz0)
    b0, den = Joined(b_own, b_far), Joined(den_own, den_far)
    sweep_wider(vb0, va0, b0, w0, dinv0, -2, 10, NX0)
    sweep_wider(va0, vb0, b0, w0, dinv0, -1, 9, NX0)

    def advect(x, carry):
        xm, xp = lax.rem(x + NX0 - 1, NX0), x + 1
        d = den[x]
        change = jnp.zeros_like(d)
        spreading = -6.0 * d
        for axis in range(3):
            u = va0[axis, x]
            if axis == 0:
                u_up, u_lo, d_up, d_lo = va0[0, xp], va0[0, xm], den[xp], den[xm]
            else:
                u_up, u_lo = back(u, axis - 1), forth(u, axis - 1)
                d_up, d_lo = back(d, axis - 1), forth(d, axis - 1)
            hi, lo = 0.5 * (u + u_up), 0.5 * (u_lo + u)
            change = change + (jnp.maximum(hi, 0.0) * d + jnp.minimum(hi, 0.0) * d_up)
            change = change - (jnp.maximum(lo, 0.0) * d_lo + jnp.minimum(lo, 0.0) * d)
            spreading = spreading + (d_up + d_lo)
            velocity[axis, x] = u[0:32, 0:128]
        out = d - STEP_TIME * change + STEP_TIME * DIFFUSION * spreading
        new_density[x] = out[0:32, 0:128]
        return carry

    lax.fori_loop(0, 8, advect, 0)


def exchange(up, down, axis, away=1):
    n = lax.axis_size(axis)
    low = lax.ppermute(up, axis, [(i, (i + away) % n) for i in range(n)])
    high = lax.ppermute(down, axis, [(i, (i - away) % n) for i in range(n)])
    return low, high


def per_device(force, grain, density):
    gx, gy, gz = (lax.axis_index(a) for a in ("gx", "gy", "gz"))
    last = [lax.axis_size(a) - 1 for a in ("gx", "gy", "gz")]
    flags = jnp.stack(
        [gx > 0, gx < last[0], gy > 0, gy < last[1], gz > 0, gz < last[2], gx, gx > 1, gx < last[0] - 1]
    ).astype(jnp.int32)

    eta, force, density, up, down = call(
        prepare, [(8, 32, 128), (3, 8, 32, 128), (8, 32, 128), (11, 32, 128), (11, 32, 128)], start=True
    )(flags, force, grain, density)
    x0 = exchange(up, down, "gx")
    up, down = call(pack_y0, [(37, 8, 128)] * 2)(flags, force, eta, density, *x0)
    y0 = exchange(up, down, "gy")
    up, down = call(pack_z0, [(3, 40, 128)] * 2)(flags, force, eta, density, *x0, *y0)
    z0 = exchange(up, down, "gz")
    vec, one = (3, NX0, NY0, NZ0), (NX0, NY0, NZ0)
    vech, oneh = (3, NX0, NY0, 128), (NX0, NY0, 128)
    b_own, eta_own, den_own, kap_own, coeffs = call(
        assemble0, [vech, oneh, oneh, oneh, (192, 128)], [(192, 128), (2, 48, 128)]
    )(flags, force, eta, density, *x0, *y0)
    b_far, den_far, v0, dinv0, wx0, wy0, wz0, own1, up, down, far_up, far_down = call(
        fine,
        [vech, oneh, vec, one, one, one, one, (5, 4, 16, 128)]
        + [(11, 16, 128)] * 2 + [(16, 128)] * 2,
        [oneh, oneh, one, vec, (192, 128), (3, 48, 128)],
    )(flags, b_own, eta_own, kap_own, coeffs, *z0)
    x1 = exchange(up, down, "gx") + exchange(far_up, far_down, "gx", 2)
    late_up, late_down = call(pack_late, [(8, 40, 128)] * 2)(flags, v0)
    x1, late_up, late_down = lax.optimization_barrier((x1, late_up, late_down))
    late = exchange(late_up, late_down, "gx")
    middle, up, down = call(
        pack_y1, [(UNITS1, 16, 128)] + [(UNITS1 + QUADS1, 8, 128)] * 2
    )(flags, own1, *x1)
    y1 = exchange(up, down, "gy")
    y1, late = lax.optimization_barrier((y1, late))
    up, down = call(pack_z1, [(40 * QUADS1 + 32 * OCTS1, 128)] * 2)(flags, middle, *y1)
    z1 = exchange(up, down, "gz")
    (rows,) = call(assemble1, [(5, NX1, NY1, 128)])(flags, middle, *y1)
    vec1, one1 = (3, NX1, NY1, 128), (NX1, NY1, 128)
    own2, up, down = call(
        coarse,
        [(5, 24, 128), (5, 16, 128), (5, 16, 128)],
        [vec1, one1, one1, one1, one1, one1, one1, one1, vec1, vec1, (240, 128), (5, 48, 128)],
    )(flags, rows, *z1)
    y2 = exchange(up, down, "gy")
    smooth = call(smooth1, [vec1, vec1, one1, one1, one1, one1], [one1, one1, one1, vec1])(flags, rows, *z1)
    y2, smooth = lax.optimization_barrier((y2, smooth))
    (chunk,) = call(pack_x2, [(8, 168, 128)])(flags, own2, *y2)
    got = lax.all_to_all(chunk, "gx", 0, 0, tiled=True)
    vec2, one2 = (3, NX2, NY2, 128), (NX2, NY2, 128)
    vec3, one3 = (3, NX3, NY3, 128), (NX3, NY3, 128)
    velocity, new_density = call(
        finish,
        [(3, 8, 32, 128), (8, 32, 128)],
        [vec2, one2, one2, one2, one2, one2, one2, one2, vec2, vec2]
        + [vec3, one3, one3, one3, one3, one3, one3, one3, vec3, vec3]
        + [(576, 128), (576, 128), (6, 48, 128), (3, 20, 24, 128), vec1, vec1, vec, vec, (576, 256)],
        limit=32,
        final=True,
    )(flags, got, *late, *smooth, b_own, b_far, den_own, den_far, v0, dinv0, wx0, wy0, wz0)
    return velocity, new_density


def solution(mesh):
    return jax.shard_map(
        per_device,
        mesh=mesh,
        in_specs=(P(None, "gx", "gy", "gz"), P("gx", "gy", "gz"), P("gx", "gy", "gz")),
        out_specs=(P(None, "gx", "gy", "gz"), P("gx", "gy", "gz")),
        check_vma=False,
    )
```

```python
import jax
import jax.numpy as jnp
from jax import lax
from jax.experimental import pallas as pl
from jax.experimental.pallas import tpu as pltpu
from jax.sharding import PartitionSpec as P

OMEGA = 0.8
STEP_TIME = 0.1
DIFFUSION = 0.05
grain_table = [0.5 * 8.0 ** (entry / 15.0) for entry in range(16)]
F32 = jnp.float32
MIB = 1024 * 1024

W0 = (2, 2, 2, 3, 2)
OFF0 = (0, 2, 4, 6, 9)
Z0 = (4, 4, 4, 5, 4)
ZOFF0 = (5, 9, 13, 0, 17)
ZSLOT0 = 22
NX0, NY0, NZ0 = 14, 48, 256
PAIRS0 = ((0, 1), (2, 3), (4, 5), (6, 7), (8, 13), (9, 12))
LATE = ((0, 3), (0, 2), (0, 1), (1, 2), (1, 1), (2, 2), (2, 1))
W1 = (4, 4, 4, 5, 5)
OFF1 = (0, 4, 8, 12, 17)
FAR1 = ((0, -5), (0, 8), (3, -6), (3, 9))
NX1, NY1 = 16, 40
NEAR1 = (2, 2, 2, 3, 2)
PIECES1 = [(f, x) for f in range(5) for x in range(-NEAR1[f], 4 + NEAR1[f])]
WIDE1 = len(PIECES1) // 2
PIECES1 += [(f, x) for f in range(5) for x in range(-W1[f], 4 + W1[f]) if (f, x) not in PIECES1]
UNITS1 = len(PIECES1) // 2
QUADS1 = (WIDE1 + 1) // 2
OCTS1 = (UNITS1 - WIDE1 + 7) // 8
NX2, NY2 = 10, 40
NX3, NY3 = 6, 24


def iota(shape, dim):
    return lax.broadcasted_iota(jnp.int32, shape, dim)


def back(value, axis):
    return pltpu.roll(value, value.shape[axis] - 1, axis)


def forth(value, axis):
    return pltpu.roll(value, 1, axis)


def turn(value, shift, axis):
    shift = shift % value.shape[axis]
    return value if shift == 0 else pltpu.roll(value, shift, axis)


def call(body, outs, scratch=(), limit=12, start=False, final=False):
    def run(flags, *operands):
        if not final:
            shapes = [pltpu.VMEM(s, F32) for s in outs]
        else:
            shapes = [jax.ShapeDtypeStruct(s, F32) for s in outs]
        return pl.pallas_call(
            body,
            out_shape=shapes,
            in_specs=[pl.BlockSpec(memory_space=pltpu.SMEM)]
            + [pl.BlockSpec(memory_space=pltpu.VMEM)] * len(operands),
            out_specs=[pl.BlockSpec(memory_space=pltpu.VMEM)] * len(outs),
            scratch_shapes=[pltpu.VMEM(s, F32) for s in scratch],
            compiler_params=pltpu.CompilerParams(vmem_limit_bytes=limit * MIB),
        )(flags, *[pltpu.with_memory_space_constraint(o, pltpu.HBM if start else pltpu.VMEM) for o in operands])

    return run


def flag(flags, index):
    return flags[index].astype(F32)


def weighted(v, w, c, x, xp, xm):
    wx, wy, wz = w
    here = v[c, x]
    total = wx[x] * v[c, xp] + wx[xm] * v[c, xm]
    a = wy[x]
    total = total + a * back(here, 0) + forth(a * here, 0)
    a = wz[x]
    total = total + a * back(here, 1) + forth(a * here, 1)
    return here, total


def planes(lo, hi, n, body, unroll=2):
    assert (hi - lo) % unroll == 0

    def step(k, carry):
        for j in range(unroll):
            x = lax.rem(unroll * k + (lo + n + j), n)
            body(x, lax.rem(x + 1, n), lax.rem(x + n - 1, n))
        return carry

    lax.fori_loop(0, (hi - lo) // unroll, step, 0)


def sweep(dst, src, b, w, dinv, lo, hi, n, unroll=2):
    def body(x, xp, xm):
        scale = dinv[x]
        for c in range(3):
            here, total = weighted(src, w, c, x, xp, xm)
            dst[c, x] = 0.2 * here + scale * (b[c, x] + total)

    planes(lo, hi, n, body, unroll)


def sweep_wider(dst, src, b, w, dinv, lo, hi, n):
    sweep(dst, src, b, w, dinv, lo + 1, hi - 1, n)
    for x in (lo % n, (hi - 1) % n):
        here, total = weighted(src, w, 0, x, (x + 1) % n, (x - 1) % n)
        dst[0, x] = 0.2 * here + dinv[x] * (b[0, x] + total)


def weights(eta, w, factor, lo, hi, n, unroll=2):
    wx, wy, wz = w
    half = 0.5 * factor

    def body(x, xp, xm):
        here = eta[x]
        wx[x] = half * (here + eta[xp])
        wy[x] = half * (here + back(here, 0))
        wz[x] = half * (here + back(here, 1))

    planes(lo, hi, n, body, unroll)


def diagonals(kap, w, dg, dinv, v, b, lo, hi, n):
    wx, wy, wz = w

    def body(x, xp, xm):
        k, a, g = kap[x], wy[x], wz[x]
        d = k + (wx[x] + wx[xm]) + (a + forth(a, 0)) + (g + forth(g, 1))
        inside = k > 0.0
        scale = jnp.where(inside, OMEGA / jnp.where(inside, d, 1.0), 0.0)
        dg[x] = d
        dinv[x] = scale
        for c in range(3):
            v[c, x] = scale * b[c, x]

    planes(lo, hi, n, body)


def rest(v, b, w, dg, c, x, xp, xm):
    here, total = weighted(v, w, c, x, xp, xm)
    return b[c, x] - dg[x] * here + total


def mean_matrix(source):
    k, j = iota((128, 128), 0), iota((128, 128), 1)
    return jnp.where((k >> 1) == source(j), 0.125, 0.0).astype(F32)


def repeat_matrix(source, out=128):
    k, j = iota((128, out), 0), iota((128, out), 1)
    return jnp.where(k == source(j), 1.0, 0.0).astype(F32)


def mean1(j):
    return j & 63


def mean2(j):
    return (j + 48) & 63


def mean3(j):
    return jnp.where((j & 63) < 32, ((j >> 6) << 5) + (j & 63), -1)


def repeat2(j):
    return (j & 64) + ((j & 63) >> 1)


def repeat1(j):
    return ((j >> 1) + 16) & 63


def repeat0(j):
    return j >> 1


def dot(a, b):
    b = b.astype(jnp.bfloat16)
    high = a.astype(jnp.bfloat16)
    rest_of = a - high.astype(F32)
    middle = rest_of.astype(jnp.bfloat16)
    low = (rest_of - middle.astype(F32)).astype(jnp.bfloat16)
    product = lambda piece: jnp.dot(piece, b, preferred_element_type=F32)
    return product(high) + (product(middle) + product(low))


class Joined:
    def __init__(self, left, right):
        self.parts = (left, right)

    def __getitem__(self, index):
        return jnp.concatenate([part[index] for part in self.parts], axis=1)


def row_pairs(tmp, value):
    rows = value.shape[0]
    tmp[pl.ds(0, rows), :] = value
    return tmp[pl.ds(0, rows // 2, stride=2), :] + tmp[pl.ds(1, rows // 2, stride=2), :]


def prepare(flags, force, grain, dens, eta, force_kept, dens_kept, up, down):
    for x in range(8):
        ids = grain[x]
        looked = jnp.full(ids.shape, grain_table[0], F32)
        for entry in range(1, 16):
            looked = jnp.where(ids == entry, grain_table[entry], looked)
        d = dens[x]
        eta[x] = looked * d * d * d
        dens_kept[x] = d
        for c in range(3):
            force_kept[c, x] = force[c, x]
    for f in range(5):
        for k in range(W0[f]):
            for out, x in ((up, 8 - W0[f] + k), (down, k)):
                out[OFF0[f] + k] = force[f, x] if f < 3 else (eta if f == 3 else dens)[x]


def plane0(flags, own, f, x, rows):
    force, eta, dens, low, high = own
    if 0 <= x < 8:
        return force[f, x, rows] if f < 3 else (eta if f == 3 else dens)[x, rows]
    away = x - 8 if x >= 8 else -x - 1
    if away >= W0[f]:
        return jnp.zeros((rows.stop - rows.start, 128), F32)
    if x >= 8:
        return high[OFF0[f] + away, rows] * flag(flags, 1)
    return low[OFF0[f] + W0[f] - 1 - away, rows] * flag(flags, 0)


def rel0(x):
    return x if x < 11 else x - NX0


YT0 = (0, 5, 10, 20, 15)
FIFTH0 = 26


def halo0(f, x):
    for q, pair in enumerate(PAIRS0[:6 if f == 3 else 5]):
        if x in pair:
            return q, pair.index(x)
    return None


def pack_y0(flags, force, eta, dens, low, high, up, down):
    own = (force, eta, dens, low, high)
    sub = iota((8, 128), 0)
    for f in range(5):
        for q, pair in enumerate(PAIRS0[:6 if f == 3 else 5]):
            a, b = (rel0(x) for x in pair)
            top, bottom = slice(24, 32), slice(0, 8)
            up[YT0[f] + q] = jnp.where(
                sub < 4, turn(plane0(flags, own, f, a, top), 4, 0), plane0(flags, own, f, b, top)
            )
            down[YT0[f] + q] = jnp.where(
                sub < 4, plane0(flags, own, f, a, bottom), turn(plane0(flags, own, f, b, bottom), 4, 0)
            )
    hi = lo = jnp.zeros((8, 128), F32)
    for x in range(8):
        hi = jnp.where(sub == x, turn(eta[x, 24:32], x - 3, 0), hi)
        lo = jnp.where(sub == x, turn(eta[x, 0:8], x - 4, 0), lo)
    up[FIFTH0], down[FIFTH0] = hi, lo


def rows0(flags, own, lowy, highy, f, x):
    sub = iota((8, 128), 0)
    middle = plane0(flags, own, f, rel0(x), slice(0, 32))
    if halo0(f, x) is None:
        return jnp.concatenate([middle, jnp.zeros((16, 128), F32)], axis=0)
    q, second = halo0(f, x)
    high, low = highy[YT0[f] + q], lowy[YT0[f] + q]
    if second:
        high = turn(high, 4, 0)
    else:
        low = turn(low, 4, 0)
    if f == 3 and x < 8:
        high = jnp.where(sub == 4, turn(highy[FIFTH0], 4 - x, 0), high)
        low = jnp.where(sub == 3, turn(lowy[FIFTH0], 3 - x, 0), low)
    return jnp.concatenate([middle, high * flag(flags, 3), low * flag(flags, 2)], axis=0)


def slot0(f, x):
    if x in PAIRS0[5]:
        return PAIRS0[5].index(x), 5 * ZSLOT0 + 5
    order = x if x < 9 else 9
    return order // 5, ZSLOT0 * (order % 5) + 5 + ZOFF0[f]


def pack_z0(flags, force, eta, dens, lowx, highx, lowy, highy, up, down):
    own = (force, eta, dens, lowx, highx)
    lane, sub = iota((40, 128), 1), iota((8, 128), 0)
    for g in range(2):
        hi = lo = jnp.zeros((40, 128), F32)
        for f in range(5):
            for x in range(NX0):
                if halo0(f, x) is None or slot0(f, x)[0] != g:
                    continue
                at, w = slot0(f, x)[1], Z0[f]
                value = rows0(flags, own, lowy, highy, f, x)
                mix = jnp.where(sub < 4, value[32:40], value[40:48])
                value = turn(jnp.concatenate([value[0:32], mix], axis=0), at, 1)
                hi = jnp.where((lane >= at - w) & (lane < at), value, hi)
                lo = jnp.where((lane >= at) & (lane < at + w), value, lo)
        up[g], down[g] = hi, lo


def assemble0(flags, force, eta, dens, lowx, highx, lowy, highy, b, eta0, den, kap, coeffs, pairs, tmp):
    own = (force, eta, dens, lowx, highx)
    for x in range(NX0):
        for f in range(5):
            value = rows0(flags, own, lowy, highy, f, x)
            if f < 3:
                b[f, x] = value
            else:
                (eta0 if f == 3 else den)[x] = value
                if f == 4:
                    kap[x] = jnp.where(value > 0.0, 0.02 + 0.08 * value, 0.0)
    for i in range(-1, 5):
        x = (2 * i) % NX0
        for k, field in enumerate((eta0, kap)):
            r = field[x, 0:32] + field[x + 1, 0:32]
            pairs[pl.ds((6 * k + i + 1) * 16, 16), :] = row_pairs(tmp.at[k], r)
    coeffs[...] = dot(pairs[...], mean_matrix(mean1))


def fine(flags, b_own, eta_own, kap_own, coeffs, lowz, highz,
         b_far, den_far, v, dinv, wx, wy, wz, own1, up, down, far_up, far_down,
         eta_far, kap_far, dg, v0, pairs, tmp):
    lane = iota((40, 128), 1)
    fhi, flo = flag(flags, 5), flag(flags, 4)
    packets = [(highz[g] * fhi, lowz[g] * flo) for g in range(2)]
    for x in range(NX0):
        for f in range(5):
            if halo0(f, x) is None:
                zero = jnp.zeros((NY0, 128), F32)
                if f < 3:
                    b_far[f, x] = zero
                elif f == 3:
                    eta_far[x] = zero
                else:
                    den_far[x], kap_far[x] = zero, zero
                continue
            (g, at), w = slot0(f, x), Z0[f]
            both = turn(jnp.where(lane >= at, *packets[g]), -at, 1)
            beyond = jnp.where((lane < w) | (lane >= 128 - w), both, 0.0)
            beyond = jnp.concatenate([beyond, beyond[32:40]], axis=0)
            if f < 3:
                b_far[f, x] = beyond
            elif f == 3:
                eta_far[x] = beyond
            else:
                den_far[x] = beyond
                kap_far[x] = jnp.where(beyond > 0.0, 0.02 + 0.08 * beyond, 0.0)
    b, eta0, kap = Joined(b_own, b_far), Joined(eta_own, eta_far), Joined(kap_own, kap_far)
    w = (wx, wy, wz)
    weights(eta0, w, 1.0, -3, 11, NX0)
    diagonals(kap, w, dg, dinv, v0, b, -2, 10, NX0)
    sweep(v, v0, b, w, dinv, -1, 9, NX0)

    def blocks(i, carry):
        x0 = 2 * i
        xm, xp, xq = lax.rem(x0 + NX0 - 1, NX0), x0 + 1, x0 + 2
        for c in range(3):
            r = rest(v, b, w, dg, c, x0, xp, xm) + rest(v, b, w, dg, c, xp, xq, x0)
            at = pl.multiple_of((c * 4 + i) * 16, 16)
            pairs[pl.ds(at, 16), :] = row_pairs(tmp.at[c], r[0:32, 0:128])
        return carry

    lax.fori_loop(0, 4, blocks, 0)
    pairs[...] = dot(pairs[...], mean_matrix(mean1))

    def piece(f, i):
        if f < 3:
            return pairs[pl.ds((f * 4 + i) * 16, 16), :]
        return coeffs[pl.ds((6 * (f - 3) + i + 1) * 16, 16), :]

    half = iota((16, 128), 1) < 64
    ups = [(f, i) for f in range(5) for i in range(4 - W1[f], 4)]
    downs = [(f, i) for f in range(5) for i in range(0, W1[f])]
    for k in range(11):
        up[k] = jnp.where(half, piece(*ups[2 * k]), piece(*ups[2 * k + 1]))
        down[k] = jnp.where(half, piece(*downs[2 * k]), piece(*downs[2 * k + 1]))
    far_up[...] = jnp.where(half, piece(0, 3), piece(3, 2))
    far_down[...] = jnp.where(half, piece(0, 0), piece(3, 1))
    for f in range(5):
        for i in range(4):
            own1[f, i] = piece(f, i)


def pack_late(flags, v, late_up, late_down):
    sub, slot = iota((8, 128), 0), iota((40, 128), 1) >> 3
    for out, top in ((late_up, True), (late_down, False)):
        edge = jnp.zeros((40, 128), F32)
        for p, (c, away) in enumerate(LATE):
            x = 8 - away if top else away - 1
            for half in range(2):
                value = v[c, x, :, 128 * half:128 * half + 128]
                mix = jnp.where(sub < 4, value[32:40], value[40:48])
                value = jnp.concatenate([value[0:32], mix], axis=0)
                if half == 0:
                    out[p] = value
                else:
                    edge = jnp.where(slot == p, turn(value, 8 * p + 4, 1), edge)
        out[7] = edge


def plane1(flags, own1, lowx, highx, f, x, half):
    if 0 <= x < 4:
        return own1[f, x]
    away = x - 4 if x >= 4 else -x - 1
    if x >= 4:
        at = OFF1[f] + away
        source, there = highx[at // 2], flag(flags, 1)
    else:
        at = OFF1[f] + W1[f] - 1 - away
        source, there = lowx[at // 2], flag(flags, 0)
    return turn(source, 64 * ((at + half) % 2), 1) * there


def pack_y1(flags, own1, lowx, highx, middle, up, down):
    sub = iota((8, 128), 0)
    left = iota((16, 128), 1) < 64
    sent = (flags, own1, lowx, highx)
    hi = lo = None
    for u in range(UNITS1):
        value = jnp.where(left, plane1(*sent, *PIECES1[2 * u], 0), plane1(*sent, *PIECES1[2 * u + 1], 1))
        middle[u] = value
        up[u], down[u] = value[8:16], value[0:8]
        if u < WIDE1:
            if u % 2 == 0:
                hi, lo = turn(value[0:8], 4, 0), value[8:16]
            else:
                hi, lo = jnp.where(sub < 4, hi, value[0:8]), jnp.where(sub < 4, lo, turn(value[8:16], 4, 0))
            up[UNITS1 + u // 2], down[UNITS1 + u // 2] = hi, lo


def unit1(flags, middle, lowy, highy, u):
    sub = iota((8, 128), 0)
    fhi, flo = flag(flags, 3), flag(flags, 2)
    if u < WIDE1:
        high, low = highy[UNITS1 + u // 2], lowy[UNITS1 + u // 2]
        high, low = (turn(high, 4, 0), low) if u % 2 else (high, turn(low, 4, 0))
        mix = jnp.where(sub < 4, high * fhi, low * flo)
    else:
        mix = jnp.zeros((8, 128), F32)
    value = jnp.concatenate([middle[u], highy[u] * fhi, mix, lowy[u] * flo], axis=0)
    return value


def assemble1(flags, middle, lowy, highy, rows):
    for u in range(UNITS1):
        value = unit1(flags, middle, lowy, highy, u)
        for h in range(2):
            f, x = PIECES1[2 * u + h]
            rows[f, x % NX1] = turn(value, 64 * h, 1)


def pack_z1(flags, middle, lowy, highy, up, down):
    lane = iota((40, 128), 1)

    def unit(u):
        return unit1(flags, middle, lowy, highy, u)

    odd = ((lane >> 5) & 1) == 1
    for g in range(QUADS1):
        a = unit(2 * g)
        b = unit(2 * g + 1) if 2 * g + 1 < WIDE1 else a
        b = turn(b, 32, 1)
        up[pl.ds(40 * g, 40), :] = jnp.where(odd, a, b)
        down[pl.ds(40 * g, 40), :] = jnp.where(odd, b, a)
    slot = (iota((32, 128), 1) >> 3) & 7
    for q in range(OCTS1):
        hi = lo = jnp.zeros((32, 128), F32)
        for j in range(8):
            u = WIDE1 + 8 * q + j
            if u < UNITS1:
                value = unit(u)
                value = jnp.concatenate([value[0:24], value[32:40]], axis=0)
                hi = jnp.where(slot == j, turn(value, 8 * j - 56, 1), hi)
                lo = jnp.where(slot == j, turn(value, 8 * j, 1), lo)
        at = 40 * QUADS1 + 32 * q
        up[pl.ds(at, 32), :], down[pl.ds(at, 32), :] = hi, lo


def all_rows1(value):
    return jnp.concatenate([value[0:24], value[16:32]], axis=0)


def load1(flags, rows, lowz, highz, b, eta, kap, count):
    lane = iota((NY1, 128), 1)
    slot = iota((40, 128), 1) >> 5
    fhi, flo = flag(flags, 5), flag(flags, 4)
    for p, (f, x) in enumerate(PIECES1[:count]):
        u, h = p // 2, p % 2
        if u < WIDE1:
            place = pl.ds(40 * (u // 2), 40)
            part = 2 * h + u % 2
            both = jnp.where(slot == part, highz[place, :] * fhi, lowz[place, :] * flo)
            beyond = turn(both, 64 - 32 * part, 1)
        else:
            q, j = (u - WIDE1) // 8, (u - WIDE1) % 8
            place = pl.ds(40 * QUADS1 + 32 * q, 32)
            high = all_rows1(turn(highz[place, :] * fhi, 64 - 8 * j - 64 * h, 1))
            low = all_rows1(turn(lowz[place, :] * flo, 120 - 8 * j - 64 * h, 1))
            beyond = jnp.where(lane < 96, high, low)
        value = jnp.where(lane < 64, rows[f, x % NX1], beyond)
        if f < 3:
            b[f, x % NX1] = value
        else:
            (eta if f == 3 else kap)[x % NX1] = value

def coarse(flags, rows, lowz, highz, own2, up, down, b, eta, kap, wx, wy, wz, dg, dinv, v0, v, pairs, tmp):
    load1(flags, rows, lowz, highz, b, eta, kap, 2 * WIDE1)
    w = (wx, wy, wz)
    weights(eta, w, 0.25, -3, 7, NX1)
    diagonals(kap, w, dg, dinv, v0, b, -2, 6, NX1)
    sweep(v, v0, b, w, dinv, -1, 5, NX1)

    def blocks(i, carry):
        x0 = 2 * i
        for c in range(3):
            r = rest(v, b, w, dg, c, x0, x0 + 1, lax.rem(x0 + NX1 - 1, NX1))
            r = r + rest(v, b, w, dg, c, x0 + 1, x0 + 2, x0)
            at = pl.multiple_of((c * 2 + i) * 24, 8)
            pairs[pl.ds(at, 20), :] = row_pairs(tmp.at[c], r)
        at = pl.multiple_of((6 + i) * 24, 8)
        pairs[pl.ds(at, 20), :] = row_pairs(tmp.at[3], eta[x0] + eta[x0 + 1])
        at = pl.multiple_of((8 + i) * 24, 8)
        pairs[pl.ds(at, 20), :] = row_pairs(tmp.at[4], kap[x0] + kap[x0 + 1])
        return carry

    lax.fori_loop(0, 2, blocks, 0)
    pairs[...] = dot(pairs[...], mean_matrix(mean2))
    left = iota((8, 128), 1) < 64
    for f in range(5):
        own, high, low = (
            jnp.where(left, pairs[pl.ds(48 * f + at, 8), :], pairs[pl.ds(48 * f + 24 + at, 8), :])
            for at in (0, 8, 12)
        )
        own2[f] = own
        up[f, 0:8], up[f, 8:16] = low, own
        down[f, 0:8], down[f, 8:16] = own, high


def smooth1(flags, rows, lowz, highz, far_low, far_high, b, v, dinv, wx, wy, wz, eta, kap, dg, v0):
    none = jnp.zeros((NY1, 128), F32)
    for x in (-6, 9):
        kap[x % NX1] = none
    for x in (-5, 8):
        for c in (1, 2):
            b[c, x % NX1] = none
    for f, x in FAR1:
        source = far_high[...] * flag(flags, 8) if x > 0 else far_low[...] * flag(flags, 7)
        value = jnp.concatenate([turn(source, 64 * int(f == 3), 1), none[0:24]], axis=0)
        if f == 0:
            b[0, x % NX1] = value
        else:
            eta[x % NX1] = value
    load1(flags, rows, lowz, highz, b, eta, kap, len(PIECES1))
    w = (wx, wy, wz)
    weights(eta, w, 0.25, -6, 10, NX1)
    diagonals(kap, w, dg, dinv, v0, b, -5, 9, NX1)
    sweep(v, v0, b, w, dinv, -4, 8, NX1)


def pack_x2(flags, own2, lowy, highy, out):
    sub = iota((8, 128), 0)
    for f in range(5):
        near, far = highy[f, 0:8] * flag(flags, 3), highy[f, 8:16] * flag(flags, 3)
        far_low, near_low = lowy[f, 0:8] * flag(flags, 2), lowy[f, 8:16] * flag(flags, 2)
        value = jnp.concatenate([own2[f], near, jnp.where(sub < 4, far, far_low), near_low], axis=0)
        for d in range(8):
            out[d, 32 * f:32 * f + 32] = value
        if f == 3:
            for d in range(8):
                out[d, 160:168] = jnp.where(sub == 4, far, far_low)


def finish(flags, got, late_low, late_high, b1, v1, dinv1, wx1, wy1, wz1, b_own, b_far, den_own, den_far, v0, dinv0, wx0, wy0, wz0,
           velocity, new_density,
           b2, eta2, kap2, dg2, dinv2, wx2, wy2, wz2, va2, vb2,
           b3, eta3, kap3, dg3, dinv3, wx3, wy3, wz3, va3, vb3,
           pairs, spread, tmp, e2, va1, vb1, va0, vb0, wide):
    sub = iota((8, 128), 0)
    left2, left3 = iota((NY2, 128), 1) < 64, iota((NY3, 128), 1) < 64
    for f in range(5):
        two = []
        for d in range(8):
            own, near = got[d, 32 * f:32 * f + 8], got[d, 32 * f + 8:32 * f + 16]
            mix, low = got[d, 32 * f + 16:32 * f + 24], got[d, 32 * f + 24:32 * f + 32]
            far, far_low = mix, mix
            if f == 3:
                extra = got[d, 160:168]
                far, far_low = jnp.where(sub == 4, extra, mix), jnp.where(sub == 3, extra, mix)
            two.append(jnp.concatenate([far_low, low, own, near, far], axis=0))
        for d in range(4):
            even = jnp.where(left2, two[d], pltpu.roll(two[d + 4], 64, 1))
            odd = jnp.where(left2, pltpu.roll(two[d], 64, 1), two[d + 4])
            if f < 3:
                b2[f, 2 * d], b2[f, 2 * d + 1] = even, odd
            else:
                out = eta2 if f == 3 else kap2
                out[2 * d], out[2 * d + 1] = even, odd

    def ends(ref, n, left, lead=()):
        first_plane, last_plane = ref[lead + (0,)], ref[lead + (n - 1,)]
        ref[lead + (n,)] = jnp.where(left, pltpu.roll(first_plane, 64, 1), 0.0)
        ref[lead + (n + 1,)] = jnp.where(left, 0.0, pltpu.roll(last_plane, 64, 1))

    def ends2(ref):
        for c in range(3):
            ends(ref, 8, left2, (c,))

    def ends3(ref):
        for c in range(3):
            ends(ref, 4, left3, (c,))

    w2 = (wx2, wy2, wz2)
    ends(eta2, 8, left2)
    weights(eta2, w2, 0.0625, -1, 8, NX2, 3)
    diagonals(kap2, w2, dg2, dinv2, va2, b2, 0, 8, NX2)
    ends2(va2)
    sweep(vb2, va2, b2, w2, dinv2, 0, 8, NX2, 4)
    ends2(vb2)

    def blocks(i, carry):
        x0 = 2 * i
        xm, xp, xq = lax.rem(x0 + NX2 - 1, NX2), x0 + 1, x0 + 2
        for c in range(3):
            r = rest(vb2, b2, w2, dg2, c, x0, xp, xm) + rest(vb2, b2, w2, dg2, c, xp, xq, x0)
            pairs[pl.ds(pl.multiple_of((c * 4 + i) * 24, 8), 20), :] = row_pairs(tmp.at[c], r)
        pairs[pl.ds(pl.multiple_of((12 + i) * 24, 8), 20), :] = row_pairs(tmp.at[3], eta2[x0] + eta2[xp])
        pairs[pl.ds(pl.multiple_of((16 + i) * 24, 8), 20), :] = row_pairs(tmp.at[4], kap2[x0] + kap2[xp])
        return carry

    lax.fori_loop(0, 4, blocks, 0)
    pairs[pl.ds(0, 480), :] = dot(pairs[pl.ds(0, 480), :], mean_matrix(mean3))
    for i in range(4):
        for c in range(3):
            b3[c, i] = pairs[pl.ds((c * 4 + i) * 24, 24), :]
        eta3[i] = pairs[pl.ds((12 + i) * 24, 24), :]
        kap3[i] = pairs[pl.ds((16 + i) * 24, 24), :]
    w3 = (wx3, wy3, wz3)
    ends(eta3, 4, left3)
    weights(eta3, w3, 0.015625, -1, 4, NX3, 5)
    diagonals(kap3, w3, dg3, dinv3, va3, b3, 0, 4, NX3)
    ends3(va3)
    sweep(vb3, va3, b3, w3, dinv3, 0, 4, NX3, 4)
    ends3(vb3)
    sweep(va3, vb3, b3, w3, dinv3, 0, 4, NX3, 4)
    ends3(va3)
    sweep(vb3, va3, b3, w3, dinv3, 0, 4, NX3, 4)

    for c in range(3):
        for i in range(4):
            pairs[pl.ds((c * 4 + i) * 24, 24), :] = vb3[c, i]
    spread[pl.ds(0, 288), :] = dot(pairs[pl.ds(0, 288), :], repeat_matrix(repeat2))

    def rise2(i, carry):
        for c in range(3):
            e = spread[pl.ds(pl.multiple_of((c * 4 + i) * 24, 8), 24), :]
            tmp[c, pl.ds(0, 24, stride=2), :] = e
            tmp[c, pl.ds(1, 24, stride=2), :] = e
            e = tmp[c, 0:40]
            vb2[c, 2 * i] = vb2[c, 2 * i] + e
            vb2[c, 2 * i + 1] = vb2[c, 2 * i + 1] + e
        return carry

    lax.fori_loop(0, 4, rise2, 0)
    ends2(vb2)
    sweep(va2, vb2, b2, w2, dinv2, 0, 8, NX2, 4)
    ends2(va2)
    sweep(vb2, va2, b2, w2, dinv2, 0, 8, NX2, 4)

    none = jnp.zeros((24, 128), F32)
    for c in range(3):
        for x in (0, 1, 18, 19):
            e2[c, x] = none
        for x in range(8):
            value = jnp.concatenate([vb2[c, x, 16:32], turn(vb2[c, x, 8:16], 4, 0)], axis=0)
            e2[c, 2 + x] = value
            e2[c, 10 + x] = pltpu.roll(value, 64, 1)
    start = 2 * flags[6]
    for c in range(3):
        for k in range(6):
            pairs[pl.ds((c * 6 + k) * 24, 24), :] = e2[c, start + k]
    spread[pl.ds(0, 432), :] = dot(pairs[pl.ds(0, 432), :], repeat_matrix(repeat1))

    def rise1(k, carry):
        x = lax.rem(2 * k - 4 + NX1, NX1)
        for c in range(3):
            e = spread[pl.ds(pl.multiple_of((c * 6 + k) * 24, 8), 24), :]
            tmp[c, pl.ds(0, 24, stride=2), :] = e
            tmp[c, pl.ds(1, 24, stride=2), :] = e
            e = tmp[c, 0:40]
            va1[c, x] = v1[c, x] + e
            va1[c, x + 1] = v1[c, x + 1] + e
        return carry

    lax.fori_loop(0, 6, rise1, 0)
    w1 = (wx1, wy1, wz1)
    sweep_wider(vb1, va1, b1, w1, dinv1, -3, 7, NX1)
    sweep_wider(va1, vb1, b1, w1, dinv1, -2, 6, NX1)

    for c in range(3):
        for i in range(-2, 6):
            at = (c * 8 + i + 2) * 24
            x = i % NX1
            pairs[pl.ds(at, 16), :] = va1[c, x, 0:16]
            pairs[pl.ds(at + 16, 8), :] = jnp.where(sub < 4, va1[c, x, 16:24], va1[c, x, 32:40])
    wide[...] = dot(pairs[pl.ds(0, 576), :], repeat_matrix(repeat0, 256))

    def risen(c, i, half):
        here = tmp.at[2 * c + half]
        e = wide[pl.ds(pl.multiple_of((c * 8 + i) * 24, 8), 24), 128 * half:128 * half + 128]
        here[pl.ds(0, 24, stride=2), :] = e
        here[pl.ds(1, 24, stride=2), :] = e
        return here[...]

    def rise0(i, carry):
        for c in range(3):
            for half in range(2):
                e = risen(c, i + 2, half)
                lanes = slice(128 * half, 128 * half + 128)
                va0[c, 2 * i, :, lanes] = v0[c, 2 * i, :, lanes] + e
                va0[c, 2 * i + 1, :, lanes] = v0[c, 2 * i + 1, :, lanes] + e
        return carry

    lax.fori_loop(0, 4, rise0, 0)
    lane = iota((40, 128), 1)
    for high, late in ((True, late_high), (False, late_low)):
        there = flag(flags, 1 if high else 0)
        for p, (c, away) in enumerate(LATE):
            x = 7 + away if high else NX0 - away
            for half in range(2):
                if half == 0:
                    value = late[p]
                else:
                    value = turn(late[7], -8 * p - 4, 1)
                    value = jnp.where((lane < 4) | (lane >= 124), value, 0.0)
                value = jnp.concatenate([value, value[32:40]], axis=0) * there
                e = risen(c, (5 + (away + 1) // 2) if high else 2 - (away + 1) // 2, half)
                va0[c, x, :, 128 * half:128 * half + 128] = value + e
    w0 = (wx0, wy0, wz0)
    b0, den = Joined(b_own, b_far), Joined(den_own, den_far)
    sweep_wider(vb0, va0, b0, w0, dinv0, -2, 10, NX0)
    sweep_wider(va0, vb0, b0, w0, dinv0, -1, 9, NX0)

    def advect(x, carry):
        xm, xp = lax.rem(x + NX0 - 1, NX0), x + 1
        d = den[x]
        change = jnp.zeros_like(d)
        spreading = -6.0 * d
        for axis in range(3):
            u = va0[axis, x]
            if axis == 0:
                u_up, u_lo, d_up, d_lo = va0[0, xp], va0[0, xm], den[xp], den[xm]
            else:
                u_up, u_lo = back(u, axis - 1), forth(u, axis - 1)
                d_up, d_lo = back(d, axis - 1), forth(d, axis - 1)
            hi, lo = 0.5 * (u + u_up), 0.5 * (u_lo + u)
            change = change + (jnp.maximum(hi, 0.0) * d + jnp.minimum(hi, 0.0) * d_up)
            change = change - (jnp.maximum(lo, 0.0) * d_lo + jnp.minimum(lo, 0.0) * d)
            spreading = spreading + (d_up + d_lo)
            velocity[axis, x] = u[0:32, 0:128]
        out = d - STEP_TIME * change + STEP_TIME * DIFFUSION * spreading
        new_density[x] = out[0:32, 0:128]
        return carry

    lax.fori_loop(0, 8, advect, 0)


def exchange(up, down, axis, away=1):
    n = lax.axis_size(axis)
    low = lax.ppermute(up, axis, [(i, (i + away) % n) for i in range(n)])
    high = lax.ppermute(down, axis, [(i, (i - away) % n) for i in range(n)])
    return low, high


def per_device(force, grain, density):
    gx, gy, gz = (lax.axis_index(a) for a in ("gx", "gy", "gz"))
    last = [lax.axis_size(a) - 1 for a in ("gx", "gy", "gz")]
    flags = jnp.stack(
        [gx > 0, gx < last[0], gy > 0, gy < last[1], gz > 0, gz < last[2], gx, gx > 1, gx < last[0] - 1]
    ).astype(jnp.int32)

    eta, force, density, up, down = call(
        prepare, [(8, 32, 128), (3, 8, 32, 128), (8, 32, 128), (11, 32, 128), (11, 32, 128)], start=True
    )(flags, force, grain, density)
    x0 = exchange(up, down, "gx")
    up, down = call(pack_y0, [(27, 8, 128)] * 2)(flags, force, eta, density, *x0)
    y0 = exchange(up, down, "gy")
    up, down = call(pack_z0, [(2, 40, 128)] * 2)(flags, force, eta, density, *x0, *y0)
    z0 = exchange(up, down, "gz")
    vec, one = (3, NX0, NY0, NZ0), (NX0, NY0, NZ0)
    vech, oneh = (3, NX0, NY0, 128), (NX0, NY0, 128)
    b_own, eta_own, den_own, kap_own, coeffs = call(
        assemble0, [vech, oneh, oneh, oneh, (192, 128)], [(192, 128), (2, 48, 128)]
    )(flags, force, eta, density, *x0, *y0)
    b_far, den_far, v0, dinv0, wx0, wy0, wz0, own1, up, down, far_up, far_down = call(
        fine,
        [vech, oneh, vec, one, one, one, one, (5, 4, 16, 128)]
        + [(11, 16, 128)] * 2 + [(16, 128)] * 2,
        [oneh, oneh, one, vec, (192, 128), (3, 48, 128)],
    )(flags, b_own, eta_own, kap_own, coeffs, *z0)
    x1 = exchange(up, down, "gx")
    late_up, late_down = call(pack_late, [(8, 40, 128)] * 2)(flags, v0)
    x1, late_up, late_down = lax.optimization_barrier((x1, late_up, late_down))
    late = exchange(late_up, late_down, "gx")
    middle, up, down = call(
        pack_y1, [(UNITS1, 16, 128)] + [(UNITS1 + QUADS1, 8, 128)] * 2
    )(flags, own1, *x1)
    y1 = exchange(up, down, "gy")
    y1, late = lax.optimization_barrier((y1, late))
    up, down = call(pack_z1, [(40 * QUADS1 + 32 * OCTS1, 128)] * 2)(flags, middle, *y1)
    z1 = exchange(up, down, "gz")
    far = exchange(far_up, far_down, "gx", 2)
    z1, far = lax.optimization_barrier((z1, far))
    (rows,) = call(assemble1, [(5, NX1, NY1, 128)])(flags, middle, *y1)
    vec1, one1 = (3, NX1, NY1, 128), (NX1, NY1, 128)
    own2, up, down = call(
        coarse,
        [(5, 8, 128), (5, 16, 128), (5, 16, 128)],
        [vec1, one1, one1, one1, one1, one1, one1, one1, vec1, vec1, (240, 128), (5, 48, 128)],
    )(flags, rows, *z1)
    y2 = exchange(up, down, "gy")
    smooth = call(smooth1, [vec1, vec1, one1, one1, one1, one1], [one1, one1, one1, vec1])(flags, rows, *z1, *far)
    y2, smooth = lax.optimization_barrier((y2, smooth))
    (chunk,) = call(pack_x2, [(8, 168, 128)])(flags, own2, *y2)
    got = lax.all_to_all(chunk, "gx", 0, 0, tiled=True)
    vec2, one2 = (3, NX2, NY2, 128), (NX2, NY2, 128)
    vec3, one3 = (3, NX3, NY3, 128), (NX3, NY3, 128)
    velocity, new_density = call(
        finish,
        [(3, 8, 32, 128), (8, 32, 128)],
        [vec2, one2, one2, one2, one2, one2, one2, one2, vec2, vec2]
        + [vec3, one3, one3, one3, one3, one3, one3, one3, vec3, vec3]
        + [(576, 128), (576, 128), (6, 48, 128), (3, 20, 24, 128), vec1, vec1, vec, vec, (576, 256)],
        limit=32,
        final=True,
    )(flags, got, *late, *smooth, b_own, b_far, den_own, den_far, v0, dinv0, wx0, wy0, wz0)
    return velocity, new_density


def solution(mesh):
    return jax.shard_map(
        per_device,
        mesh=mesh,
        in_specs=(P(None, "gx", "gy", "gz"), P("gx", "gy", "gz"), P("gx", "gy", "gz")),
        out_specs=(P(None, "gx", "gy", "gz"), P("gx", "gy", "gz")),
        check_vma=False,
    )
```

```python
import jax
import jax.numpy as jnp
from jax import lax
from jax.experimental import pallas as pl
from jax.experimental.pallas import tpu as pltpu
from jax.sharding import PartitionSpec as P

OMEGA = 0.8
STEP_TIME = 0.1
DIFFUSION = 0.05
grain_table = [0.5 * 8.0 ** (entry / 15.0) for entry in range(16)]
F32 = jnp.float32
MIB = 1024 * 1024

W0 = (2, 2, 2, 3, 2)
OFF0 = (0, 2, 4, 6, 9)
Z0 = (2, 2, 2, 3, 2)
ZOFF0 = (3, 5, 7, 0, 9)
ZSLOT0 = 12
NX0, NY0, NZ0 = 14, 48, 256
PAIRS0 = ((0, 1), (2, 3), (4, 5), (6, 7), (8, 13), (9, 12))
LATE = ((0, 3), (0, 2), (0, 1), (1, 2), (1, 1), (2, 2), (2, 1))
W1 = (4, 4, 4, 5, 5)
OFF1 = (0, 4, 8, 12, 17)
FAR1 = ((0, -5), (0, 8), (3, -6), (3, 9))
NX1, NY1 = 16, 40
NEAR1 = (2, 2, 2, 3, 2)
PIECES1 = [(f, x) for f in range(5) for x in range(-NEAR1[f], 4 + NEAR1[f])]
WIDE1 = len(PIECES1) // 2
PIECES1 += [(f, x) for f in range(5) for x in range(-W1[f], 4 + W1[f]) if (f, x) not in PIECES1]
UNITS1 = len(PIECES1) // 2
QUADS1 = (WIDE1 + 1) // 2
OCTS1 = (UNITS1 - WIDE1 + 7) // 8
NX2, NY2 = 10, 40
NX3, NY3 = 6, 24


def iota(shape, dim):
    return lax.broadcasted_iota(jnp.int32, shape, dim)


def back(value, axis):
    if axis == 1 and value.shape[1] == 256:
        return jnp.concatenate([value[:, 128:256], pltpu.roll(value[:, 0:128], 127, 1)], axis=1)
    return pltpu.roll(value, value.shape[axis] - 1, axis)


def forth(value, axis):
    if axis == 1 and value.shape[1] == 256:
        return jnp.concatenate([pltpu.roll(value[:, 128:256], 1, 1), value[:, 0:128]], axis=1)
    return pltpu.roll(value, 1, axis)


def turn(value, shift, axis):
    shift = shift % value.shape[axis]
    return value if shift == 0 else pltpu.roll(value, shift, axis)


def call(body, outs, scratch=(), limit=12, start=False, final=False):
    def run(flags, *operands):
        if not final:
            shapes = [pltpu.VMEM(s, F32) for s in outs]
        else:
            shapes = [jax.ShapeDtypeStruct(s, F32) for s in outs]
        return pl.pallas_call(
            body,
            out_shape=shapes,
            in_specs=[pl.BlockSpec(memory_space=pltpu.SMEM)]
            + [pl.BlockSpec(memory_space=pltpu.VMEM)] * len(operands),
            out_specs=[pl.BlockSpec(memory_space=pltpu.VMEM)] * len(outs),
            scratch_shapes=[pltpu.VMEM(s, F32) for s in scratch],
            compiler_params=pltpu.CompilerParams(vmem_limit_bytes=limit * MIB),
        )(flags, *[pltpu.with_memory_space_constraint(o, pltpu.HBM if start else pltpu.VMEM) for o in operands])

    return run


def flag(flags, index):
    return flags[index].astype(F32)


def weighted(v, w, c, x, xp, xm):
    wx, wy, wz = w
    here = v[c, x]
    total = wx[x] * v[c, xp] + wx[xm] * v[c, xm]
    a = wy[x]
    total = total + a * back(here, 0) + forth(a * here, 0)
    a = wz[x]
    total = total + a * back(here, 1) + forth(a * here, 1)
    return here, total


def loop(count, body):
    for i in range(count):
        body(i)


def planes(lo, hi, n, body):
    for k in range(lo, hi):
        body(k % n, (k + 1) % n, (k - 1) % n)


def sweep(dst, src, b, w, dinv, lo, hi, n):
    def body(x, xp, xm):
        scale = dinv[x]
        for c in range(3):
            here, total = weighted(src, w, c, x, xp, xm)
            dst[c, x] = 0.2 * here + scale * (b[c, x] + total)

    planes(lo, hi, n, body)


def sweep_wider(dst, src, b, w, dinv, lo, hi, n):
    sweep(dst, src, b, w, dinv, lo + 1, hi - 1, n)
    for x in (lo % n, (hi - 1) % n):
        here, total = weighted(src, w, 0, x, (x + 1) % n, (x - 1) % n)
        dst[0, x] = 0.2 * here + dinv[x] * (b[0, x] + total)


def weights(eta, w, factor, lo, hi, n):
    wx, wy, wz = w
    half = 0.5 * factor

    def body(x, xp, xm):
        here = eta[x]
        wx[x] = half * (here + eta[xp])
        wy[x] = half * (here + back(here, 0))
        wz[x] = half * (here + back(here, 1))

    planes(lo, hi, n, body)


def diagonals(kap, w, dg, dinv, v, b, lo, hi, n):
    wx, wy, wz = w

    def body(x, xp, xm):
        k, a, g = kap[x], wy[x], wz[x]
        d = k + (wx[x] + wx[xm]) + (a + forth(a, 0)) + (g + forth(g, 1))
        inside = k > 0.0
        scale = jnp.where(inside, OMEGA / jnp.where(inside, d, 1.0), 0.0)
        dg[x] = d
        dinv[x] = scale
        for c in range(3):
            v[c, x] = scale * b[c, x]

    planes(lo, hi, n, body)


def rest(v, b, w, dg, c, x, xp, xm):
    here, total = weighted(v, w, c, x, xp, xm)
    return b[c, x] - dg[x] * here + total


def mean_matrix(source):
    k, j = iota((128, 128), 0), iota((128, 128), 1)
    return jnp.where((k >> 1) == source(j), 0.125, 0.0).astype(F32)


def repeat_matrix(source, out=128):
    k, j = iota((128, out), 0), iota((128, out), 1)
    return jnp.where(k == source(j), 1.0, 0.0).astype(F32)


def mean2(j):
    return (j + 48) & 63


def mean3(j):
    return jnp.where((j & 63) < 32, ((j >> 6) << 5) + (j & 63), -1)


def repeat2(j):
    return (j & 64) + ((j & 63) >> 1)


def repeat1(j):
    return ((j >> 1) + 16) & 63


def split0(j):
    return ((j & 63) << 1) + (j >> 6)


def merge0(j):
    return (j >> 1) + ((j & 1) << 6)


def dot(a, b):
    b = b.astype(jnp.bfloat16)
    high = a.astype(jnp.bfloat16)
    rest_of = a - high.astype(F32)
    middle = rest_of.astype(jnp.bfloat16)
    low = (rest_of - middle.astype(F32)).astype(jnp.bfloat16)
    product = lambda piece: jnp.dot(piece, b, preferred_element_type=F32)
    return product(high) + (product(middle) + product(low))


def row_pairs(tmp, value):
    rows = value.shape[0]
    tmp[pl.ds(0, rows), :] = value
    return tmp[pl.ds(0, rows // 2, stride=2), :] + tmp[pl.ds(1, rows // 2, stride=2), :]


def prepare(flags, force, grain, dens, eta, force_kept, dens_kept, up, down, lines):
    for x in range(8):
        ids = grain[x]
        looked = jnp.full(ids.shape, grain_table[0], F32)
        for entry in range(1, 16):
            looked = jnp.where(ids == entry, grain_table[entry], looked)
        d = dens[x]
        lines[pl.ds(768 + 32 * x, 32), :] = looked * d * d * d
        lines[pl.ds(1024 + 32 * x, 32), :] = d
        for c in range(3):
            lines[pl.ds(256 * c + 32 * x, 32), :] = force[c, x]
    lines[...] = dot(lines[...], repeat_matrix(split0))
    for x in range(8):
        eta[x] = lines[pl.ds(768 + 32 * x, 32), :]
        dens_kept[x] = lines[pl.ds(1024 + 32 * x, 32), :]
        for c in range(3):
            force_kept[c, x] = lines[pl.ds(256 * c + 32 * x, 32), :]
    force, dens = force_kept, dens_kept
    for f in range(5):
        for k in range(W0[f]):
            for out, x in ((up, 8 - W0[f] + k), (down, k)):
                out[OFF0[f] + k] = force[f, x] if f < 3 else (eta if f == 3 else dens)[x]


def plane0(flags, own, f, x, rows):
    force, eta, dens, low, high = own
    if 0 <= x < 8:
        return force[f, x, rows] if f < 3 else (eta if f == 3 else dens)[x, rows]
    away = x - 8 if x >= 8 else -x - 1
    if away >= W0[f]:
        return jnp.zeros((rows.stop - rows.start, 128), F32)
    if x >= 8:
        return high[OFF0[f] + away, rows] * flag(flags, 1)
    return low[OFF0[f] + W0[f] - 1 - away, rows] * flag(flags, 0)


def rel0(x):
    return x if x < 11 else x - NX0


YT0 = (0, 5, 10, 20, 15)
FIFTH0 = 26


def halo0(f, x):
    for q, pair in enumerate(PAIRS0[:6 if f == 3 else 5]):
        if x in pair:
            return q, pair.index(x)
    return None


def pack_y0(flags, force, eta, dens, low, high, up, down):
    own = (force, eta, dens, low, high)
    sub = iota((8, 128), 0)
    for f in range(5):
        for q, pair in enumerate(PAIRS0[:6 if f == 3 else 5]):
            a, b = (rel0(x) for x in pair)
            top, bottom = slice(24, 32), slice(0, 8)
            up[YT0[f] + q] = jnp.where(
                sub < 4, turn(plane0(flags, own, f, a, top), 4, 0), plane0(flags, own, f, b, top)
            )
            down[YT0[f] + q] = jnp.where(
                sub < 4, plane0(flags, own, f, a, bottom), turn(plane0(flags, own, f, b, bottom), 4, 0)
            )
    hi = lo = jnp.zeros((8, 128), F32)
    for x in range(8):
        hi = jnp.where(sub == x, turn(eta[x, 24:32], x - 3, 0), hi)
        lo = jnp.where(sub == x, turn(eta[x, 0:8], x - 4, 0), lo)
    up[FIFTH0], down[FIFTH0] = hi, lo


def rows0(flags, own, lowy, highy, f, x):
    sub = iota((8, 128), 0)
    middle = plane0(flags, own, f, rel0(x), slice(0, 32))
    if halo0(f, x) is None:
        return jnp.concatenate([middle, jnp.zeros((16, 128), F32)], axis=0)
    q, second = halo0(f, x)
    high, low = highy[YT0[f] + q], lowy[YT0[f] + q]
    if second:
        high = turn(high, 4, 0)
    else:
        low = turn(low, 4, 0)
    if f == 3 and x < 8:
        high = jnp.where(sub == 4, turn(highy[FIFTH0], 4 - x, 0), high)
        low = jnp.where(sub == 3, turn(lowy[FIFTH0], 3 - x, 0), low)
    return jnp.concatenate([middle, high * flag(flags, 3), low * flag(flags, 2)], axis=0)


def slot0(f, x):
    if x in PAIRS0[5]:
        return PAIRS0[5].index(x), 5 * ZSLOT0 + 3
    order = x if x < 9 else 9
    return order // 5, ZSLOT0 * (order % 5) + 3 + ZOFF0[f]


def pack_z0(flags, force, eta, dens, lowx, highx, lowy, highy, up, down):
    own = (force, eta, dens, lowx, highx)
    lane, sub = iota((40, 128), 1), iota((8, 128), 0)
    for g in range(2):
        hi = lo = jnp.zeros((40, 128), F32)
        for f in range(5):
            for x in range(NX0):
                if halo0(f, x) is None or slot0(f, x)[0] != g:
                    continue
                at, w = slot0(f, x)[1], Z0[f]
                value = rows0(flags, own, lowy, highy, f, x)
                mix = jnp.where(sub < 4, value[32:40], value[40:48])
                value = turn(jnp.concatenate([value[0:32], mix], axis=0), at, 1)
                hi = jnp.where(((lane + (128 + w - at)) & 63) < w, value, hi)
                lo = jnp.where(((lane + (128 - at)) & 63) < w, value, lo)
        up[g], down[g] = hi, lo


def assemble0(flags, force, eta, dens, lowx, highx, lowy, highy, even, odd, coeffs, kap, tmp):
    own = (force, eta, dens, lowx, highx)
    for x in range(NX0):
        for f in range(5):
            value = rows0(flags, own, lowy, highy, f, x)
            even[f, x] = value
            odd[f, x] = pltpu.roll(value, 64, 1)
            if f == 4:
                kap[x] = jnp.where(value > 0.0, 0.02 + 0.08 * value, 0.0)
    for i in range(-1, 5):
        x = (2 * i) % NX0
        for k, field in enumerate((even.at[3], kap)):
            r = row_pairs(tmp.at[k], field[x, 0:32] + field[x + 1, 0:32])
            coeffs[pl.ds((6 * k + i + 1) * 16, 16), :] = 0.125 * (r + pltpu.roll(r, 64, 1))


def fine(flags, even, odd, coeffs, lowz, highz,
         b, den, v, dinv, wx, wy, wz, own1, up, down, far_up, far_down,
         eta0, kap, dg, v0, pairs, tmp):
    lane, own = iota((40, 128), 1), iota((NY0, 128), 1) < 64
    fhi, flo = flag(flags, 5), flag(flags, 4)
    packets = [(highz[g] * fhi, lowz[g] * flo) for g in range(2)]
    for x in range(NX0):
        for f in range(5):
            if halo0(f, x) is None:
                far = far_even = jnp.zeros((NY0, 128), F32)
            else:
                (g, at), w = slot0(f, x), Z0[f]
                both = jnp.where(((lane + (128 - at)) & 63) < w, *packets[g])
                far, far_even = turn(both, -at, 1), turn(both, 64 - at, 1)
                far = jnp.concatenate([far, far[32:40]], axis=0)
                far_even = jnp.concatenate([far_even, far_even[32:40]], axis=0)
            parts = (jnp.where(own, even[f, x], far_even), jnp.where(own, odd[f, x], far))
            for half, value in enumerate(parts):
                lanes = slice(128 * half, 128 * half + 128)
                if f < 3:
                    b[f, x, :, lanes] = value
                elif f == 3:
                    eta0[x, :, lanes] = value
                else:
                    den[x, :, lanes] = value
                    kap[x, :, lanes] = jnp.where(value > 0.0, 0.02 + 0.08 * value, 0.0)
    w = (wx, wy, wz)
    weights(eta0, w, 1.0, -3, 11, NX0)
    diagonals(kap, w, dg, dinv, v0, b, -2, 10, NX0)
    sweep(v, v0, b, w, dinv, -1, 9, NX0)

    def blocks(i):
        x0 = 2 * i
        xm, xp, xq = (x0 + NX0 - 1) % NX0, x0 + 1, x0 + 2
        for c in range(3):
            r = rest(v, b, w, dg, c, x0, xp, xm) + rest(v, b, w, dg, c, xp, xq, x0)
            at = (c * 4 + i) * 16
            r = 0.125 * row_pairs(tmp.at[c], r[0:32, 0:128] + r[0:32, 128:256])
            pairs[pl.ds(at, 16), :] = jnp.where(iota((16, 128), 1) < 64, r, pltpu.roll(r, 64, 1))

    loop(4, blocks)

    def piece(f, i):
        if f < 3:
            return pairs[pl.ds((f * 4 + i) * 16, 16), :]
        return coeffs[pl.ds((6 * (f - 3) + i + 1) * 16, 16), :]

    half = iota((16, 128), 1) < 64
    ups = [(f, i) for f in range(5) for i in range(4 - W1[f], 4)]
    downs = [(f, i) for f in range(5) for i in range(0, W1[f])]
    for k in range(11):
        up[k] = jnp.where(half, piece(*ups[2 * k]), piece(*ups[2 * k + 1]))
        down[k] = jnp.where(half, piece(*downs[2 * k]), piece(*downs[2 * k + 1]))
    far_up[...] = jnp.where(half, piece(0, 3), piece(3, 2))
    far_down[...] = jnp.where(half, piece(0, 0), piece(3, 1))
    for f in range(5):
        for i in range(4):
            own1[f, i] = piece(f, i)


def pack_late(flags, v, late_up, late_down):
    sub, lane = iota((8, 128), 0), iota((40, 128), 1)
    for out, top in ((late_up, True), (late_down, False)):
        edge = jnp.zeros((40, 128), F32)
        for p, (c, away) in enumerate(LATE):
            x = 8 - away if top else away - 1
            parts = []
            for half in range(2):
                value = v[c, x, :, 128 * half:128 * half + 128]
                mix = jnp.where(sub < 4, value[32:40], value[40:48])
                parts.append(jnp.concatenate([value[0:32], mix], axis=0))
            even, odd = parts
            out[p] = jnp.where(lane < 64, even, pltpu.roll(odd, 64, 1))
            value = jnp.where(lane < 64, pltpu.roll(even, 64, 1), odd)
            edge = jnp.where(((lane & 63) >> 2) == p, turn(value, 4 * p + 2, 1), edge)
        out[7] = edge


def plane1(flags, own1, lowx, highx, f, x, half):
    if 0 <= x < 4:
        return own1[f, x]
    away = x - 4 if x >= 4 else -x - 1
    if x >= 4:
        at = OFF1[f] + away
        source, there = highx[at // 2], flag(flags, 1)
    else:
        at = OFF1[f] + W1[f] - 1 - away
        source, there = lowx[at // 2], flag(flags, 0)
    return turn(source, 64 * ((at + half) % 2), 1) * there


def pack_y1(flags, own1, lowx, highx, middle, up, down):
    sub = iota((8, 128), 0)
    left = iota((16, 128), 1) < 64
    sent = (flags, own1, lowx, highx)
    hi = lo = None
    for u in range(UNITS1):
        value = jnp.where(left, plane1(*sent, *PIECES1[2 * u], 0), plane1(*sent, *PIECES1[2 * u + 1], 1))
        middle[u] = value
        up[u], down[u] = value[8:16], value[0:8]
        if u < WIDE1:
            if u % 2 == 0:
                hi, lo = turn(value[0:8], 4, 0), value[8:16]
            else:
                hi, lo = jnp.where(sub < 4, hi, value[0:8]), jnp.where(sub < 4, lo, turn(value[8:16], 4, 0))
            up[UNITS1 + u // 2], down[UNITS1 + u // 2] = hi, lo


def unit1(flags, middle, lowy, highy, u):
    sub = iota((8, 128), 0)
    fhi, flo = flag(flags, 3), flag(flags, 2)
    if u < WIDE1:
        high, low = highy[UNITS1 + u // 2], lowy[UNITS1 + u // 2]
        high, low = (turn(high, 4, 0), low) if u % 2 else (high, turn(low, 4, 0))
        mix = jnp.where(sub < 4, high * fhi, low * flo)
    else:
        mix = jnp.zeros((8, 128), F32)
    value = jnp.concatenate([middle[u], highy[u] * fhi, mix, lowy[u] * flo], axis=0)
    return value


def assemble1(flags, middle, lowy, highy, rows):
    for u in range(UNITS1):
        value = unit1(flags, middle, lowy, highy, u)
        for h in range(2):
            f, x = PIECES1[2 * u + h]
            rows[f, x % NX1] = turn(value, 64 * h, 1)


def pack_z1(flags, middle, lowy, highy, up, down):
    lane = iota((40, 128), 1)

    def unit(u):
        return unit1(flags, middle, lowy, highy, u)

    odd = ((lane >> 5) & 1) == 1
    for g in range(QUADS1):
        a = unit(2 * g)
        b = unit(2 * g + 1) if 2 * g + 1 < WIDE1 else a
        b = turn(b, 32, 1)
        up[pl.ds(40 * g, 40), :] = jnp.where(odd, a, b)
        down[pl.ds(40 * g, 40), :] = jnp.where(odd, b, a)
    slot = (iota((32, 128), 1) >> 3) & 7
    for q in range(OCTS1):
        hi = lo = jnp.zeros((32, 128), F32)
        for j in range(8):
            u = WIDE1 + 8 * q + j
            if u < UNITS1:
                value = unit(u)
                value = jnp.concatenate([value[0:24], value[32:40]], axis=0)
                hi = jnp.where(slot == j, turn(value, 8 * j - 56, 1), hi)
                lo = jnp.where(slot == j, turn(value, 8 * j, 1), lo)
        at = 40 * QUADS1 + 32 * q
        up[pl.ds(at, 32), :], down[pl.ds(at, 32), :] = hi, lo


def all_rows1(value):
    return jnp.concatenate([value[0:24], value[16:32]], axis=0)


def load1(flags, rows, lowz, highz, b, eta, kap, count):
    lane = iota((NY1, 128), 1)
    slot = iota((40, 128), 1) >> 5
    fhi, flo = flag(flags, 5), flag(flags, 4)
    for p, (f, x) in enumerate(PIECES1[:count]):
        u, h = p // 2, p % 2
        if u < WIDE1:
            place = pl.ds(40 * (u // 2), 40)
            part = 2 * h + u % 2
            both = jnp.where(slot == part, highz[place, :] * fhi, lowz[place, :] * flo)
            beyond = turn(both, 64 - 32 * part, 1)
        else:
            q, j = (u - WIDE1) // 8, (u - WIDE1) % 8
            place = pl.ds(40 * QUADS1 + 32 * q, 32)
            high = all_rows1(turn(highz[place, :] * fhi, 64 - 8 * j - 64 * h, 1))
            low = all_rows1(turn(lowz[place, :] * flo, 120 - 8 * j - 64 * h, 1))
            beyond = jnp.where(lane < 96, high, low)
        value = jnp.where(lane < 64, rows[f, x % NX1], beyond)
        if f < 3:
            b[f, x % NX1] = value
        else:
            (eta if f == 3 else kap)[x % NX1] = value

def coarse(flags, rows, lowz, highz, own2, up, down, b, eta, kap, wx, wy, wz, dg, dinv, v0, v, pairs, tmp):
    load1(flags, rows, lowz, highz, b, eta, kap, 2 * WIDE1)
    w = (wx, wy, wz)
    weights(eta, w, 0.25, -3, 7, NX1)
    diagonals(kap, w, dg, dinv, v0, b, -2, 6, NX1)
    sweep(v, v0, b, w, dinv, -1, 5, NX1)

    def blocks(i):
        x0 = 2 * i
        for c in range(3):
            r = rest(v, b, w, dg, c, x0, x0 + 1, (x0 + NX1 - 1) % NX1)
            r = r + rest(v, b, w, dg, c, x0 + 1, x0 + 2, x0)
            at = (c * 2 + i) * 24
            pairs[pl.ds(at, 20), :] = row_pairs(tmp.at[c], r)
        at = (6 + i) * 24
        pairs[pl.ds(at, 20), :] = row_pairs(tmp.at[3], eta[x0] + eta[x0 + 1])
        at = (8 + i) * 24
        pairs[pl.ds(at, 20), :] = row_pairs(tmp.at[4], kap[x0] + kap[x0 + 1])

    loop(2, blocks)
    pairs[...] = dot(pairs[...], mean_matrix(mean2))
    left = iota((8, 128), 1) < 64
    for f in range(5):
        own, high, low = (
            jnp.where(left, pairs[pl.ds(48 * f + at, 8), :], pairs[pl.ds(48 * f + 24 + at, 8), :])
            for at in (0, 8, 12)
        )
        own2[f] = own
        up[f, 0:8], up[f, 8:16] = low, own
        down[f, 0:8], down[f, 8:16] = own, high


def smooth1(flags, rows, lowz, highz, far_low, far_high, b, v, dinv, wx, wy, wz, eta, kap, dg, v0):
    none = jnp.zeros((NY1, 128), F32)
    for x in (-6, 9):
        kap[x % NX1] = none
    for x in (-5, 8):
        for c in (1, 2):
            b[c, x % NX1] = none
    for f, x in FAR1:
        source = far_high[...] * flag(flags, 8) if x > 0 else far_low[...] * flag(flags, 7)
        value = jnp.concatenate([turn(source, 64 * int(f == 3), 1), none[0:24]], axis=0)
        if f == 0:
            b[0, x % NX1] = value
        else:
            eta[x % NX1] = value
    load1(flags, rows, lowz, highz, b, eta, kap, len(PIECES1))
    w = (wx, wy, wz)
    weights(eta, w, 0.25, -6, 10, NX1)
    diagonals(kap, w, dg, dinv, v0, b, -5, 9, NX1)
    sweep(v, v0, b, w, dinv, -4, 8, NX1)


def pack_x2(flags, own2, lowy, highy, out):
    sub = iota((8, 128), 0)
    for f in range(5):
        near, far = highy[f, 0:8] * flag(flags, 3), highy[f, 8:16] * flag(flags, 3)
        far_low, near_low = lowy[f, 0:8] * flag(flags, 2), lowy[f, 8:16] * flag(flags, 2)
        value = jnp.concatenate([own2[f], near, jnp.where(sub < 4, far, far_low), near_low], axis=0)
        for d in range(8):
            out[d, 32 * f:32 * f + 32] = value
        if f == 3:
            for d in range(8):
                out[d, 160:168] = jnp.where(sub == 4, far, far_low)


def finish(flags, got, late_low, late_high, b1, v1, dinv1, wx1, wy1, wz1, b0, den, v0, dinv0, wx0, wy0, wz0,
           velocity, new_density,
           b2, eta2, kap2, dg2, dinv2, wx2, wy2, wz2, va2, vb2,
           b3, eta3, kap3, dg3, dinv3, wx3, wy3, wz3, va3, vb3,
           pairs, spread, tmp, e2, va1, vb1, va0, vb0, lines):
    sub = iota((8, 128), 0)
    left2, left3 = iota((NY2, 128), 1) < 64, iota((NY3, 128), 1) < 64
    for f in range(5):
        two = []
        for d in range(8):
            own, near = got[d, 32 * f:32 * f + 8], got[d, 32 * f + 8:32 * f + 16]
            mix, low = got[d, 32 * f + 16:32 * f + 24], got[d, 32 * f + 24:32 * f + 32]
            far, far_low = mix, mix
            if f == 3:
                extra = got[d, 160:168]
                far, far_low = jnp.where(sub == 4, extra, mix), jnp.where(sub == 3, extra, mix)
            two.append(jnp.concatenate([far_low, low, own, near, far], axis=0))
        for d in range(4):
            even = jnp.where(left2, two[d], pltpu.roll(two[d + 4], 64, 1))
            odd = jnp.where(left2, pltpu.roll(two[d], 64, 1), two[d + 4])
            if f < 3:
                b2[f, 2 * d], b2[f, 2 * d + 1] = even, odd
            else:
                out = eta2 if f == 3 else kap2
                out[2 * d], out[2 * d + 1] = even, odd

    def ends(ref, n, left, lead=()):
        first_plane, last_plane = ref[lead + (0,)], ref[lead + (n - 1,)]
        ref[lead + (n,)] = jnp.where(left, pltpu.roll(first_plane, 64, 1), 0.0)
        ref[lead + (n + 1,)] = jnp.where(left, 0.0, pltpu.roll(last_plane, 64, 1))

    def ends2(ref):
        for c in range(3):
            ends(ref, 8, left2, (c,))

    def ends3(ref):
        for c in range(3):
            ends(ref, 4, left3, (c,))

    w2 = (wx2, wy2, wz2)
    ends(eta2, 8, left2)
    weights(eta2, w2, 0.0625, -1, 8, NX2)
    diagonals(kap2, w2, dg2, dinv2, va2, b2, 0, 8, NX2)
    ends2(va2)
    sweep(vb2, va2, b2, w2, dinv2, 0, 8, NX2)
    ends2(vb2)

    def blocks(i):
        x0 = 2 * i
        xm, xp, xq = (x0 + NX2 - 1) % NX2, x0 + 1, x0 + 2
        for c in range(3):
            r = rest(vb2, b2, w2, dg2, c, x0, xp, xm) + rest(vb2, b2, w2, dg2, c, xp, xq, x0)
            pairs[pl.ds((c * 4 + i) * 24, 20), :] = row_pairs(tmp.at[c], r)
        pairs[pl.ds((12 + i) * 24, 20), :] = row_pairs(tmp.at[3], eta2[x0] + eta2[xp])
        pairs[pl.ds((16 + i) * 24, 20), :] = row_pairs(tmp.at[4], kap2[x0] + kap2[xp])

    loop(4, blocks)
    pairs[pl.ds(0, 480), :] = dot(pairs[pl.ds(0, 480), :], mean_matrix(mean3))
    for i in range(4):
        for c in range(3):
            b3[c, i] = pairs[pl.ds((c * 4 + i) * 24, 24), :]
        eta3[i] = pairs[pl.ds((12 + i) * 24, 24), :]
        kap3[i] = pairs[pl.ds((16 + i) * 24, 24), :]
    w3 = (wx3, wy3, wz3)
    ends(eta3, 4, left3)
    weights(eta3, w3, 0.015625, -1, 4, NX3)
    diagonals(kap3, w3, dg3, dinv3, va3, b3, 0, 4, NX3)
    ends3(va3)
    sweep(vb3, va3, b3, w3, dinv3, 0, 4, NX3)
    ends3(vb3)
    sweep(va3, vb3, b3, w3, dinv3, 0, 4, NX3)
    ends3(va3)
    sweep(vb3, va3, b3, w3, dinv3, 0, 4, NX3)

    for c in range(3):
        for i in range(4):
            pairs[pl.ds((c * 4 + i) * 24, 24), :] = vb3[c, i]
    spread[pl.ds(0, 288), :] = dot(pairs[pl.ds(0, 288), :], repeat_matrix(repeat2))

    def rise2(i):
        for c in range(3):
            e = spread[pl.ds((c * 4 + i) * 24, 24), :]
            tmp[c, pl.ds(0, 24, stride=2), :] = e
            tmp[c, pl.ds(1, 24, stride=2), :] = e
            e = tmp[c, 0:40]
            vb2[c, 2 * i] = vb2[c, 2 * i] + e
            vb2[c, 2 * i + 1] = vb2[c, 2 * i + 1] + e

    loop(4, rise2)
    ends2(vb2)
    sweep(va2, vb2, b2, w2, dinv2, 0, 8, NX2)
    ends2(va2)
    sweep(vb2, va2, b2, w2, dinv2, 0, 8, NX2)

    none = jnp.zeros((24, 128), F32)
    for c in range(3):
        for x in (0, 1, 18, 19):
            e2[c, x] = none
        for x in range(8):
            value = jnp.concatenate([vb2[c, x, 16:32], turn(vb2[c, x, 8:16], 4, 0)], axis=0)
            e2[c, 2 + x] = value
            e2[c, 10 + x] = pltpu.roll(value, 64, 1)
    start = 2 * flags[6]
    for c in range(3):
        for k in range(6):
            pairs[pl.ds((c * 6 + k) * 24, 24), :] = e2[c, start + k]
    spread[pl.ds(0, 432), :] = dot(pairs[pl.ds(0, 432), :], repeat_matrix(repeat1))

    def rise1(k):
        x = (2 * k - 4 + NX1) % NX1
        for c in range(3):
            e = spread[pl.ds((c * 6 + k) * 24, 24), :]
            tmp[c, pl.ds(0, 24, stride=2), :] = e
            tmp[c, pl.ds(1, 24, stride=2), :] = e
            e = tmp[c, 0:40]
            va1[c, x] = v1[c, x] + e
            va1[c, x + 1] = v1[c, x + 1] + e

    loop(6, rise1)
    w1 = (wx1, wy1, wz1)
    sweep_wider(vb1, va1, b1, w1, dinv1, -3, 7, NX1)
    sweep_wider(va1, vb1, b1, w1, dinv1, -2, 6, NX1)

    for c in range(3):
        for i in range(-2, 6):
            at = (c * 8 + i + 2) * 24
            x = i % NX1
            pairs[pl.ds(at, 16), :] = va1[c, x, 0:16]
            pairs[pl.ds(at + 16, 8), :] = jnp.where(sub < 4, va1[c, x, 16:24], va1[c, x, 32:40])

    def risen(c, i):
        here = tmp.at[c]
        e = pairs[pl.ds((c * 8 + i) * 24, 24), :]
        here[pl.ds(0, 24, stride=2), :] = e
        here[pl.ds(1, 24, stride=2), :] = e
        e = here[...]
        return jnp.concatenate([e, e], axis=1)

    def rise0(i):
        for c in range(3):
            e = risen(c, i + 2)
            va0[c, 2 * i] = v0[c, 2 * i] + e
            va0[c, 2 * i + 1] = v0[c, 2 * i + 1] + e

    loop(4, rise0)
    lane = iota((40, 128), 1)
    for high, late in ((True, late_high), (False, late_low)):
        there = flag(flags, 1 if high else 0)
        for p, (c, away) in enumerate(LATE):
            x = 7 + away if high else NX0 - away
            own, edge = late[p], late[7]
            even = jnp.where(lane < 64, own, turn(edge, 62 - 4 * p, 1))
            odd = jnp.where(lane < 64, pltpu.roll(own, 64, 1), turn(edge, -4 * p - 2, 1))
            value = jnp.concatenate([even, odd], axis=1) * there
            value = jnp.concatenate([value, value[32:40]], axis=0)
            va0[c, x] = value + risen(c, (5 + (away + 1) // 2) if high else 2 - (away + 1) // 2)
    w0 = (wx0, wy0, wz0)
    first_lanes = iota((32, 128), 1) < 64

    def keep(at, x, value):
        at = 256 * at + 32 * x
        lines[pl.ds(at, 32), :] = jnp.where(
            first_lanes, value[0:32, 0:128], pltpu.roll(value[0:32, 128:256], 64, 1)
        )
    sweep_wider(vb0, va0, b0, w0, dinv0, -2, 10, NX0)
    sweep_wider(va0, vb0, b0, w0, dinv0, -1, 9, NX0)

    def advect(x):
        xm, xp = (x + NX0 - 1) % NX0, x + 1
        d = den[x]
        change = jnp.zeros_like(d)
        spreading = -6.0 * d
        for axis in range(3):
            u = va0[axis, x]
            if axis == 0:
                u_up, u_lo, d_up, d_lo = va0[0, xp], va0[0, xm], den[xp], den[xm]
            else:
                u_up, u_lo = back(u, axis - 1), forth(u, axis - 1)
                d_up, d_lo = back(d, axis - 1), forth(d, axis - 1)
            hi, lo = 0.5 * (u + u_up), 0.5 * (u_lo + u)
            change = change + (jnp.maximum(hi, 0.0) * d + jnp.minimum(hi, 0.0) * d_up)
            change = change - (jnp.maximum(lo, 0.0) * d_lo + jnp.minimum(lo, 0.0) * d)
            spreading = spreading + (d_up + d_lo)
            keep(axis, x, u)
        out = d - STEP_TIME * change + STEP_TIME * DIFFUSION * spreading
        keep(3, x, out)

    loop(8, advect)
    lines[...] = dot(lines[...], repeat_matrix(merge0))
    for x in range(8):
        for c in range(3):
            velocity[c, x] = lines[pl.ds(256 * c + 32 * x, 32), :]
        new_density[x] = lines[pl.ds(768 + 32 * x, 32), :]


def exchange(up, down, axis, away=1):
    n = lax.axis_size(axis)
    low = lax.ppermute(up, axis, [(i, (i + away) % n) for i in range(n)])
    high = lax.ppermute(down, axis, [(i, (i - away) % n) for i in range(n)])
    return low, high


def per_device(force, grain, density):
    gx, gy, gz = (lax.axis_index(a) for a in ("gx", "gy", "gz"))
    last = [lax.axis_size(a) - 1 for a in ("gx", "gy", "gz")]
    flags = jnp.stack(
        [gx > 0, gx < last[0], gy > 0, gy < last[1], gz > 0, gz < last[2], gx, gx > 1, gx < last[0] - 1]
    ).astype(jnp.int32)

    eta, force, density, up, down = call(
        prepare, [(8, 32, 128), (3, 8, 32, 128), (8, 32, 128), (11, 32, 128), (11, 32, 128)],
        [(1280, 128)], start=True
    )(flags, force, grain, density)
    x0 = exchange(up, down, "gx")
    up, down = call(pack_y0, [(27, 8, 128)] * 2)(flags, force, eta, density, *x0)
    y0 = exchange(up, down, "gy")
    up, down = call(pack_z0, [(2, 40, 128)] * 2)(flags, force, eta, density, *x0, *y0)
    z0 = exchange(up, down, "gz")
    vec, one = (3, NX0, NY0, NZ0), (NX0, NY0, NZ0)
    oneh = (NX0, NY0, 128)
    even, odd, coeffs = call(
        assemble0, [(5, NX0, NY0, 128)] * 2 + [(192, 128)], [oneh, (2, 48, 128)]
    )(flags, force, eta, density, *x0, *y0)
    b0, den, v0, dinv0, wx0, wy0, wz0, own1, up, down, far_up, far_down = call(
        fine,
        [vec, one, vec, one, one, one, one, (5, 4, 16, 128)] + [(11, 16, 128)] * 2 + [(16, 128)] * 2,
        [one, one, one, vec, (192, 128), (3, 48, 128)],
    )(flags, even, odd, coeffs, *z0)
    x1 = exchange(up, down, "gx")
    late_up, late_down = call(pack_late, [(8, 40, 128)] * 2)(flags, v0)
    x1, late_up, late_down = lax.optimization_barrier((x1, late_up, late_down))
    late = exchange(late_up, late_down, "gx")
    middle, up, down = call(
        pack_y1, [(UNITS1, 16, 128)] + [(UNITS1 + QUADS1, 8, 128)] * 2
    )(flags, own1, *x1)
    y1 = exchange(up, down, "gy")
    y1, late = lax.optimization_barrier((y1, late))
    up, down = call(pack_z1, [(40 * QUADS1 + 32 * OCTS1, 128)] * 2)(flags, middle, *y1)
    z1 = exchange(up, down, "gz")
    far = exchange(far_up, far_down, "gx", 2)
    z1, far = lax.optimization_barrier((z1, far))
    (rows,) = call(assemble1, [(5, NX1, NY1, 128)])(flags, middle, *y1)
    vec1, one1 = (3, NX1, NY1, 128), (NX1, NY1, 128)
    own2, up, down = call(
        coarse,
        [(5, 8, 128), (5, 16, 128), (5, 16, 128)],
        [vec1, one1, one1, one1, one1, one1, one1, one1, vec1, vec1, (240, 128), (5, 48, 128)],
    )(flags, rows, *z1)
    y2 = exchange(up, down, "gy")
    smooth = call(smooth1, [vec1, vec1, one1, one1, one1, one1], [one1, one1, one1, vec1])(flags, rows, *z1, *far)
    y2, smooth = lax.optimization_barrier((y2, smooth))
    (chunk,) = call(pack_x2, [(8, 168, 128)])(flags, own2, *y2)
    got = lax.all_to_all(chunk, "gx", 0, 0, tiled=True)
    vec2, one2 = (3, NX2, NY2, 128), (NX2, NY2, 128)
    vec3, one3 = (3, NX3, NY3, 128), (NX3, NY3, 128)
    velocity, new_density = call(
        finish,
        [(3, 8, 32, 128), (8, 32, 128)],
        [vec2, one2, one2, one2, one2, one2, one2, one2, vec2, vec2]
        + [vec3, one3, one3, one3, one3, one3, one3, one3, vec3, vec3]
        + [(576, 128), (576, 128), (6, 48, 128), (3, 20, 24, 128), vec1, vec1, vec, vec, (1024, 128)],
        limit=32,
        final=True,
    )(flags, got, *late, *smooth, b0, den, v0, dinv0, wx0, wy0, wz0)
    return velocity, new_density


def solution(mesh):
    return jax.shard_map(
        per_device,
        mesh=mesh,
        in_specs=(P(None, "gx", "gy", "gz"), P("gx", "gy", "gz"), P("gx", "gy", "gz")),
        out_specs=(P(None, "gx", "gy", "gz"), P("gx", "gy", "gz")),
        check_vma=False,
    )
```

```python
import jax
import jax.numpy as jnp
from jax import lax
from jax.experimental import pallas as pl
from jax.experimental.pallas import tpu as pltpu
from jax.sharding import PartitionSpec as P

OMEGA = 0.8
STEP_TIME = 0.1
DIFFUSION = 0.05
grain_table = [0.5 * 8.0 ** (entry / 15.0) for entry in range(16)]
F32 = jnp.float32
MIB = 1024 * 1024

W0 = (2, 2, 2, 3, 2)
OFF0 = (0, 2, 4, 6, 9)
Z0 = (2, 2, 2, 3, 2)
ZOFF0 = (3, 5, 7, 0, 9)
ZSLOT0 = 12
NX0, NY0, NZ0 = 14, 48, 256
PAIRS0 = ((0, 1), (2, 3), (4, 5), (6, 7), (8, 13), (9, 12))
LATE = ((0, 3), (0, 2), (0, 1), (1, 2), (1, 1), (2, 2), (2, 1))
W1 = (4, 4, 4, 5, 5)
OFF1 = (0, 4, 8, 12, 17)
FAR1 = ((0, -5), (0, 8), (3, -6), (3, 9))
NX1, NY1 = 16, 40
NEAR1 = (2, 2, 2, 3, 2)
PIECES1 = [(f, x) for f in range(5) for x in range(-NEAR1[f], 4 + NEAR1[f])]
WIDE1 = len(PIECES1) // 2
PIECES1 += [(f, x) for f in range(5) for x in range(-W1[f], 4 + W1[f]) if (f, x) not in PIECES1]
UNITS1 = len(PIECES1) // 2
QUADS1 = (WIDE1 + 1) // 2
OCTS1 = (UNITS1 - WIDE1 + 7) // 8
NX2, NY2 = 10, 40
NX3, NY3 = 6, 24


def iota(shape, dim):
    return lax.broadcasted_iota(jnp.int32, shape, dim)


def back(value, axis):
    if axis == 1 and value.shape[1] == 256:
        return jnp.concatenate([value[:, 128:256], pltpu.roll(value[:, 0:128], 127, 1)], axis=1)
    return pltpu.roll(value, value.shape[axis] - 1, axis)


def forth(value, axis):
    if axis == 1 and value.shape[1] == 256:
        return jnp.concatenate([pltpu.roll(value[:, 128:256], 1, 1), value[:, 0:128]], axis=1)
    return pltpu.roll(value, 1, axis)


def turn(value, shift, axis):
    shift = shift % value.shape[axis]
    return value if shift == 0 else pltpu.roll(value, shift, axis)


def call(body, outs, scratch=(), limit=12, start=False, final=False):
    def run(flags, *operands):
        if not final:
            shapes = [pltpu.VMEM(s, F32) for s in outs]
        else:
            shapes = [jax.ShapeDtypeStruct(s, F32) for s in outs]
        return pl.pallas_call(
            body,
            out_shape=shapes,
            in_specs=[pl.BlockSpec(memory_space=pltpu.SMEM)]
            + [pl.BlockSpec(memory_space=pltpu.VMEM)] * len(operands),
            out_specs=[pl.BlockSpec(memory_space=pltpu.VMEM)] * len(outs),
            scratch_shapes=[pltpu.VMEM(s, F32) for s in scratch],
            compiler_params=pltpu.CompilerParams(vmem_limit_bytes=limit * MIB),
        )(flags, *[pltpu.with_memory_space_constraint(o, pltpu.HBM if start else pltpu.VMEM) for o in operands])

    return run


def flag(flags, index):
    return flags[index].astype(F32)


def weighted(v, w, c, x, xp, xm):
    wx, wy, wz = w
    here = v[c, x]
    total = wx[x] * v[c, xp] + wx[xm] * v[c, xm]
    a = wy[x]
    total = total + a * back(here, 0) + forth(a * here, 0)
    a = wz[x]
    total = total + a * back(here, 1) + forth(a * here, 1)
    return here, total


def loop(count, body):
    for i in range(count):
        body(i)


def planes(lo, hi, n, body):
    for k in range(lo, hi):
        body(k % n, (k + 1) % n, (k - 1) % n)


def sweep(dst, src, b, w, dinv, lo, hi, n):
    def body(x, xp, xm):
        scale = dinv[x]
        for c in range(3):
            here, total = weighted(src, w, c, x, xp, xm)
            dst[c, x] = 0.2 * here + scale * (b[c, x] + total)

    planes(lo, hi, n, body)


def sweep_wider(dst, src, b, w, dinv, lo, hi, n):
    sweep(dst, src, b, w, dinv, lo + 1, hi - 1, n)
    for x in (lo % n, (hi - 1) % n):
        here, total = weighted(src, w, 0, x, (x + 1) % n, (x - 1) % n)
        dst[0, x] = 0.2 * here + dinv[x] * (b[0, x] + total)


def weights(eta, w, factor, lo, hi, n):
    wx, wy, wz = w
    half = 0.5 * factor

    def body(x, xp, xm):
        here = eta[x]
        wx[x] = half * (here + eta[xp])
        wy[x] = half * (here + back(here, 0))
        wz[x] = half * (here + back(here, 1))

    planes(lo, hi, n, body)


def diagonals(kap, w, dg, dinv, v, b, lo, hi, n):
    wx, wy, wz = w

    def body(x, xp, xm):
        k, a, g = kap[x], wy[x], wz[x]
        d = k + (wx[x] + wx[xm]) + (a + forth(a, 0)) + (g + forth(g, 1))
        inside = k > 0.0
        scale = jnp.where(inside, OMEGA / jnp.where(inside, d, 1.0), 0.0)
        dg[x] = d
        dinv[x] = scale
        for c in range(3):
            v[c, x] = scale * b[c, x]

    planes(lo, hi, n, body)


def rest(v, b, w, dg, c, x, xp, xm):
    here, total = weighted(v, w, c, x, xp, xm)
    return b[c, x] - dg[x] * here + total


def mean_matrix(source):
    k, j = iota((128, 128), 0), iota((128, 128), 1)
    return jnp.where((k >> 1) == source(j), 0.125, 0.0).astype(F32)


def repeat_matrix(source, out=128):
    k, j = iota((128, out), 0), iota((128, out), 1)
    return jnp.where(k == source(j), 1.0, 0.0).astype(F32)


def mean2(j):
    return (j + 48) & 63


def mean3(j):
    return jnp.where((j & 63) < 32, ((j >> 6) << 5) + (j & 63), -1)


def repeat2(j):
    return (j & 64) + ((j & 63) >> 1)


def repeat1(j):
    return ((j >> 1) + 16) & 63


def split0(j):
    return ((j & 63) << 1) + (j >> 6)


def merge0(j):
    return (j >> 1) + ((j & 1) << 6)


def dot(a, b):
    b = b.astype(jnp.bfloat16)
    high = a.astype(jnp.bfloat16)
    rest_of = a - high.astype(F32)
    middle = rest_of.astype(jnp.bfloat16)
    low = (rest_of - middle.astype(F32)).astype(jnp.bfloat16)
    product = lambda piece: jnp.dot(piece, b, preferred_element_type=F32)
    return product(high) + (product(middle) + product(low))


def row_pairs(tmp, value):
    rows = value.shape[0]
    tmp[pl.ds(0, rows), :] = value
    return tmp[pl.ds(0, rows // 2, stride=2), :] + tmp[pl.ds(1, rows // 2, stride=2), :]


def prepare(flags, force, grain, dens, eta, force_kept, dens_kept, up, down, lines):
    for x in range(8):
        ids = grain[x]
        looked = jnp.full(ids.shape, grain_table[0], F32)
        for entry in range(1, 16):
            looked = jnp.where(ids == entry, grain_table[entry], looked)
        d = dens[x]
        lines[pl.ds(768 + 32 * x, 32), :] = looked * d * d * d
        lines[pl.ds(1024 + 32 * x, 32), :] = d
        for c in range(3):
            lines[pl.ds(256 * c + 32 * x, 32), :] = force[c, x]
    lines[...] = dot(lines[...], repeat_matrix(split0))
    for x in range(8):
        eta[x] = lines[pl.ds(768 + 32 * x, 32), :]
        dens_kept[x] = lines[pl.ds(1024 + 32 * x, 32), :]
        for c in range(3):
            force_kept[c, x] = lines[pl.ds(256 * c + 32 * x, 32), :]
    force, dens = force_kept, dens_kept
    for f in range(5):
        for k in range(W0[f]):
            for out, x in ((up, 8 - W0[f] + k), (down, k)):
                out[OFF0[f] + k] = force[f, x] if f < 3 else (eta if f == 3 else dens)[x]


def plane0(flags, own, f, x, rows):
    force, eta, dens, low, high = own
    if 0 <= x < 8:
        return force[f, x, rows] if f < 3 else (eta if f == 3 else dens)[x, rows]
    away = x - 8 if x >= 8 else -x - 1
    if away >= W0[f]:
        return jnp.zeros((rows.stop - rows.start, 128), F32)
    if x >= 8:
        return high[OFF0[f] + away, rows] * flag(flags, 1)
    return low[OFF0[f] + W0[f] - 1 - away, rows] * flag(flags, 0)


def rel0(x):
    return x if x < 11 else x - NX0


YT0 = (0, 5, 10, 20, 15)
FIFTH0 = 26


def halo0(f, x):
    for q, pair in enumerate(PAIRS0[:6 if f == 3 else 5]):
        if x in pair:
            return q, pair.index(x)
    return None


def pack_y0(flags, force, eta, dens, low, high, up, down):
    own = (force, eta, dens, low, high)
    sub = iota((8, 128), 0)
    for f in range(5):
        for q, pair in enumerate(PAIRS0[:6 if f == 3 else 5]):
            a, b = (rel0(x) for x in pair)
            top, bottom = slice(24, 32), slice(0, 8)
            up[YT0[f] + q] = jnp.where(
                sub < 4, turn(plane0(flags, own, f, a, top), 4, 0), plane0(flags, own, f, b, top)
            )
            down[YT0[f] + q] = jnp.where(
                sub < 4, plane0(flags, own, f, a, bottom), turn(plane0(flags, own, f, b, bottom), 4, 0)
            )
    hi = lo = jnp.zeros((8, 128), F32)
    for x in range(8):
        hi = jnp.where(sub == x, turn(eta[x, 24:32], x - 3, 0), hi)
        lo = jnp.where(sub == x, turn(eta[x, 0:8], x - 4, 0), lo)
    up[FIFTH0], down[FIFTH0] = hi, lo


def rows0(flags, own, lowy, highy, f, x):
    sub = iota((8, 128), 0)
    middle = plane0(flags, own, f, rel0(x), slice(0, 32))
    if halo0(f, x) is None:
        return jnp.concatenate([middle, jnp.zeros((16, 128), F32)], axis=0)
    q, second = halo0(f, x)
    high, low = highy[YT0[f] + q], lowy[YT0[f] + q]
    if second:
        high = turn(high, 4, 0)
    else:
        low = turn(low, 4, 0)
    if f == 3 and x < 8:
        high = jnp.where(sub == 4, turn(highy[FIFTH0], 4 - x, 0), high)
        low = jnp.where(sub == 3, turn(lowy[FIFTH0], 3 - x, 0), low)
    return jnp.concatenate([middle, high * flag(flags, 3), low * flag(flags, 2)], axis=0)


def slot0(f, x):
    if x in PAIRS0[5]:
        return PAIRS0[5].index(x), 5 * ZSLOT0 + 3
    order = x if x < 9 else 9
    return order // 5, ZSLOT0 * (order % 5) + 3 + ZOFF0[f]


def pack_z0(flags, force, eta, dens, lowx, highx, lowy, highy, up, down):
    own = (force, eta, dens, lowx, highx)
    lane, sub = iota((40, 128), 1), iota((8, 128), 0)
    for g in range(2):
        hi = lo = jnp.zeros((40, 128), F32)
        for f in range(5):
            for x in range(NX0):
                if halo0(f, x) is None or slot0(f, x)[0] != g:
                    continue
                at, w = slot0(f, x)[1], Z0[f]
                value = rows0(flags, own, lowy, highy, f, x)
                mix = jnp.where(sub < 4, value[32:40], value[40:48])
                value = turn(jnp.concatenate([value[0:32], mix], axis=0), at, 1)
                hi = jnp.where(((lane + (128 + w - at)) & 63) < w, value, hi)
                lo = jnp.where(((lane + (128 - at)) & 63) < w, value, lo)
        up[g], down[g] = hi, lo


def assemble0(flags, force, eta, dens, lowx, highx, lowy, highy, even, odd, coeffs, kap, tmp):
    own = (force, eta, dens, lowx, highx)
    for x in range(NX0):
        for f in range(5):
            value = rows0(flags, own, lowy, highy, f, x)
            even[f, x] = value
            odd[f, x] = pltpu.roll(value, 64, 1)
            if f == 4:
                kap[x] = jnp.where(value > 0.0, 0.02 + 0.08 * value, 0.0)
    for i in range(-1, 5):
        x = (2 * i) % NX0
        for k, field in enumerate((even.at[3], kap)):
            r = row_pairs(tmp.at[k], field[x, 0:32] + field[x + 1, 0:32])
            coeffs[pl.ds((6 * k + i + 1) * 16, 16), :] = 0.125 * (r + pltpu.roll(r, 64, 1))


def fine(flags, even, odd, coeffs, lowz, highz,
         b, den, v, dinv, wx, wy, wz, own1, up, down, far_up, far_down,
         eta0, kap, dg, v0, pairs, tmp):
    lane, own = iota((40, 128), 1), iota((NY0, 128), 1) < 64
    fhi, flo = flag(flags, 5), flag(flags, 4)
    packets = [(highz[g] * fhi, lowz[g] * flo) for g in range(2)]
    for x in range(NX0):
        for f in range(5):
            if halo0(f, x) is None:
                far = far_even = jnp.zeros((NY0, 128), F32)
            else:
                (g, at), w = slot0(f, x), Z0[f]
                both = jnp.where(((lane + (128 - at)) & 63) < w, *packets[g])
                far, far_even = turn(both, -at, 1), turn(both, 64 - at, 1)
                far = jnp.concatenate([far, far[32:40]], axis=0)
                far_even = jnp.concatenate([far_even, far_even[32:40]], axis=0)
            parts = (jnp.where(own, even[f, x], far_even), jnp.where(own, odd[f, x], far))
            for half, value in enumerate(parts):
                lanes = slice(128 * half, 128 * half + 128)
                if f < 3:
                    b[f, x, :, lanes] = value
                elif f == 3:
                    eta0[x, :, lanes] = value
                else:
                    den[x, :, lanes] = value
                    kap[x, :, lanes] = jnp.where(value > 0.0, 0.02 + 0.08 * value, 0.0)
    w = (wx, wy, wz)
    weights(eta0, w, 1.0, -3, 11, NX0)
    diagonals(kap, w, dg, dinv, v0, b, -2, 10, NX0)
    sweep(v, v0, b, w, dinv, -1, 9, NX0)

    def blocks(i):
        x0 = 2 * i
        xm, xp, xq = (x0 + NX0 - 1) % NX0, x0 + 1, x0 + 2
        for c in range(3):
            r = rest(v, b, w, dg, c, x0, xp, xm) + rest(v, b, w, dg, c, xp, xq, x0)
            at = (c * 4 + i) * 16
            r = 0.125 * row_pairs(tmp.at[c], r[0:32, 0:128] + r[0:32, 128:256])
            pairs[pl.ds(at, 16), :] = jnp.where(iota((16, 128), 1) < 64, r, pltpu.roll(r, 64, 1))

    loop(4, blocks)

    def piece(f, i):
        if f < 3:
            return pairs[pl.ds((f * 4 + i) * 16, 16), :]
        return coeffs[pl.ds((6 * (f - 3) + i + 1) * 16, 16), :]

    half = iota((16, 128), 1) < 64
    ups = [(f, i) for f in range(5) for i in range(4 - W1[f], 4)]
    downs = [(f, i) for f in range(5) for i in range(0, W1[f])]
    for k in range(11):
        up[k] = jnp.where(half, piece(*ups[2 * k]), piece(*ups[2 * k + 1]))
        down[k] = jnp.where(half, piece(*downs[2 * k]), piece(*downs[2 * k + 1]))
    far_up[...] = jnp.where(half, piece(0, 3), piece(3, 2))
    far_down[...] = jnp.where(half, piece(0, 0), piece(3, 1))
    for f in range(5):
        for i in range(4):
            own1[f, i] = piece(f, i)


def pack_late(flags, v, late_up, late_down):
    sub, lane = iota((8, 128), 0), iota((40, 128), 1)
    for out, top in ((late_up, True), (late_down, False)):
        edge = jnp.zeros((40, 128), F32)
        for p, (c, away) in enumerate(LATE):
            x = 8 - away if top else away - 1
            parts = []
            for half in range(2):
                value = v[c, x, :, 128 * half:128 * half + 128]
                mix = jnp.where(sub < 4, value[32:40], value[40:48])
                parts.append(jnp.concatenate([value[0:32], mix], axis=0))
            even, odd = parts
            out[p] = jnp.where(lane < 64, even, pltpu.roll(odd, 64, 1))
            value = jnp.where(lane < 64, pltpu.roll(even, 64, 1), odd)
            edge = jnp.where(((lane & 63) >> 2) == p, turn(value, 4 * p + 2, 1), edge)
        out[7] = edge


def plane1(flags, own1, lowx, highx, f, x, half):
    if 0 <= x < 4:
        return own1[f, x]
    away = x - 4 if x >= 4 else -x - 1
    if x >= 4:
        at = OFF1[f] + away
        source, there = highx[at // 2], flag(flags, 1)
    else:
        at = OFF1[f] + W1[f] - 1 - away
        source, there = lowx[at // 2], flag(flags, 0)
    return turn(source, 64 * ((at + half) % 2), 1) * there


def pack_y1(flags, own1, lowx, highx, middle, up, down):
    sub = iota((8, 128), 0)
    left = iota((16, 128), 1) < 64
    sent = (flags, own1, lowx, highx)
    hi = lo = None
    for u in range(UNITS1):
        value = jnp.where(left, plane1(*sent, *PIECES1[2 * u], 0), plane1(*sent, *PIECES1[2 * u + 1], 1))
        middle[u] = value
        up[u], down[u] = value[8:16], value[0:8]
        if u < WIDE1:
            if u % 2 == 0:
                hi, lo = turn(value[0:8], 4, 0), value[8:16]
            else:
                hi, lo = jnp.where(sub < 4, hi, value[0:8]), jnp.where(sub < 4, lo, turn(value[8:16], 4, 0))
            up[UNITS1 + u // 2], down[UNITS1 + u // 2] = hi, lo


def unit1(flags, middle, lowy, highy, u):
    sub = iota((8, 128), 0)
    fhi, flo = flag(flags, 3), flag(flags, 2)
    if u < WIDE1:
        high, low = highy[UNITS1 + u // 2], lowy[UNITS1 + u // 2]
        high, low = (turn(high, 4, 0), low) if u % 2 else (high, turn(low, 4, 0))
        mix = jnp.where(sub < 4, high * fhi, low * flo)
    else:
        mix = jnp.zeros((8, 128), F32)
    value = jnp.concatenate([middle[u], highy[u] * fhi, mix, lowy[u] * flo], axis=0)
    return value


def assemble1(flags, middle, lowy, highy, rows):
    for u in range(UNITS1):
        value = unit1(flags, middle, lowy, highy, u)
        for h in range(2):
            f, x = PIECES1[2 * u + h]
            rows[f, x % NX1] = turn(value, 64 * h, 1)


def pack_z1(flags, middle, lowy, highy, up, down):
    lane = iota((40, 128), 1)

    def unit(u):
        return unit1(flags, middle, lowy, highy, u)

    odd = ((lane >> 5) & 1) == 1
    for g in range(QUADS1):
        a = unit(2 * g)
        b = unit(2 * g + 1) if 2 * g + 1 < WIDE1 else a
        b = turn(b, 32, 1)
        up[pl.ds(40 * g, 40), :] = jnp.where(odd, a, b)
        down[pl.ds(40 * g, 40), :] = jnp.where(odd, b, a)
    slot = (iota((32, 128), 1) >> 3) & 7
    for q in range(OCTS1):
        hi = lo = jnp.zeros((32, 128), F32)
        for j in range(8):
            u = WIDE1 + 8 * q + j
            if u < UNITS1:
                value = unit(u)
                value = jnp.concatenate([value[0:24], value[32:40]], axis=0)
                hi = jnp.where(slot == j, turn(value, 8 * j - 56, 1), hi)
                lo = jnp.where(slot == j, turn(value, 8 * j, 1), lo)
        at = 40 * QUADS1 + 32 * q
        up[pl.ds(at, 32), :], down[pl.ds(at, 32), :] = hi, lo


def all_rows1(value):
    return jnp.concatenate([value[0:24], value[16:32]], axis=0)


def load1(flags, rows, lowz, highz, b, eta, kap, count):
    lane = iota((NY1, 128), 1)
    slot = iota((40, 128), 1) >> 5
    fhi, flo = flag(flags, 5), flag(flags, 4)
    for p, (f, x) in enumerate(PIECES1[:count]):
        u, h = p // 2, p % 2
        if u < WIDE1:
            place = pl.ds(40 * (u // 2), 40)
            part = 2 * h + u % 2
            both = jnp.where(slot == part, highz[place, :] * fhi, lowz[place, :] * flo)
            beyond = turn(both, 64 - 32 * part, 1)
        else:
            q, j = (u - WIDE1) // 8, (u - WIDE1) % 8
            place = pl.ds(40 * QUADS1 + 32 * q, 32)
            high = all_rows1(turn(highz[place, :] * fhi, 64 - 8 * j - 64 * h, 1))
            low = all_rows1(turn(lowz[place, :] * flo, 120 - 8 * j - 64 * h, 1))
            beyond = jnp.where(lane < 96, high, low)
        value = jnp.where(lane < 64, rows[f, x % NX1], beyond)
        if f < 3:
            b[f, x % NX1] = value
        else:
            (eta if f == 3 else kap)[x % NX1] = value

def coarse(flags, rows, lowz, highz, own2, up, down, b, eta, kap, wx, wy, wz, dg, dinv, v0, v, pairs, tmp):
    load1(flags, rows, lowz, highz, b, eta, kap, 2 * WIDE1)
    w = (wx, wy, wz)
    weights(eta, w, 0.25, -3, 7, NX1)
    diagonals(kap, w, dg, dinv, v0, b, -2, 6, NX1)
    sweep(v, v0, b, w, dinv, -1, 5, NX1)

    def blocks(i):
        x0 = 2 * i
        for c in range(3):
            r = rest(v, b, w, dg, c, x0, x0 + 1, (x0 + NX1 - 1) % NX1)
            r = r + rest(v, b, w, dg, c, x0 + 1, x0 + 2, x0)
            at = (c * 2 + i) * 24
            pairs[pl.ds(at, 20), :] = row_pairs(tmp.at[c], r)
        at = (6 + i) * 24
        pairs[pl.ds(at, 20), :] = row_pairs(tmp.at[3], eta[x0] + eta[x0 + 1])
        at = (8 + i) * 24
        pairs[pl.ds(at, 20), :] = row_pairs(tmp.at[4], kap[x0] + kap[x0 + 1])

    loop(2, blocks)
    pairs[...] = dot(pairs[...], mean_matrix(mean2))
    left = iota((8, 128), 1) < 64
    for f in range(5):
        own, high, low = (
            jnp.where(left, pairs[pl.ds(48 * f + at, 8), :], pairs[pl.ds(48 * f + 24 + at, 8), :])
            for at in (0, 8, 12)
        )
        own2[f] = own
        up[f, 0:8], up[f, 8:16] = low, own
        down[f, 0:8], down[f, 8:16] = own, high


def smooth1(flags, rows, lowz, highz, far_low, far_high, b, v, dinv, wx, wy, wz, eta, kap, dg, v0):
    none = jnp.zeros((NY1, 128), F32)
    for x in (-6, 9):
        kap[x % NX1] = none
    for x in (-5, 8):
        for c in (1, 2):
            b[c, x % NX1] = none
    for f, x in FAR1:
        source = far_high[...] * flag(flags, 8) if x > 0 else far_low[...] * flag(flags, 7)
        value = jnp.concatenate([turn(source, 64 * int(f == 3), 1), none[0:24]], axis=0)
        if f == 0:
            b[0, x % NX1] = value
        else:
            eta[x % NX1] = value
    load1(flags, rows, lowz, highz, b, eta, kap, len(PIECES1))
    w = (wx, wy, wz)
    weights(eta, w, 0.25, -6, 10, NX1)
    diagonals(kap, w, dg, dinv, v0, b, -5, 9, NX1)
    sweep(v, v0, b, w, dinv, -4, 8, NX1)


def pack_x2(flags, own2, lowy, highy, out):
    sub = iota((8, 128), 0)
    for f in range(5):
        near, far = highy[f, 0:8] * flag(flags, 3), highy[f, 8:16] * flag(flags, 3)
        far_low, near_low = lowy[f, 0:8] * flag(flags, 2), lowy[f, 8:16] * flag(flags, 2)
        value = jnp.concatenate([own2[f], near, jnp.where(sub < 4, far, far_low), near_low], axis=0)
        for d in range(8):
            out[d, 32 * f:32 * f + 32] = value
        if f == 3:
            for d in range(8):
                out[d, 160:168] = jnp.where(sub == 4, far, far_low)


def finish(flags, got, late_low, late_high, b1, v1, dinv1, wx1, wy1, wz1, b0, den, v0, dinv0, wx0, wy0, wz0,
           velocity, new_density,
           b2, eta2, kap2, dg2, dinv2, wx2, wy2, wz2, va2, vb2,
           b3, eta3, kap3, dg3, dinv3, wx3, wy3, wz3, va3, vb3,
           pairs, spread, tmp, e2, va1, vb1, va0, vb0, lines):
    sub = iota((8, 128), 0)
    left2, left3 = iota((NY2, 128), 1) < 64, iota((NY3, 128), 1) < 64
    for f in range(5):
        two = []
        for d in range(8):
            own, near = got[d, 32 * f:32 * f + 8], got[d, 32 * f + 8:32 * f + 16]
            mix, low = got[d, 32 * f + 16:32 * f + 24], got[d, 32 * f + 24:32 * f + 32]
            far, far_low = mix, mix
            if f == 3:
                extra = got[d, 160:168]
                far, far_low = jnp.where(sub == 4, extra, mix), jnp.where(sub == 3, extra, mix)
            two.append(jnp.concatenate([far_low, low, own, near, far], axis=0))
        for d in range(4):
            even = jnp.where(left2, two[d], pltpu.roll(two[d + 4], 64, 1))
            odd = jnp.where(left2, pltpu.roll(two[d], 64, 1), two[d + 4])
            if f < 3:
                b2[f, 2 * d], b2[f, 2 * d + 1] = even, odd
            else:
                out = eta2 if f == 3 else kap2
                out[2 * d], out[2 * d + 1] = even, odd

    def ends(ref, n, left, lead=()):
        first_plane, last_plane = ref[lead + (0,)], ref[lead + (n - 1,)]
        ref[lead + (n,)] = jnp.where(left, pltpu.roll(first_plane, 64, 1), 0.0)
        ref[lead + (n + 1,)] = jnp.where(left, 0.0, pltpu.roll(last_plane, 64, 1))

    def ends2(ref):
        for c in range(3):
            ends(ref, 8, left2, (c,))

    def ends3(ref):
        for c in range(3):
            ends(ref, 4, left3, (c,))

    w2 = (wx2, wy2, wz2)
    ends(eta2, 8, left2)
    weights(eta2, w2, 0.0625, -1, 8, NX2)
    diagonals(kap2, w2, dg2, dinv2, va2, b2, 0, 8, NX2)
    ends2(va2)
    sweep(vb2, va2, b2, w2, dinv2, 0, 8, NX2)
    ends2(vb2)

    def blocks(i):
        x0 = 2 * i
        xm, xp, xq = (x0 + NX2 - 1) % NX2, x0 + 1, x0 + 2
        for c in range(3):
            r = rest(vb2, b2, w2, dg2, c, x0, xp, xm) + rest(vb2, b2, w2, dg2, c, xp, xq, x0)
            pairs[pl.ds((c * 4 + i) * 24, 20), :] = row_pairs(tmp.at[c], r)
        pairs[pl.ds((12 + i) * 24, 20), :] = row_pairs(tmp.at[3], eta2[x0] + eta2[xp])
        pairs[pl.ds((16 + i) * 24, 20), :] = row_pairs(tmp.at[4], kap2[x0] + kap2[xp])

    loop(4, blocks)
    pairs[pl.ds(0, 480), :] = dot(pairs[pl.ds(0, 480), :], mean_matrix(mean3))
    for i in range(4):
        for c in range(3):
            b3[c, i] = pairs[pl.ds((c * 4 + i) * 24, 24), :]
        eta3[i] = pairs[pl.ds((12 + i) * 24, 24), :]
        kap3[i] = pairs[pl.ds((16 + i) * 24, 24), :]
    w3 = (wx3, wy3, wz3)
    ends(eta3, 4, left3)
    weights(eta3, w3, 0.015625, -1, 4, NX3)
    diagonals(kap3, w3, dg3, dinv3, va3, b3, 0, 4, NX3)
    ends3(va3)
    sweep(vb3, va3, b3, w3, dinv3, 0, 4, NX3)
    ends3(vb3)
    sweep(va3, vb3, b3, w3, dinv3, 0, 4, NX3)
    ends3(va3)
    sweep(vb3, va3, b3, w3, dinv3, 0, 4, NX3)

    for c in range(3):
        for i in range(4):
            pairs[pl.ds((c * 4 + i) * 24, 24), :] = vb3[c, i]
    spread[pl.ds(0, 288), :] = dot(pairs[pl.ds(0, 288), :], repeat_matrix(repeat2))

    def rise2(i):
        for c in range(3):
            e = spread[pl.ds((c * 4 + i) * 24, 24), :]
            tmp[c, pl.ds(0, 24, stride=2), :] = e
            tmp[c, pl.ds(1, 24, stride=2), :] = e
            e = tmp[c, 0:40]
            vb2[c, 2 * i] = vb2[c, 2 * i] + e
            vb2[c, 2 * i + 1] = vb2[c, 2 * i + 1] + e

    loop(4, rise2)
    ends2(vb2)
    sweep(va2, vb2, b2, w2, dinv2, 0, 8, NX2)
    ends2(va2)
    sweep(vb2, va2, b2, w2, dinv2, 0, 8, NX2)

    none = jnp.zeros((24, 128), F32)
    for c in range(3):
        for x in (0, 1, 18, 19):
            e2[c, x] = none
        for x in range(8):
            value = jnp.concatenate([vb2[c, x, 16:32], turn(vb2[c, x, 8:16], 4, 0)], axis=0)
            e2[c, 2 + x] = value
            e2[c, 10 + x] = pltpu.roll(value, 64, 1)
    start = 2 * flags[6]
    for c in range(3):
        for k in range(6):
            pairs[pl.ds((c * 6 + k) * 24, 24), :] = e2[c, start + k]
    spread[pl.ds(0, 432), :] = dot(pairs[pl.ds(0, 432), :], repeat_matrix(repeat1))

    def rise1(k):
        x = (2 * k - 4 + NX1) % NX1
        for c in range(3):
            e = spread[pl.ds((c * 6 + k) * 24, 24), :]
            tmp[c, pl.ds(0, 24, stride=2), :] = e
            tmp[c, pl.ds(1, 24, stride=2), :] = e
            e = tmp[c, 0:40]
            va1[c, x] = v1[c, x] + e
            va1[c, x + 1] = v1[c, x + 1] + e

    loop(6, rise1)
    w1 = (wx1, wy1, wz1)
    sweep_wider(vb1, va1, b1, w1, dinv1, -3, 7, NX1)
    sweep_wider(va1, vb1, b1, w1, dinv1, -2, 6, NX1)

    for c in range(3):
        for i in range(-2, 6):
            at = (c * 8 + i + 2) * 24
            x = i % NX1
            pairs[pl.ds(at, 16), :] = va1[c, x, 0:16]
            pairs[pl.ds(at + 16, 8), :] = jnp.where(sub < 4, va1[c, x, 16:24], va1[c, x, 32:40])

    def risen(c, i):
        here = tmp.at[c]
        e = pairs[pl.ds((c * 8 + i) * 24, 24), :]
        here[pl.ds(0, 24, stride=2), :] = e
        here[pl.ds(1, 24, stride=2), :] = e
        e = here[...]
        return jnp.concatenate([e, e], axis=1)

    def rise0(i):
        for c in range(3):
            e = risen(c, i + 2)
            va0[c, 2 * i] = v0[c, 2 * i] + e
            va0[c, 2 * i + 1] = v0[c, 2 * i + 1] + e

    loop(4, rise0)
    lane = iota((40, 128), 1)
    for high, late in ((True, late_high), (False, late_low)):
        there = flag(flags, 1 if high else 0)
        for p, (c, away) in enumerate(LATE):
            x = 7 + away if high else NX0 - away
            own, edge = late[p], late[7]
            even = jnp.where(lane < 64, own, turn(edge, 62 - 4 * p, 1))
            odd = jnp.where(lane < 64, pltpu.roll(own, 64, 1), turn(edge, -4 * p - 2, 1))
            value = jnp.concatenate([even, odd], axis=1) * there
            value = jnp.concatenate([value, value[32:40]], axis=0)
            va0[c, x] = value + risen(c, (5 + (away + 1) // 2) if high else 2 - (away + 1) // 2)
    w0 = (wx0, wy0, wz0)
    first_lanes = iota((32, 128), 1) < 64

    def keep(at, x, value):
        at = 256 * at + 32 * x
        lines[pl.ds(at, 32), :] = jnp.where(
            first_lanes, value[0:32, 0:128], pltpu.roll(value[0:32, 128:256], 64, 1)
        )
    sweep_wider(vb0, va0, b0, w0, dinv0, -2, 10, NX0)
    sweep_wider(va0, vb0, b0, w0, dinv0, -1, 9, NX0)

    def advect(x):
        xm, xp = (x + NX0 - 1) % NX0, x + 1
        d = den[x]
        change = jnp.zeros_like(d)
        spreading = -6.0 * d
        for axis in range(3):
            u = va0[axis, x]
            if axis == 0:
                u_up, u_lo, d_up, d_lo = va0[0, xp], va0[0, xm], den[xp], den[xm]
            else:
                u_up, u_lo = back(u, axis - 1), forth(u, axis - 1)
                d_up, d_lo = back(d, axis - 1), forth(d, axis - 1)
            hi, lo = 0.5 * (u + u_up), 0.5 * (u_lo + u)
            change = change + (jnp.maximum(hi, 0.0) * d + jnp.minimum(hi, 0.0) * d_up)
            change = change - (jnp.maximum(lo, 0.0) * d_lo + jnp.minimum(lo, 0.0) * d)
            spreading = spreading + (d_up + d_lo)
            keep(axis, x, u)
        out = d - STEP_TIME * change + STEP_TIME * DIFFUSION * spreading
        keep(3, x, out)

    loop(8, advect)
    lines[...] = dot(lines[...], repeat_matrix(merge0))
    for x in range(8):
        for c in range(3):
            velocity[c, x] = lines[pl.ds(256 * c + 32 * x, 32), :]
        new_density[x] = lines[pl.ds(768 + 32 * x, 32), :]


def exchange(up, down, axis, away=1):
    n = lax.axis_size(axis)
    low = lax.ppermute(up, axis, [(i, (i + away) % n) for i in range(n)])
    high = lax.ppermute(down, axis, [(i, (i - away) % n) for i in range(n)])
    return low, high


def per_device(force, grain, density):
    gx, gy, gz = (lax.axis_index(a) for a in ("gx", "gy", "gz"))
    last = [lax.axis_size(a) - 1 for a in ("gx", "gy", "gz")]
    flags = jnp.stack(
        [gx > 0, gx < last[0], gy > 0, gy < last[1], gz > 0, gz < last[2], gx, gx > 1, gx < last[0] - 1]
    ).astype(jnp.int32)

    eta, force, density, up, down = call(
        prepare, [(8, 32, 128), (3, 8, 32, 128), (8, 32, 128), (11, 32, 128), (11, 32, 128)],
        [(1280, 128)], start=True
    )(flags, force, grain, density)
    x0 = exchange(up, down, "gx")
    up, down = call(pack_y0, [(27, 8, 128)] * 2)(flags, force, eta, density, *x0)
    y0 = exchange(up, down, "gy")
    up, down = call(pack_z0, [(2, 40, 128)] * 2)(flags, force, eta, density, *x0, *y0)
    z0 = exchange(up, down, "gz")
    vec, one = (3, NX0, NY0, NZ0), (NX0, NY0, NZ0)
    oneh = (NX0, NY0, 128)
    even, odd, coeffs = call(
        assemble0, [(5, NX0, NY0, 128)] * 2 + [(192, 128)], [oneh, (2, 48, 128)]
    )(flags, force, eta, density, *x0, *y0)
    b0, den, v0, dinv0, wx0, wy0, wz0, own1, up, down, far_up, far_down = call(
        fine,
        [vec, one, vec, one, one, one, one, (5, 4, 16, 128)] + [(11, 16, 128)] * 2 + [(16, 128)] * 2,
        [one, one, one, vec, (192, 128), (3, 48, 128)],
    )(flags, even, odd, coeffs, *z0)
    x1 = exchange(up, down, "gx")
    late_up, late_down = call(pack_late, [(8, 40, 128)] * 2)(flags, v0)
    x1, late_up, late_down = lax.optimization_barrier((x1, late_up, late_down))
    late = exchange(late_up, late_down, "gx")
    middle, up, down = call(
        pack_y1, [(UNITS1, 16, 128)] + [(UNITS1 + QUADS1, 8, 128)] * 2
    )(flags, own1, *x1)
    y1 = exchange(up, down, "gy")
    up, down = call(pack_z1, [(40 * QUADS1 + 32 * OCTS1, 128)] * 2)(flags, middle, *y1)
    up, down, late = lax.optimization_barrier((up, down, late))
    z1 = exchange(up, down, "gz")
    far = exchange(far_up, far_down, "gx", 2)
    z1, far = lax.optimization_barrier((z1, far))
    (rows,) = call(assemble1, [(5, NX1, NY1, 128)])(flags, middle, *y1)
    vec1, one1 = (3, NX1, NY1, 128), (NX1, NY1, 128)
    own2, up, down = call(
        coarse,
        [(5, 8, 128), (5, 16, 128), (5, 16, 128)],
        [vec1, one1, one1, one1, one1, one1, one1, one1, vec1, vec1, (240, 128), (5, 48, 128)],
    )(flags, rows, *z1)
    y2 = exchange(up, down, "gy")
    smooth = call(smooth1, [vec1, vec1, one1, one1, one1, one1], [one1, one1, one1, vec1])(flags, rows, *z1, *far)
    y2, smooth = lax.optimization_barrier((y2, smooth))
    (chunk,) = call(pack_x2, [(8, 168, 128)])(flags, own2, *y2)
    got = lax.all_to_all(chunk, "gx", 0, 0, tiled=True)
    vec2, one2 = (3, NX2, NY2, 128), (NX2, NY2, 128)
    vec3, one3 = (3, NX3, NY3, 128), (NX3, NY3, 128)
    velocity, new_density = call(
        finish,
        [(3, 8, 32, 128), (8, 32, 128)],
        [vec2, one2, one2, one2, one2, one2, one2, one2, vec2, vec2]
        + [vec3, one3, one3, one3, one3, one3, one3, one3, vec3, vec3]
        + [(576, 128), (576, 128), (6, 48, 128), (3, 20, 24, 128), vec1, vec1, vec, vec, (1024, 128)],
        limit=32,
        final=True,
    )(flags, got, *late, *smooth, b0, den, v0, dinv0, wx0, wy0, wz0)
    return velocity, new_density


def solution(mesh):
    return jax.shard_map(
        per_device,
        mesh=mesh,
        in_specs=(P(None, "gx", "gy", "gz"), P("gx", "gy", "gz"), P("gx", "gy", "gz")),
        out_specs=(P(None, "gx", "gy", "gz"), P("gx", "gy", "gz")),
        check_vma=False,
    )
```

```python
import jax
import jax.numpy as jnp
from jax import lax
from jax.experimental import pallas as pl
from jax.experimental.pallas import tpu as pltpu
from jax.sharding import PartitionSpec as P

OMEGA = 0.8
STEP_TIME = 0.1
DIFFUSION = 0.05
grain_table = [0.5 * 8.0 ** (entry / 15.0) for entry in range(16)]
F32 = jnp.float32
MIB = 1024 * 1024

W0 = (2, 2, 2, 3, 2)
OFF0 = (0, 2, 4, 6, 9)
Z0 = (2, 2, 2, 3, 2)
ZOFF0 = (3, 5, 7, 0, 9)
ZSLOT0 = 12
NX0, NY0, NZ0 = 14, 48, 256
PAIRS0 = ((0, 1), (2, 3), (4, 5), (6, 7), (8, 13), (9, 12))
LATE = ((0, 3), (0, 2), (0, 1), (1, 2), (1, 1), (2, 2), (2, 1))
W1 = (4, 4, 4, 5, 5)
OFF1 = (0, 4, 8, 12, 17)
FAR1 = ((0, -5), (0, 8), (3, -6), (3, 9))
NX1, NY1 = 16, 40
NEAR1 = (2, 2, 2, 3, 2)
PIECES1 = [(f, x) for f in range(5) for x in range(-NEAR1[f], 4 + NEAR1[f])]
WIDE1 = len(PIECES1) // 2
PIECES1 += [(f, x) for f in range(5) for x in range(-W1[f], 4 + W1[f]) if (f, x) not in PIECES1]
UNITS1 = len(PIECES1) // 2
QUADS1 = (WIDE1 + 1) // 2
OCTS1 = (UNITS1 - WIDE1 + 7) // 8
NX2, NY2 = 10, 40
NX3, NY3 = 6, 24


def iota(shape, dim):
    return lax.broadcasted_iota(jnp.int32, shape, dim)


def back(value, axis):
    if axis == 1 and value.shape[1] == 256:
        return jnp.concatenate([value[:, 128:256], pltpu.roll(value[:, 0:128], 127, 1)], axis=1)
    return pltpu.roll(value, value.shape[axis] - 1, axis)


def forth(value, axis):
    if axis == 1 and value.shape[1] == 256:
        return jnp.concatenate([pltpu.roll(value[:, 128:256], 1, 1), value[:, 0:128]], axis=1)
    return pltpu.roll(value, 1, axis)


def turn(value, shift, axis):
    shift = shift % value.shape[axis]
    return value if shift == 0 else pltpu.roll(value, shift, axis)


def call(body, outs, scratch=(), limit=12, start=False, final=False):
    def run(flags, *operands):
        if not final:
            shapes = [pltpu.VMEM(s, F32) for s in outs]
        else:
            shapes = [jax.ShapeDtypeStruct(s, F32) for s in outs]
        return pl.pallas_call(
            body,
            out_shape=shapes,
            in_specs=[pl.BlockSpec(memory_space=pltpu.SMEM)]
            + [pl.BlockSpec(memory_space=pltpu.VMEM)] * len(operands),
            out_specs=[pl.BlockSpec(memory_space=pltpu.VMEM)] * len(outs),
            scratch_shapes=[pltpu.VMEM(s, F32) for s in scratch],
            compiler_params=pltpu.CompilerParams(vmem_limit_bytes=limit * MIB),
        )(flags, *[pltpu.with_memory_space_constraint(o, pltpu.HBM if start else pltpu.VMEM) for o in operands])

    return run


def flag(flags, index):
    return flags[index].astype(F32)


def weighted(v, w, c, x, xp, xm):
    wx, wy, wz = w
    here = v[c, x]
    total = wx[x] * v[c, xp] + wx[xm] * v[c, xm]
    a = wy[x]
    total = total + a * back(here, 0) + forth(a * here, 0)
    a = wz[x]
    total = total + a * back(here, 1) + forth(a * here, 1)
    return here, total


def loop(count, body):
    for i in range(count):
        body(i)


def planes(lo, hi, n, body):
    for k in range(lo, hi):
        body(k % n, (k + 1) % n, (k - 1) % n)


def sweep(dst, src, b, w, dinv, lo, hi, n):
    def body(x, xp, xm):
        scale = dinv[x]
        for c in range(3):
            here, total = weighted(src, w, c, x, xp, xm)
            dst[c, x] = 0.2 * here + scale * (b[c, x] + total)

    planes(lo, hi, n, body)


def sweep_wider(dst, src, b, w, dinv, lo, hi, n):
    sweep(dst, src, b, w, dinv, lo + 1, hi - 1, n)
    for x in (lo % n, (hi - 1) % n):
        here, total = weighted(src, w, 0, x, (x + 1) % n, (x - 1) % n)
        dst[0, x] = 0.2 * here + dinv[x] * (b[0, x] + total)


def weights(eta, w, factor, lo, hi, n):
    wx, wy, wz = w
    half = 0.5 * factor

    def body(x, xp, xm):
        here = eta[x]
        wx[x] = half * (here + eta[xp])
        wy[x] = half * (here + back(here, 0))
        wz[x] = half * (here + back(here, 1))

    planes(lo, hi, n, body)
    x = (lo - 1) % n
    wx[x] = half * (eta[x] + eta[lo % n])


def diagonals(kap, w, dg, dinv, v, b, lo, hi, n):
    wx, wy, wz = w

    def body(x, xp, xm):
        k, a, g = kap[x], wy[x], wz[x]
        d = k + (wx[x] + wx[xm]) + (a + forth(a, 0)) + (g + forth(g, 1))
        inside = k > 0.0
        scale = jnp.where(inside, OMEGA / jnp.where(inside, d, 1.0), 0.0)
        dg[x] = d
        dinv[x] = scale
        for c in range(3):
            v[c, x] = scale * b[c, x]

    planes(lo, hi, n, body)


def rest(v, b, w, dg, c, x, xp, xm):
    here, total = weighted(v, w, c, x, xp, xm)
    return b[c, x] - dg[x] * here + total


def mean_matrix(source):
    k, j = iota((128, 128), 0), iota((128, 128), 1)
    return jnp.where((k >> 1) == source(j), 0.125, 0.0).astype(F32)


def repeat_matrix(source, out=128):
    k, j = iota((128, out), 0), iota((128, out), 1)
    return jnp.where(k == source(j), 1.0, 0.0).astype(F32)


def mean2(j):
    return (j + 48) & 63


def mean3(j):
    return jnp.where((j & 63) < 32, ((j >> 6) << 5) + (j & 63), -1)


def repeat2(j):
    return (j & 64) + ((j & 63) >> 1)


def repeat1(j):
    return ((j >> 1) + 16) & 63


def split0(j):
    return ((j & 63) << 1) + (j >> 6)


def merge0(j):
    return (j >> 1) + ((j & 1) << 6)


def dot(a, b):
    b = b.astype(jnp.bfloat16)
    high = a.astype(jnp.bfloat16)
    rest_of = a - high.astype(F32)
    middle = rest_of.astype(jnp.bfloat16)
    low = (rest_of - middle.astype(F32)).astype(jnp.bfloat16)
    product = lambda piece: jnp.dot(piece, b, preferred_element_type=F32)
    return product(high) + (product(middle) + product(low))


def row_pairs(tmp, value):
    rows = value.shape[0]
    tmp[pl.ds(0, rows), :] = value
    return tmp[pl.ds(0, rows // 2, stride=2), :] + tmp[pl.ds(1, rows // 2, stride=2), :]


def prepare(flags, force, grain, dens, eta, force_kept, dens_kept, up, down, lines):
    for x in range(8):
        ids = grain[x]
        looked = jnp.full(ids.shape, grain_table[0], F32)
        for entry in range(1, 16):
            looked = jnp.where(ids == entry, grain_table[entry], looked)
        d = dens[x]
        lines[pl.ds(768 + 32 * x, 32), :] = looked * d * d * d
        lines[pl.ds(1024 + 32 * x, 32), :] = d
        for c in range(3):
            lines[pl.ds(256 * c + 32 * x, 32), :] = force[c, x]
    lines[...] = dot(lines[...], repeat_matrix(split0))
    for x in range(8):
        eta[x] = lines[pl.ds(768 + 32 * x, 32), :]
        dens_kept[x] = lines[pl.ds(1024 + 32 * x, 32), :]
        for c in range(3):
            force_kept[c, x] = lines[pl.ds(256 * c + 32 * x, 32), :]
    force, dens = force_kept, dens_kept
    for f in range(5):
        for k in range(W0[f]):
            for out, x in ((up, 8 - W0[f] + k), (down, k)):
                out[OFF0[f] + k] = force[f, x] if f < 3 else (eta if f == 3 else dens)[x]


def plane0(flags, own, f, x, rows):
    force, eta, dens, low, high = own
    if 0 <= x < 8:
        return force[f, x, rows] if f < 3 else (eta if f == 3 else dens)[x, rows]
    away = x - 8 if x >= 8 else -x - 1
    if away >= W0[f]:
        return jnp.zeros((rows.stop - rows.start, 128), F32)
    if x >= 8:
        return high[OFF0[f] + away, rows] * flag(flags, 1)
    return low[OFF0[f] + W0[f] - 1 - away, rows] * flag(flags, 0)


def rel0(x):
    return x if x < 11 else x - NX0


YT0 = (0, 5, 10, 20, 15)
FIFTH0 = 26


def halo0(f, x):
    for q, pair in enumerate(PAIRS0[:6 if f == 3 else 5]):
        if x in pair:
            return q, pair.index(x)
    return None


def pack_y0(flags, force, eta, dens, low, high, up, down):
    own = (force, eta, dens, low, high)
    sub = iota((8, 128), 0)
    for f in range(5):
        for q, pair in enumerate(PAIRS0[:6 if f == 3 else 5]):
            a, b = (rel0(x) for x in pair)
            top, bottom = slice(24, 32), slice(0, 8)
            up[YT0[f] + q] = jnp.where(
                sub < 4, turn(plane0(flags, own, f, a, top), 4, 0), plane0(flags, own, f, b, top)
            )
            down[YT0[f] + q] = jnp.where(
                sub < 4, plane0(flags, own, f, a, bottom), turn(plane0(flags, own, f, b, bottom), 4, 0)
            )
    hi = lo = jnp.zeros((8, 128), F32)
    for x in range(8):
        hi = jnp.where(sub == x, turn(eta[x, 24:32], x - 3, 0), hi)
        lo = jnp.where(sub == x, turn(eta[x, 0:8], x - 4, 0), lo)
    up[FIFTH0], down[FIFTH0] = hi, lo


def rows0(flags, own, lowy, highy, f, x):
    sub = iota((8, 128), 0)
    middle = plane0(flags, own, f, rel0(x), slice(0, 32))
    if halo0(f, x) is None:
        return jnp.concatenate([middle, jnp.zeros((16, 128), F32)], axis=0)
    q, second = halo0(f, x)
    high, low = highy[YT0[f] + q], lowy[YT0[f] + q]
    if second:
        high = turn(high, 4, 0)
    else:
        low = turn(low, 4, 0)
    if f == 3 and x < 8:
        high = jnp.where(sub == 4, turn(highy[FIFTH0], 4 - x, 0), high)
        low = jnp.where(sub == 3, turn(lowy[FIFTH0], 3 - x, 0), low)
    return jnp.concatenate([middle, high * flag(flags, 3), low * flag(flags, 2)], axis=0)


def slot0(f, x):
    if x in PAIRS0[5]:
        return PAIRS0[5].index(x), 5 * ZSLOT0 + 3
    order = x if x < 9 else 9
    return order // 5, ZSLOT0 * (order % 5) + 3 + ZOFF0[f]


def pack_z0(flags, force, eta, dens, lowx, highx, lowy, highy, up, down):
    own = (force, eta, dens, lowx, highx)
    lane, sub = iota((40, 128), 1), iota((8, 128), 0)
    for g in range(2):
        hi = lo = jnp.zeros((40, 128), F32)
        for f in range(5):
            for x in range(NX0):
                if halo0(f, x) is None or slot0(f, x)[0] != g:
                    continue
                at, w = slot0(f, x)[1], Z0[f]
                value = rows0(flags, own, lowy, highy, f, x)
                mix = jnp.where(sub < 4, value[32:40], value[40:48])
                value = turn(jnp.concatenate([value[0:32], mix], axis=0), at, 1)
                hi = jnp.where(((lane + (128 + w - at)) & 63) < w, value, hi)
                lo = jnp.where(((lane + (128 - at)) & 63) < w, value, lo)
        up[g], down[g] = hi, lo


def assemble0(flags, force, eta, dens, lowx, highx, lowy, highy, even, odd, coeffs, kap, tmp):
    own = (force, eta, dens, lowx, highx)
    for x in range(NX0):
        for f in range(5):
            value = rows0(flags, own, lowy, highy, f, x)
            even[f, x] = value
            odd[f, x] = pltpu.roll(value, 64, 1)
            if f == 4:
                kap[x] = jnp.where(value > 0.0, 0.02 + 0.08 * value, 0.0)
    for i in range(-1, 5):
        x = (2 * i) % NX0
        for k, field in enumerate((even.at[3], kap)):
            r = row_pairs(tmp.at[k], field[x, 0:32] + field[x + 1, 0:32])
            coeffs[pl.ds((6 * k + i + 1) * 16, 16), :] = 0.125 * (r + pltpu.roll(r, 64, 1))


def fine(flags, even, odd, coeffs, lowz, highz,
         b, den, v, dinv, wx, wy, wz, own1, up, down, far_up, far_down,
         eta0, kap, dg, v0, pairs, tmp):
    lane, own = iota((40, 128), 1), iota((NY0, 128), 1) < 64
    fhi, flo = flag(flags, 5), flag(flags, 4)
    packets = [(highz[g] * fhi, lowz[g] * flo) for g in range(2)]
    for x in range(NX0):
        for f in range(5):
            if halo0(f, x) is None:
                far = far_even = jnp.zeros((NY0, 128), F32)
            else:
                (g, at), w = slot0(f, x), Z0[f]
                both = jnp.where(((lane + (128 - at)) & 63) < w, *packets[g])
                far, far_even = turn(both, -at, 1), turn(both, 64 - at, 1)
                far = jnp.concatenate([far, far[32:40]], axis=0)
                far_even = jnp.concatenate([far_even, far_even[32:40]], axis=0)
            parts = (jnp.where(own, even[f, x], far_even), jnp.where(own, odd[f, x], far))
            for half, value in enumerate(parts):
                lanes = slice(128 * half, 128 * half + 128)
                if f < 3:
                    b[f, x, :, lanes] = value
                elif f == 3:
                    eta0[x, :, lanes] = value
                else:
                    den[x, :, lanes] = value
                    kap[x, :, lanes] = jnp.where(value > 0.0, 0.02 + 0.08 * value, 0.0)
    w = (wx, wy, wz)
    weights(eta0, w, 1.0, -2, 10, NX0)
    diagonals(kap, w, dg, dinv, v0, b, -2, 10, NX0)
    sweep(v, v0, b, w, dinv, -1, 9, NX0)

    def blocks(i):
        x0 = 2 * i
        xm, xp, xq = (x0 + NX0 - 1) % NX0, x0 + 1, x0 + 2
        for c in range(3):
            r = rest(v, b, w, dg, c, x0, xp, xm) + rest(v, b, w, dg, c, xp, xq, x0)
            at = (c * 4 + i) * 16
            r = 0.125 * row_pairs(tmp.at[c], r[0:32, 0:128] + r[0:32, 128:256])
            pairs[pl.ds(at, 16), :] = jnp.where(iota((16, 128), 1) < 64, r, pltpu.roll(r, 64, 1))

    loop(4, blocks)

    def piece(f, i):
        if f < 3:
            return pairs[pl.ds((f * 4 + i) * 16, 16), :]
        return coeffs[pl.ds((6 * (f - 3) + i + 1) * 16, 16), :]

    half = iota((16, 128), 1) < 64
    ups = [(f, i) for f in range(5) for i in range(4 - W1[f], 4)]
    downs = [(f, i) for f in range(5) for i in range(0, W1[f])]
    for k in range(11):
        up[k] = jnp.where(half, piece(*ups[2 * k]), piece(*ups[2 * k + 1]))
        down[k] = jnp.where(half, piece(*downs[2 * k]), piece(*downs[2 * k + 1]))
    far_up[...] = jnp.where(half, piece(0, 3), piece(3, 2))
    far_down[...] = jnp.where(half, piece(0, 0), piece(3, 1))
    for f in range(5):
        for i in range(4):
            own1[f, i] = piece(f, i)


def pack_late(flags, v, late_up, late_down):
    sub, lane = iota((8, 128), 0), iota((40, 128), 1)
    for out, top in ((late_up, True), (late_down, False)):
        edge = jnp.zeros((40, 128), F32)
        for p, (c, away) in enumerate(LATE):
            x = 8 - away if top else away - 1
            parts = []
            for half in range(2):
                value = v[c, x, :, 128 * half:128 * half + 128]
                mix = jnp.where(sub < 4, value[32:40], value[40:48])
                parts.append(jnp.concatenate([value[0:32], mix], axis=0))
            even, odd = parts
            out[p] = jnp.where(lane < 64, even, pltpu.roll(odd, 64, 1))
            value = jnp.where(lane < 64, pltpu.roll(even, 64, 1), odd)
            edge = jnp.where(((lane & 63) >> 2) == p, turn(value, 4 * p + 2, 1), edge)
        out[7] = edge


def plane1(flags, own1, lowx, highx, f, x, half):
    if 0 <= x < 4:
        return own1[f, x]
    away = x - 4 if x >= 4 else -x - 1
    if x >= 4:
        at = OFF1[f] + away
        source, there = highx[at // 2], flag(flags, 1)
    else:
        at = OFF1[f] + W1[f] - 1 - away
        source, there = lowx[at // 2], flag(flags, 0)
    return turn(source, 64 * ((at + half) % 2), 1) * there


def pack_y1(flags, own1, lowx, highx, middle, up, down):
    sub = iota((8, 128), 0)
    left = iota((16, 128), 1) < 64
    sent = (flags, own1, lowx, highx)
    hi = lo = None
    for u in range(UNITS1):
        value = jnp.where(left, plane1(*sent, *PIECES1[2 * u], 0), plane1(*sent, *PIECES1[2 * u + 1], 1))
        middle[u] = value
        up[u], down[u] = value[8:16], value[0:8]
        if u < WIDE1:
            if u % 2 == 0:
                hi, lo = turn(value[0:8], 4, 0), value[8:16]
            else:
                hi, lo = jnp.where(sub < 4, hi, value[0:8]), jnp.where(sub < 4, lo, turn(value[8:16], 4, 0))
            up[UNITS1 + u // 2], down[UNITS1 + u // 2] = hi, lo


def unit1(flags, middle, lowy, highy, u):
    sub = iota((8, 128), 0)
    fhi, flo = flag(flags, 3), flag(flags, 2)
    if u < WIDE1:
        high, low = highy[UNITS1 + u // 2], lowy[UNITS1 + u // 2]
        high, low = (turn(high, 4, 0), low) if u % 2 else (high, turn(low, 4, 0))
        mix = jnp.where(sub < 4, high * fhi, low * flo)
    else:
        mix = jnp.zeros((8, 128), F32)
    value = jnp.concatenate([middle[u], highy[u] * fhi, mix, lowy[u] * flo], axis=0)
    return value


def assemble1(flags, middle, lowy, highy, rows):
    for u in range(UNITS1):
        value = unit1(flags, middle, lowy, highy, u)
        for h in range(2):
            f, x = PIECES1[2 * u + h]
            rows[f, x % NX1] = turn(value, 64 * h, 1)


def pack_z1(flags, middle, lowy, highy, up, down):
    lane = iota((40, 128), 1)

    def unit(u):
        return unit1(flags, middle, lowy, highy, u)

    odd = ((lane >> 5) & 1) == 1
    for g in range(QUADS1):
        a = unit(2 * g)
        b = unit(2 * g + 1) if 2 * g + 1 < WIDE1 else a
        b = turn(b, 32, 1)
        up[pl.ds(40 * g, 40), :] = jnp.where(odd, a, b)
        down[pl.ds(40 * g, 40), :] = jnp.where(odd, b, a)
    slot = (iota((32, 128), 1) >> 3) & 7
    for q in range(OCTS1):
        hi = lo = jnp.zeros((32, 128), F32)
        for j in range(8):
            u = WIDE1 + 8 * q + j
            if u < UNITS1:
                value = unit(u)
                value = jnp.concatenate([value[0:24], value[32:40]], axis=0)
                hi = jnp.where(slot == j, turn(value, 8 * j - 56, 1), hi)
                lo = jnp.where(slot == j, turn(value, 8 * j, 1), lo)
        at = 40 * QUADS1 + 32 * q
        up[pl.ds(at, 32), :], down[pl.ds(at, 32), :] = hi, lo


def all_rows1(value):
    return jnp.concatenate([value[0:24], value[16:32]], axis=0)


def load1(flags, rows, lowz, highz, b, eta, kap, count):
    lane = iota((NY1, 128), 1)
    slot = iota((40, 128), 1) >> 5
    fhi, flo = flag(flags, 5), flag(flags, 4)
    for p, (f, x) in enumerate(PIECES1[:count]):
        u, h = p // 2, p % 2
        if u < WIDE1:
            place = pl.ds(40 * (u // 2), 40)
            part = 2 * h + u % 2
            both = jnp.where(slot == part, highz[place, :] * fhi, lowz[place, :] * flo)
            beyond = turn(both, 64 - 32 * part, 1)
        else:
            q, j = (u - WIDE1) // 8, (u - WIDE1) % 8
            place = pl.ds(40 * QUADS1 + 32 * q, 32)
            high = all_rows1(turn(highz[place, :] * fhi, 64 - 8 * j - 64 * h, 1))
            low = all_rows1(turn(lowz[place, :] * flo, 120 - 8 * j - 64 * h, 1))
            beyond = jnp.where(lane < 96, high, low)
        value = jnp.where(lane < 64, rows[f, x % NX1], beyond)
        if f < 3:
            b[f, x % NX1] = value
        else:
            (eta if f == 3 else kap)[x % NX1] = value

def coarse(flags, rows, lowz, highz, own2, up, down, b, eta, kap, wx, wy, wz, dg, dinv, v0, v, pairs, tmp):
    load1(flags, rows, lowz, highz, b, eta, kap, 2 * WIDE1)
    w = (wx, wy, wz)
    weights(eta, w, 0.25, -2, 6, NX1)
    diagonals(kap, w, dg, dinv, v0, b, -2, 6, NX1)
    sweep(v, v0, b, w, dinv, -1, 5, NX1)

    def blocks(i):
        x0 = 2 * i
        for c in range(3):
            r = rest(v, b, w, dg, c, x0, x0 + 1, (x0 + NX1 - 1) % NX1)
            r = r + rest(v, b, w, dg, c, x0 + 1, x0 + 2, x0)
            at = (c * 2 + i) * 24
            pairs[pl.ds(at, 20), :] = row_pairs(tmp.at[c], r)
        at = (6 + i) * 24
        pairs[pl.ds(at, 20), :] = row_pairs(tmp.at[3], eta[x0] + eta[x0 + 1])
        at = (8 + i) * 24
        pairs[pl.ds(at, 20), :] = row_pairs(tmp.at[4], kap[x0] + kap[x0 + 1])

    loop(2, blocks)
    pairs[...] = dot(pairs[...], mean_matrix(mean2))
    left = iota((8, 128), 1) < 64
    for f in range(5):
        own, high, low = (
            jnp.where(left, pairs[pl.ds(48 * f + at, 8), :], pairs[pl.ds(48 * f + 24 + at, 8), :])
            for at in (0, 8, 12)
        )
        own2[f] = own
        up[f, 0:8], up[f, 8:16] = low, own
        down[f, 0:8], down[f, 8:16] = own, high


def smooth1(flags, rows, lowz, highz, far_low, far_high, b, v, dinv, wx, wy, wz, eta, kap, dg, v0):
    none = jnp.zeros((NY1, 128), F32)
    for x in (-6, 9):
        kap[x % NX1] = none
    for x in (-5, 8):
        for c in (1, 2):
            b[c, x % NX1] = none
    for f, x in FAR1:
        source = far_high[...] * flag(flags, 8) if x > 0 else far_low[...] * flag(flags, 7)
        value = jnp.concatenate([turn(source, 64 * int(f == 3), 1), none[0:24]], axis=0)
        if f == 0:
            b[0, x % NX1] = value
        else:
            eta[x % NX1] = value
    load1(flags, rows, lowz, highz, b, eta, kap, len(PIECES1))
    w = (wx, wy, wz)
    weights(eta, w, 0.25, -5, 9, NX1)
    diagonals(kap, w, dg, dinv, v0, b, -5, 9, NX1)
    sweep(v, v0, b, w, dinv, -4, 8, NX1)


def pack_x2(flags, own2, lowy, highy, out):
    sub = iota((8, 128), 0)
    for f in range(5):
        near, far = highy[f, 0:8] * flag(flags, 3), highy[f, 8:16] * flag(flags, 3)
        far_low, near_low = lowy[f, 0:8] * flag(flags, 2), lowy[f, 8:16] * flag(flags, 2)
        value = jnp.concatenate([own2[f], near, jnp.where(sub < 4, far, far_low), near_low], axis=0)
        for d in range(8):
            out[d, 32 * f:32 * f + 32] = value
        if f == 3:
            for d in range(8):
                out[d, 160:168] = jnp.where(sub == 4, far, far_low)


def finish(flags, got, late_low, late_high, b1, v1, dinv1, wx1, wy1, wz1, b0, den, v0, dinv0, wx0, wy0, wz0,
           velocity, new_density,
           b2, eta2, kap2, dg2, dinv2, wx2, wy2, wz2, va2, vb2,
           b3, eta3, kap3, dg3, dinv3, wx3, wy3, wz3, va3, vb3,
           pairs, spread, tmp, e2, va1, vb1, va0, vb0, lines):
    sub = iota((8, 128), 0)
    left2, left3 = iota((NY2, 128), 1) < 64, iota((NY3, 128), 1) < 64
    for f in range(5):
        two = []
        for d in range(8):
            own, near = got[d, 32 * f:32 * f + 8], got[d, 32 * f + 8:32 * f + 16]
            mix, low = got[d, 32 * f + 16:32 * f + 24], got[d, 32 * f + 24:32 * f + 32]
            far, far_low = mix, mix
            if f == 3:
                extra = got[d, 160:168]
                far, far_low = jnp.where(sub == 4, extra, mix), jnp.where(sub == 3, extra, mix)
            two.append(jnp.concatenate([far_low, low, own, near, far], axis=0))
        for d in range(4):
            even = jnp.where(left2, two[d], pltpu.roll(two[d + 4], 64, 1))
            odd = jnp.where(left2, pltpu.roll(two[d], 64, 1), two[d + 4])
            if f < 3:
                b2[f, 2 * d], b2[f, 2 * d + 1] = even, odd
            else:
                out = eta2 if f == 3 else kap2
                out[2 * d], out[2 * d + 1] = even, odd

    def ends(ref, n, left, lead=()):
        first_plane, last_plane = ref[lead + (0,)], ref[lead + (n - 1,)]
        ref[lead + (n,)] = jnp.where(left, pltpu.roll(first_plane, 64, 1), 0.0)
        ref[lead + (n + 1,)] = jnp.where(left, 0.0, pltpu.roll(last_plane, 64, 1))

    def ends2(ref):
        for c in range(3):
            ends(ref, 8, left2, (c,))

    def ends3(ref):
        for c in range(3):
            ends(ref, 4, left3, (c,))

    w2 = (wx2, wy2, wz2)
    ends(eta2, 8, left2)
    weights(eta2, w2, 0.0625, 0, 8, NX2)
    diagonals(kap2, w2, dg2, dinv2, va2, b2, 0, 8, NX2)
    ends2(va2)
    sweep(vb2, va2, b2, w2, dinv2, 0, 8, NX2)
    ends2(vb2)

    def blocks(i):
        x0 = 2 * i
        xm, xp, xq = (x0 + NX2 - 1) % NX2, x0 + 1, x0 + 2
        for c in range(3):
            r = rest(vb2, b2, w2, dg2, c, x0, xp, xm) + rest(vb2, b2, w2, dg2, c, xp, xq, x0)
            pairs[pl.ds((c * 4 + i) * 24, 20), :] = row_pairs(tmp.at[c], r)
        pairs[pl.ds((12 + i) * 24, 20), :] = row_pairs(tmp.at[3], eta2[x0] + eta2[xp])
        pairs[pl.ds((16 + i) * 24, 20), :] = row_pairs(tmp.at[4], kap2[x0] + kap2[xp])

    loop(4, blocks)
    pairs[pl.ds(0, 480), :] = dot(pairs[pl.ds(0, 480), :], mean_matrix(mean3))
    for i in range(4):
        for c in range(3):
            b3[c, i] = pairs[pl.ds((c * 4 + i) * 24, 24), :]
        eta3[i] = pairs[pl.ds((12 + i) * 24, 24), :]
        kap3[i] = pairs[pl.ds((16 + i) * 24, 24), :]
    w3 = (wx3, wy3, wz3)
    ends(eta3, 4, left3)
    weights(eta3, w3, 0.015625, 0, 4, NX3)
    diagonals(kap3, w3, dg3, dinv3, va3, b3, 0, 4, NX3)
    ends3(va3)
    sweep(vb3, va3, b3, w3, dinv3, 0, 4, NX3)
    ends3(vb3)
    sweep(va3, vb3, b3, w3, dinv3, 0, 4, NX3)
    ends3(va3)
    sweep(vb3, va3, b3, w3, dinv3, 0, 4, NX3)

    for c in range(3):
        for i in range(4):
            pairs[pl.ds((c * 4 + i) * 24, 24), :] = vb3[c, i]
    spread[pl.ds(0, 288), :] = dot(pairs[pl.ds(0, 288), :], repeat_matrix(repeat2))

    def rise2(i):
        for c in range(3):
            e = spread[pl.ds((c * 4 + i) * 24, 24), :]
            tmp[c, pl.ds(0, 24, stride=2), :] = e
            tmp[c, pl.ds(1, 24, stride=2), :] = e
            e = tmp[c, 0:40]
            vb2[c, 2 * i] = vb2[c, 2 * i] + e
            vb2[c, 2 * i + 1] = vb2[c, 2 * i + 1] + e

    loop(4, rise2)
    ends2(vb2)
    sweep(va2, vb2, b2, w2, dinv2, 0, 8, NX2)
    ends2(va2)
    sweep(vb2, va2, b2, w2, dinv2, 0, 8, NX2)

    none = jnp.zeros((24, 128), F32)
    for c in range(3):
        for x in (0, 1, 18, 19):
            e2[c, x] = none
        for x in range(8):
            value = jnp.concatenate([vb2[c, x, 16:32], turn(vb2[c, x, 8:16], 4, 0)], axis=0)
            e2[c, 2 + x] = value
            e2[c, 10 + x] = pltpu.roll(value, 64, 1)
    start = 2 * flags[6]
    for c in range(3):
        for k in range(6):
            pairs[pl.ds((c * 6 + k) * 24, 24), :] = e2[c, start + k]
    spread[pl.ds(0, 432), :] = dot(pairs[pl.ds(0, 432), :], repeat_matrix(repeat1))

    def rise1(k):
        x = (2 * k - 4 + NX1) % NX1
        for c in range(3):
            e = spread[pl.ds((c * 6 + k) * 24, 24), :]
            tmp[c, pl.ds(0, 24, stride=2), :] = e
            tmp[c, pl.ds(1, 24, stride=2), :] = e
            e = tmp[c, 0:40]
            va1[c, x] = v1[c, x] + e
            va1[c, x + 1] = v1[c, x + 1] + e

    loop(6, rise1)
    w1 = (wx1, wy1, wz1)
    sweep_wider(vb1, va1, b1, w1, dinv1, -3, 7, NX1)
    sweep_wider(va1, vb1, b1, w1, dinv1, -2, 6, NX1)

    for c in range(3):
        for i in range(-2, 6):
            at = (c * 8 + i + 2) * 24
            x = i % NX1
            pairs[pl.ds(at, 16), :] = va1[c, x, 0:16]
            pairs[pl.ds(at + 16, 8), :] = jnp.where(sub < 4, va1[c, x, 16:24], va1[c, x, 32:40])

    def risen(c, i):
        here = tmp.at[c]
        e = pairs[pl.ds((c * 8 + i) * 24, 24), :]
        here[pl.ds(0, 24, stride=2), :] = e
        here[pl.ds(1, 24, stride=2), :] = e
        e = here[...]
        return jnp.concatenate([e, e], axis=1)

    def rise0(i):
        for c in range(3):
            e = risen(c, i + 2)
            va0[c, 2 * i] = v0[c, 2 * i] + e
            va0[c, 2 * i + 1] = v0[c, 2 * i + 1] + e

    loop(4, rise0)
    lane = iota((40, 128), 1)
    for high, late in ((True, late_high), (False, late_low)):
        there = flag(flags, 1 if high else 0)
        for p, (c, away) in enumerate(LATE):
            x = 7 + away if high else NX0 - away
            own, edge = late[p], late[7]
            even = jnp.where(lane < 64, own, turn(edge, 62 - 4 * p, 1))
            odd = jnp.where(lane < 64, pltpu.roll(own, 64, 1), turn(edge, -4 * p - 2, 1))
            value = jnp.concatenate([even, odd], axis=1) * there
            value = jnp.concatenate([value, value[32:40]], axis=0)
            va0[c, x] = value + risen(c, (5 + (away + 1) // 2) if high else 2 - (away + 1) // 2)
    w0 = (wx0, wy0, wz0)
    first_lanes = iota((32, 128), 1) < 64

    def keep(at, x, value):
        at = 256 * at + 32 * x
        lines[pl.ds(at, 32), :] = jnp.where(
            first_lanes, value[0:32, 0:128], pltpu.roll(value[0:32, 128:256], 64, 1)
        )
    sweep_wider(vb0, va0, b0, w0, dinv0, -2, 10, NX0)
    sweep_wider(va0, vb0, b0, w0, dinv0, -1, 9, NX0)

    def advect(x):
        xm, xp = (x + NX0 - 1) % NX0, x + 1
        d = den[x]
        change = jnp.zeros_like(d)
        spreading = -6.0 * d
        for axis in range(3):
            u = va0[axis, x]
            if axis == 0:
                u_up, u_lo, d_up, d_lo = va0[0, xp], va0[0, xm], den[xp], den[xm]
            else:
                u_up, u_lo = back(u, axis - 1), forth(u, axis - 1)
                d_up, d_lo = back(d, axis - 1), forth(d, axis - 1)
            hi, lo = 0.5 * (u + u_up), 0.5 * (u_lo + u)
            change = change + (jnp.maximum(hi, 0.0) * d + jnp.minimum(hi, 0.0) * d_up)
            change = change - (jnp.maximum(lo, 0.0) * d_lo + jnp.minimum(lo, 0.0) * d)
            spreading = spreading + (d_up + d_lo)
            keep(axis, x, u)
        out = d - STEP_TIME * change + STEP_TIME * DIFFUSION * spreading
        keep(3, x, out)

    loop(8, advect)
    lines[...] = dot(lines[...], repeat_matrix(merge0))
    for x in range(8):
        for c in range(3):
            velocity[c, x] = lines[pl.ds(256 * c + 32 * x, 32), :]
        new_density[x] = lines[pl.ds(768 + 32 * x, 32), :]


def exchange(up, down, axis, away=1):
    n = lax.axis_size(axis)
    low = lax.ppermute(up, axis, [(i, (i + away) % n) for i in range(n)])
    high = lax.ppermute(down, axis, [(i, (i - away) % n) for i in range(n)])
    return low, high


def per_device(force, grain, density):
    gx, gy, gz = (lax.axis_index(a) for a in ("gx", "gy", "gz"))
    last = [lax.axis_size(a) - 1 for a in ("gx", "gy", "gz")]
    flags = jnp.stack(
        [gx > 0, gx < last[0], gy > 0, gy < last[1], gz > 0, gz < last[2], gx, gx > 1, gx < last[0] - 1]
    ).astype(jnp.int32)

    eta, force, density, up, down = call(
        prepare, [(8, 32, 128), (3, 8, 32, 128), (8, 32, 128), (11, 32, 128), (11, 32, 128)],
        [(1280, 128)], start=True
    )(flags, force, grain, density)
    x0 = exchange(up, down, "gx")
    up, down = call(pack_y0, [(27, 8, 128)] * 2)(flags, force, eta, density, *x0)
    y0 = exchange(up, down, "gy")
    up, down = call(pack_z0, [(2, 40, 128)] * 2)(flags, force, eta, density, *x0, *y0)
    z0 = exchange(up, down, "gz")
    vec, one = (3, NX0, NY0, NZ0), (NX0, NY0, NZ0)
    oneh = (NX0, NY0, 128)
    even, odd, coeffs = call(
        assemble0, [(5, NX0, NY0, 128)] * 2 + [(192, 128)], [oneh, (2, 48, 128)]
    )(flags, force, eta, density, *x0, *y0)
    b0, den, v0, dinv0, wx0, wy0, wz0, own1, up, down, far_up, far_down = call(
        fine,
        [vec, one, vec, one, one, one, one, (5, 4, 16, 128)] + [(11, 16, 128)] * 2 + [(16, 128)] * 2,
        [one, one, one, vec, (192, 128), (3, 48, 128)],
    )(flags, even, odd, coeffs, *z0)
    x1 = exchange(up, down, "gx")
    late_up, late_down = call(pack_late, [(8, 40, 128)] * 2)(flags, v0)
    x1, late_up, late_down = lax.optimization_barrier((x1, late_up, late_down))
    late = exchange(late_up, late_down, "gx")
    middle, up, down = call(
        pack_y1, [(UNITS1, 16, 128)] + [(UNITS1 + QUADS1, 8, 128)] * 2
    )(flags, own1, *x1)
    y1 = exchange(up, down, "gy")
    up, down = call(pack_z1, [(40 * QUADS1 + 32 * OCTS1, 128)] * 2)(flags, middle, *y1)
    up, down, late = lax.optimization_barrier((up, down, late))
    z1 = exchange(up, down, "gz")
    far = exchange(far_up, far_down, "gx", 2)
    z1, far = lax.optimization_barrier((z1, far))
    (rows,) = call(assemble1, [(5, NX1, NY1, 128)])(flags, middle, *y1)
    vec1, one1 = (3, NX1, NY1, 128), (NX1, NY1, 128)
    own2, up, down = call(
        coarse,
        [(5, 8, 128), (5, 16, 128), (5, 16, 128)],
        [vec1, one1, one1, one1, one1, one1, one1, one1, vec1, vec1, (240, 128), (5, 48, 128)],
    )(flags, rows, *z1)
    y2 = exchange(up, down, "gy")
    smooth = call(smooth1, [vec1, vec1, one1, one1, one1, one1], [one1, one1, one1, vec1])(flags, rows, *z1, *far)
    y2, smooth = lax.optimization_barrier((y2, smooth))
    (chunk,) = call(pack_x2, [(8, 168, 128)])(flags, own2, *y2)
    got = lax.all_to_all(chunk, "gx", 0, 0, tiled=True)
    vec2, one2 = (3, NX2, NY2, 128), (NX2, NY2, 128)
    vec3, one3 = (3, NX3, NY3, 128), (NX3, NY3, 128)
    velocity, new_density = call(
        finish,
        [(3, 8, 32, 128), (8, 32, 128)],
        [vec2, one2, one2, one2, one2, one2, one2, one2, vec2, vec2]
        + [vec3, one3, one3, one3, one3, one3, one3, one3, vec3, vec3]
        + [(576, 128), (576, 128), (6, 48, 128), (3, 20, 24, 128), vec1, vec1, vec, vec, (1024, 128)],
        limit=32,
        final=True,
    )(flags, got, *late, *smooth, b0, den, v0, dinv0, wx0, wy0, wz0)
    return velocity, new_density


def solution(mesh):
    return jax.shard_map(
        per_device,
        mesh=mesh,
        in_specs=(P(None, "gx", "gy", "gz"), P("gx", "gy", "gz"), P("gx", "gy", "gz")),
        out_specs=(P(None, "gx", "gy", "gz"), P("gx", "gy", "gz")),
        check_vma=False,
    )
```
